128 devices in a mesh: frame: 32 (over y, z, core), head: 4 (over x).
Axes of the slice: x: 4, y: 4, z: 4, core: 2. Of those that a mesh axis runs over, the one named last changes fastest.
Arguments:
- queries: bfloat16 [16384, 3072], P('frame', 'head'), may hold values from -240 to 240
- keys_in: bfloat16 [16384, 3072], P(('frame', 'head')), may hold values from -4 to 4
- values_in: bfloat16 [16384, 3072], P(('frame', 'head')), may hold values from -6 to 6
- grad_out: bfloat16 [16384, 3072], P('frame', 'head'), may hold values from -6 to 6
- assign: int32 [16384], P('frame'), may hold values from 0 to 127
- pattern: int32 [32, 16], replicated, may hold values from 0 to 63, as said below
- live_blocks: int32 [32], replicated, may hold values from 1 to 16, 256 in all
Outputs:
- attended: bfloat16 [16384, 3072], P('frame', 'head')
- grad_queries: bfloat16 [16384, 3072], P('frame', 'head')
- grad_keys: bfloat16 [16384, 3072], P(('frame', 'head'))
- grad_values: bfloat16 [16384, 3072], P(('frame', 'head'))
The draws below stay inside these ranges and needn't reach their ends.
Inputs may be any that keep to these rules, and one draw needn't show every extreme that they name: `pattern`: each row names 16 different key blocks; row b begins with its own blocks b * 2 to (b + 1) * 2 - 1 in order; its other entries lie in frames other than b (block i lies in frame i // 2), at most 1 of them in any one frame, and exactly 1 in some frame of every row. `live_blocks`: at least 1, at most 16, and some query block attends all 16.
All inputs are finite; a program needn't handle non-finite values.
Results may differ from the reference program's by a relative error of at most 0.023.
The reference program's roundings to bfloat16 on the way (of `score_grad`) count: a program that leaves them out, or rounds other values in their place, can miss the bound.
Values may be sent and summed in bfloat16 or wider, within the bound.
A program may use at most 128 MiB of HBM per device.

```python
import math
import jax
import jax.numpy as jnp
import numpy as np
from jax import lax

HEADS = 24
HD = 128
TOK_DEV = 512
MERGE = 4
KB = 64
NSEL = 16
BLK_DEV = 2
TOKENS = 16384
HW_ALL = 3072
N_FRAME = 32


def shared_keys(key):
    return jnp.clip(jax.random.normal(key, (TOKENS, HEADS * HD), jnp.float32), -4.0, 4.0)


def draw_keys_in(key, part):
    shared = shared_keys(key)
    return shared.astype(jnp.bfloat16)


def draw_queries(key, part):
    key = jax.random.fold_in(key, 11)
    noise = jnp.clip(jax.random.normal(key, (TOKENS, HEADS * HD), jnp.float32), -5.0, 5.0)
    return noise.astype(jnp.bfloat16)


def draw_pattern(key, part):
    key = jax.random.fold_in(key, 7)
    row_keys = jax.random.split(key, N_FRAME)
    other_frames = N_FRAME - 1
    far_count = NSEL - BLK_DEV
    orders = jax.vmap(lambda subkey: jax.random.permutation(subkey, other_frames))(row_keys).astype(jnp.int32)
    turns = jax.random.randint(jax.random.fold_in(key, 8), (N_FRAME, 1), 0, BLK_DEV).astype(jnp.int32)
    row_ids = jnp.arange(N_FRAME, dtype=jnp.int32)[:, None]
    far_ids = jnp.arange(far_count, dtype=jnp.int32)
    offsets = orders[:, far_ids % other_frames]
    far_frames = (row_ids + 1 + offsets) % N_FRAME
    within = (far_ids[None, :] // other_frames + turns) % BLK_DEV
    far_blocks = (far_frames * BLK_DEV + within).astype(jnp.int32)
    own_blocks = row_ids * BLK_DEV + jnp.arange(BLK_DEV, dtype=jnp.int32)[None, :]
    return jnp.concatenate([own_blocks, far_blocks], axis=1).astype(jnp.int32)


def with_ends(drawn, key, least, top_value):
    longest = drawn.shape.index(max(drawn.shape))
    spots = []
    for shift in (0, 1):
        where = [jax.random.randint(jax.random.fold_in(key, axis), (), 0, length) for axis, length in enumerate(drawn.shape)]
        where[longest] = (where[longest] + shift) % drawn.shape[longest]
        spots.append(tuple(where))
    return drawn.at[spots[0]].set(least).at[spots[1]].set(top_value)


def shard_levels(stream_key, shape, pieces, smallest, high):
    factor_of = 1.0
    for axis_at, shards_of in pieces:
        draws = jax.random.uniform(jax.random.fold_in(jax.random.fold_in(stream_key, 6), axis_at), (shards_of,), jnp.float32, smallest / len(pieces), high / len(pieces))
        factor_of = factor_of * jnp.repeat(jnp.exp(draws), shape[axis_at] // shards_of).reshape((-1,) + (1,) * (len(shape) - 1 - axis_at))
    return factor_of


def split_up(count, total, bound, slope):
    loads = [(1 << 20) // math.isqrt(grade ** slope) + 1 for grade in range(2, count + 1)]
    surplus, holding = total - bound - (count - 1), [1] * (count - 1)
    while surplus > 0:
        free = [i for i in range(count - 1) if holding[i] < bound]
        pool, remaining = sum([loads[i] for i in free]), surplus
        for i in free:
            addition = min(bound - holding[i], max(1, remaining * loads[i] // pool), surplus)
            holding[i] = holding[i] + addition
            surplus = surplus - addition
    return np.array([bound] + holding)


def uneven_parts(own_key, amount, total, reach, slope):
    if amount == 2:
        one = jax.random.randint(own_key, (), max(1, total - reach), min(reach, total - 1) + 1)
        return jnp.stack([one, total - one])
    tallies = jnp.asarray(split_up(amount, total, reach, slope), jnp.int32)
    twos = (amount - 1) // 2
    source_of, receiver = tallies[1:1 + 2 * twos:2], tallies[2:2 + 2 * twos:2]
    margin = jnp.minimum(source_of - 1, reach - receiver)
    shifted = jax.random.randint(jax.random.fold_in(own_key, 1), (twos,), 0, 1 << 20) % (margin + 1)
    tallies = tallies.at[1:1 + 2 * twos:2].set(source_of - shifted).at[2:2 + 2 * twos:2].set(receiver + shifted)
    return tallies[jax.random.permutation(jax.random.fold_in(own_key, 2), amount)]


def centred(stream_key, dims, scale, limit, cuts=(), kind=jnp.bfloat16):
    result = scale * jax.random.normal(stream_key, dims, jnp.float32)
    if cuts:
        result = result * shard_levels(stream_key, dims, cuts, -0.22, 0.18)
    return jnp.clip(result, -limit, limit).astype(kind)


def setup_inputs(seed: int = 0) -> dict:
    splits = jax.random.split(jax.random.key(seed), 8)
    queries = draw_queries(jax.random.fold_in(splits[7], 71), 0)
    keys_in = draw_keys_in(jax.random.fold_in(splits[7], 71), 0)
    values_in = centred(splits[2], (TOKENS, HW_ALL), 1.0, 6.0, ((0, 128),))
    grad_out = centred(splits[3], (TOKENS, HW_ALL), 1.0, 6.0, ((0, 32), (1, 4)))
    assign = with_ends(jax.random.randint(splits[4], (TOKENS,), 0, TOK_DEV // MERGE), jax.random.fold_in(splits[4], 1), 0, (TOK_DEV // MERGE) - 1).astype(jnp.int32)
    pattern = draw_pattern(jax.random.fold_in(splits[7], 71), 0)
    live_blocks = uneven_parts(splits[6], N_FRAME, N_FRAME * NSEL // 2, NSEL, 2).astype(jnp.int32)
    return dict(queries=queries, keys_in=keys_in, values_in=values_in, grad_out=grad_out, assign=assign, pattern=pattern, live_blocks=live_blocks)


def rounded(values):
    return lax.optimization_barrier(values.astype(jnp.bfloat16)).astype(jnp.float32)

def reference(queries, keys_in, values_in, grad_out, assign, pattern, live_blocks):
    merged_rows = TOK_DEV // MERGE
    slot_total = N_FRAME * merged_rows
    block_total = slot_total // KB
    row_width = HEADS * HD
    score_scale = 1.0 / math.sqrt(HD)
    token_ids = jnp.arange(TOKENS, dtype=jnp.int32)
    global_slots = (assign + token_ids // TOK_DEV * merged_rows).astype(jnp.int32)
    counts = jax.ops.segment_sum(jnp.ones((TOKENS,), jnp.float32), global_slots, num_segments=slot_total)
    divisor = jnp.maximum(counts, 1.0)
    merged_keys = (jax.ops.segment_sum(keys_in.astype(jnp.float32), global_slots, num_segments=slot_total) / divisor[:, None]).astype(jnp.bfloat16)
    merged_values = (jax.ops.segment_sum(values_in.astype(jnp.float32), global_slots, num_segments=slot_total) / divisor[:, None]).astype(jnp.bfloat16)
    key_blocks = merged_keys.reshape(block_total, KB, HEADS, HD)
    value_blocks = merged_values.reshape(block_total, KB, HEADS, HD)

    def one_block(sums, block_row):
        key_sums, value_sums = sums
        start = block_row * TOK_DEV
        query_heads = lax.dynamic_slice_in_dim(queries, start, TOK_DEV, 0).astype(jnp.float32).reshape(TOK_DEV, HEADS, HD)
        upstream = lax.dynamic_slice_in_dim(grad_out, start, TOK_DEV, 0).astype(jnp.float32).reshape(TOK_DEV, HEADS, HD)
        chosen = pattern[block_row]
        live_count = live_blocks[block_row]
        key_sel = key_blocks[chosen].astype(jnp.float32).reshape(NSEL * KB, HEADS, HD)
        value_sel = value_blocks[chosen].astype(jnp.float32).reshape(NSEL * KB, HEADS, HD)
        valid = jnp.arange(NSEL * KB, dtype=jnp.int32) // KB < live_count
        scores = jnp.einsum('thd,khd->htk', query_heads, key_sel) * score_scale
        scores = jnp.where(valid[None, None, :], scores, -jnp.inf)
        row_max = lax.optimization_barrier(jnp.max(scores, axis=2, keepdims=True))
        expo = jnp.exp(scores - row_max)
        row_sum = lax.optimization_barrier(jnp.sum(expo, axis=2))
        weighted = jnp.einsum('htk,khd->thd', rounded(expo), value_sel)
        attended = (weighted / row_sum.T[:, :, None]).reshape(TOK_DEV, row_width).astype(jnp.bfloat16)
        probs = expo / row_sum[:, :, None]
        prob_grad = jnp.einsum('thd,khd->htk', upstream, value_sel)
        row_delta = lax.optimization_barrier(jnp.sum(upstream * attended.astype(jnp.float32).reshape(TOK_DEV, HEADS, HD), axis=2)).T
        score_grad = rounded(probs * (prob_grad - row_delta[:, :, None]))
        query_grad = (score_scale * jnp.einsum('htk,khd->thd', score_grad, key_sel)).reshape(TOK_DEV, row_width).astype(jnp.bfloat16)
        key_update = (score_scale * jnp.einsum('htk,thd->khd', score_grad, query_heads)).reshape(NSEL, KB, row_width)
        value_update = jnp.einsum('htk,thd->khd', rounded(probs), upstream).reshape(NSEL, KB, row_width)
        key_part = jnp.zeros((block_total, KB, row_width), jnp.float32).at[chosen].add(key_update)
        value_part = jnp.zeros((block_total, KB, row_width), jnp.float32).at[chosen].add(value_update)
        return ((key_sums + rounded(key_part), value_sums + rounded(value_part)), (attended, query_grad))
    start_sums = (jnp.zeros((block_total, KB, row_width), jnp.float32), jnp.zeros((block_total, KB, row_width), jnp.float32))
    sums, outputs = lax.scan(one_block, start_sums, jnp.arange(N_FRAME, dtype=jnp.int32))
    attended = outputs[0].reshape(TOKENS, row_width)
    grad_queries = outputs[1].reshape(TOKENS, row_width)
    merged_key_grad = sums[0].reshape(slot_total, row_width) / divisor[:, None]
    merged_value_grad = sums[1].reshape(slot_total, row_width) / divisor[:, None]
    grad_keys = merged_key_grad[global_slots].astype(jnp.bfloat16)
    grad_values = merged_value_grad[global_slots].astype(jnp.bfloat16)
    return (attended, grad_queries, grad_keys, grad_values)
```

```python
import functools
import math

import jax
import jax.numpy as jnp
from jax import lax
from jax.experimental import pallas as pl
from jax.experimental.pallas import tpu as pltpu
from jax.sharding import PartitionSpec as P

HD = 128
KB = 64
NSEL = 16
SIDE = 4
CORES = 2
HEADS_X = 6
HN = HEADS_X // CORES
TOK = 512
TOK_DEV = TOK // SIDE
SLOTS = 128
CHIPS = SIDE * SIDE
SHARD = CORES * SLOTS
HALF = SHARD // 2
BLOCKS = CHIPS * SHARD // KB
CHUNK = 256
SCALE = 1.0 / math.sqrt(HD)
MESH = pl.DeviceIdType.MESH
BF = jnp.bfloat16
F32 = jnp.float32
VMEM_LIMIT = 56 * 1024 * 1024
PEERS = [(dx, dc) for dx in (1, 3, 2, 0) for dc in (0, 1) if (dx, dc) != (0, 0)]
SPOTS = (0, -1, 1, 2)


class Place:
    def __init__(self):
        frame = lax.axis_index("frame")
        self.x = lax.axis_index("head")
        self.core = frame % CORES
        self.at = {"z": (frame // CORES) % SIDE, "y": frame // (CORES * SIDE)}

    def coord(self, axis, off):
        return (self.at[axis] + off + SIDE) % SIDE if off else self.at[axis]

    def chip(self, **offs):
        return self.coord("y", offs.get("y", 0)) * SIDE + self.coord("z", offs.get("z", 0))

    def ring(self, axis, step):
        return {"frame": self.chip(**{axis: step}) * CORES + self.core, "head": self.x}

    def peer(self, dx, dc):
        x = (self.x + dx) % SIDE
        core = (self.core + dc) % CORES
        return x, core, {"frame": self.chip() * CORES + core, "head": x}


def meet(place):
    partners = [place.peer(dx, dc)[2] for dx, dc in PEERS]
    partners += [place.ring(axis, step) for axis in ("y", "z") for step in (1, -1)]
    barrier = pltpu.get_barrier_semaphore()
    for target in partners:
        pl.semaphore_signal(barrier, inc=1, device_id=target, device_id_type=MESH)
    pl.semaphore_wait(barrier, len(partners))


class Links:
    def __init__(self, send, recv, anyone):
        self.send, self.recv, self.anyone = send, recv, anyone
        self.started = []

    def go(self, sem, src, dst, target):
        copy = pltpu.make_async_remote_copy(
            src_ref=src,
            dst_ref=dst,
            send_sem=self.send.at[sem],
            recv_sem=self.recv.at[sem],
            device_id=target,
            device_id_type=MESH,
        )
        copy.start()
        self.started.append(copy)

    def got(self, sem, region):
        pltpu.make_async_remote_copy(
            src_ref=region,
            dst_ref=region,
            send_sem=self.send.at[sem],
            recv_sem=self.recv.at[sem],
            device_id=self.anyone,
            device_id_type=MESH,
        ).wait_recv()

    def finish(self):
        for copy in self.started:
            copy.wait_send()


def low(ref):
    return ref.at[pl.ds(0, HALF)]


def high(ref):
    return ref.at[pl.ds(HALF, HALF)]


def gather_rounds(place, links, base, buf, first, second):
    def spot(one, two):
        return buf.at[place.chip(**{first: one, second: two})]

    def push(sem, region, axis, step):
        links.go(base + sem, region, region, place.ring(axis, step))

    def take(sem, region):
        links.got(base + sem, region)

    def round0():
        push(0, spot(0, 0), first, 1)
        push(1, spot(0, 0), first, -1)
        push(4, spot(0, 0), second, 1)
        push(5, spot(0, 0), second, -1)

    def spread(k, s):
        push(4 + 4 * k, spot(s, 0), second, 1)
        push(5 + 4 * k, spot(s, 0), second, -1)

    def relay(k, s):
        take(4 + 4 * k, spot(s, -1))
        push(6 + 4 * k, low(spot(s, -1)), second, 1)
        take(5 + 4 * k, spot(s, 1))
        push(7 + 4 * k, high(spot(s, 1)), second, -1)

    def round1():
        take(0, spot(-1, 0))
        push(2, low(spot(-1, 0)), first, 1)
        spread(1, -1)
        take(1, spot(1, 0))
        push(3, high(spot(1, 0)), first, -1)
        spread(2, 1)
        relay(0, 0)

    def round2():
        take(2, low(spot(2, 0)))
        take(3, high(spot(2, 0)))
        spread(3, 2)
        relay(1, -1)
        relay(2, 1)

    def round3():
        relay(3, 2)

    def round4():
        for k, s in enumerate(SPOTS):
            take(6 + 4 * k, low(spot(s, 2)))
            take(7 + 4 * k, high(spot(s, 2)))

    return [round0, round1, round2, round3, round4]


GATHER_SEMS = 20


def slot_hot_of(assign_row):
    slots = lax.broadcasted_iota(jnp.int32, (SLOTS, TOK), 0)
    return (slots == assign_row).astype(F32)


def run_rounds(stages, stagger):
    ticks = {}
    for h, rounds in enumerate(stages):
        for r, step in enumerate(rounds):
            ticks.setdefault(h * stagger + r, []).append((-h, step))
    for tick in sorted(ticks):
        for _, step in sorted(ticks[tick], key=lambda item: item[0]):
            step()


def gather_kernel(
    keys, values, queries, upstream, assign,
    every_key, every_value, query_out, upstream_out, assign_out,
    key_tok, value_tok, send, recv, local, asem, qsem,
):
    place = Place()
    _, other_core, sibling = place.peer(0, 1)
    meet(place)
    links = Links(send, recv, sibling)
    locals_ = []

    def a2a_sem(h, kv, j):
        return (h * 2 + kv) * len(PEERS) + j

    gather_base = HN * 2 * len(PEERS)

    links.go(gather_base + HN * 2 * GATHER_SEMS + 2, assign, assign_out.at[place.core], sibling)
    own = pltpu.make_async_copy(assign, assign_out.at[place.core], asem)
    own.start()
    sources = ((keys, key_tok), (values, value_tok))
    for h in range(HN):
        for kv, (src, dst) in enumerate(sources):
            for j, (dx, dc) in enumerate(PEERS):
                x, core, target = place.peer(dx, dc)
                cols = pl.ds(pl.multiple_of((x * HEADS_X + core * HN + h) * HD, HD), HD)
                rows = pl.ds(pl.multiple_of(place.x * TOK_DEV, TOK_DEV), TOK_DEV)
                links.go(a2a_sem(h, kv, j), src.at[:, cols], dst.at[h, place.core, rows], target)
            cols = pl.ds(pl.multiple_of((place.x * HEADS_X + place.core * HN + h) * HD, HD), HD)
            rows = pl.ds(pl.multiple_of(place.x * TOK_DEV, TOK_DEV), TOK_DEV)
            copy = pltpu.make_async_copy(src.at[:, cols], dst.at[h, place.core, rows], local.at[h, kv])
            copy.start()
            locals_.append(copy)
    own.wait()
    links.got(gather_base + HN * 2 * GATHER_SEMS + 2, assign_out.at[other_core])

    def arrive(h):
        def step():
            hots = [slot_hot_of(assign_out[c, 0:1, :]) for c in range(CORES)]
            if h == 0:
                for which, (src, dst) in enumerate(((queries, query_out), (upstream, upstream_out))):
                    for core, remote in ((other_core, True), (place.core, False)):
                        for g in range(HN):
                            cols = pl.ds(pl.multiple_of((core * HN + g) * HD, HD), HD)
                            if remote:
                                links.go(
                                    gather_base + HN * 2 * GATHER_SEMS + 3 + which * HN + g,
                                    src.at[:, cols], dst.at[place.core, g], sibling,
                                )
                            else:
                                copy = pltpu.make_async_copy(
                                    src.at[:, cols], dst.at[place.core, g], qsem.at[which, g]
                                )
                                copy.start()
                                locals_.append(copy)
            for kv, (tok, every) in enumerate(((key_tok, every_key), (value_tok, every_value))):
                locals_[h * 2 + kv].wait()
                for j, (dx, dc) in enumerate(PEERS):
                    x, core, _ = place.peer(SIDE - dx, dc)
                    rows = pl.ds(pl.multiple_of(x * TOK_DEV, TOK_DEV), TOK_DEV)
                    links.got(a2a_sem(h, kv, j), tok.at[h, core, rows])
                for c in range(CORES):
                    counts = jnp.sum(hots[c], axis=1, keepdims=True)
                    sums = jnp.dot(hots[c].astype(BF), tok[h, c], preferred_element_type=F32)
                    every[h, place.chip(), pl.ds(c * SLOTS, SLOTS)] = (
                        sums / jnp.maximum(counts, 1.0)
                    ).astype(BF)

        return step

    stages = []
    for h in range(HN):
        plans = [
            gather_rounds(
                place, links, gather_base + (h * 2 + kv) * GATHER_SEMS, every.at[h], first, second
            )
            for kv, (every, first, second) in enumerate(
                ((every_key, "y", "z"), (every_value, "z", "y"))
            )
        ]
        rounds = [arrive(h)]
        for pair in zip(*plans):
            rounds += list(pair)
        stages.append(rounds)
    run_rounds(stages, 3)
    for which, dst in enumerate((query_out, upstream_out)):
        for g in range(HN):
            links.got(gather_base + HN * 2 * GATHER_SEMS + 3 + which * HN + g, dst.at[other_core, g])
    for copy in locals_[HN * 2 :]:
        copy.wait()
    links.finish()


def attention_kernel(
    pattern, live, keys, values, query, upstream,
    attended, query_grad, key_grad, value_grad,
    ksel, vsel, expo, kpart, vpart,
):
    frame = (lax.axis_index("frame") // CORES) * CORES + pl.program_id(1)
    count = live[frame]
    chunks = (count * KB + CHUNK - 1) // CHUNK
    rows_live = count * KB

    @pl.when(pl.program_id(1) == 0)
    def _():
        key_grad[...] = jnp.zeros_like(key_grad)
        value_grad[...] = jnp.zeros_like(value_grad)

    for j in range(NSEL):
        block = pattern[frame, j]
        ksel[pl.ds(j * KB, KB), :] = keys[0, block]
        vsel[pl.ds(j * KB, KB), :] = values[0, block]
    q = query[0, 0]
    g = upstream[0, 0]
    q_t = q.T
    g_t = g.T

    def rows_of(c):
        return pl.ds(pl.multiple_of(c * CHUNK, CHUNK), CHUNK)

    def score_step(c, top):
        scores = jnp.dot(ksel[rows_of(c), :], q_t, preferred_element_type=F32) * SCALE
        ids = lax.broadcasted_iota(jnp.int32, (CHUNK, TOK), 0) + c * CHUNK
        scores = jnp.where(ids < rows_live, scores, -jnp.inf)
        expo[rows_of(c), :] = scores
        return jnp.maximum(top, jnp.max(scores, axis=0, keepdims=True))

    top = lax.fori_loop(0, chunks, score_step, jnp.full((1, TOK), -jnp.inf, F32))

    def value_step(c, state):
        total, weighted = state
        weights = jnp.exp(expo[rows_of(c), :] - top)
        expo[rows_of(c), :] = weights
        total = total + jnp.sum(weights, axis=0, keepdims=True)
        weighted = weighted + lax.dot_general(
            vsel[rows_of(c), :], weights.astype(BF), (((0,), (0,)), ((), ())),
            preferred_element_type=F32,
        )
        return total, weighted

    total, weighted = lax.fori_loop(
        0, chunks, value_step, (jnp.zeros((1, TOK), F32), jnp.zeros((HD, TOK), F32))
    )
    att_t = (weighted / total).astype(BF)
    attended[0, 0] = att_t.T
    delta = jnp.sum(g_t.astype(F32) * att_t.astype(F32), axis=0, keepdims=True)
    inverse = 1.0 / total

    def grad_step(c, dq):
        probs = expo[rows_of(c), :] * inverse
        prob_grad = jnp.dot(vsel[rows_of(c), :], g_t, preferred_element_type=F32)
        score_grad = (probs * (prob_grad - delta)).astype(BF)
        kpart[rows_of(c), :] = jnp.dot(score_grad, q, preferred_element_type=F32) * SCALE
        vpart[rows_of(c), :] = jnp.dot(probs.astype(BF), g, preferred_element_type=F32)
        return dq + lax.dot_general(
            ksel[rows_of(c), :], score_grad, (((0,), (0,)), ((), ())), preferred_element_type=F32
        )

    dq = lax.fori_loop(0, chunks, grad_step, jnp.zeros((HD, TOK), F32))
    query_grad[0, 0] = (dq * SCALE).astype(BF).T

    for j in range(NSEL):

        @pl.when(j < count)
        def _():
            block = pattern[frame, j]
            for out, part in ((key_grad, kpart), (value_grad, vpart)):
                piece = part[pl.ds(j * KB, KB), :].astype(BF).astype(F32)
                out[0, block] = (out[0, block].astype(F32) + piece).astype(BF)


def bundle_steps(place, links, base, axis, part, halves, fulls, outgoing, finish):
    def start():
        links.go(base, low(part(2)), halves.at[0], place.ring(axis, 1))
        links.go(base + 1, high(part(2)), halves.at[1], place.ring(axis, -1))

    def relay():
        links.got(base, halves.at[0])
        ahead, behind = part(1), part(-1)
        outgoing[0, 0:HALF] = ahead[0:HALF] + halves[0]
        outgoing[0, HALF:SHARD] = ahead[HALF:SHARD]
        links.go(base + 2, outgoing.at[0], fulls.at[0], place.ring(axis, 1))
        links.got(base + 1, halves.at[1])
        outgoing[1, 0:HALF] = behind[0:HALF]
        outgoing[1, HALF:SHARD] = behind[HALF:SHARD] + halves[1]
        links.go(base + 3, outgoing.at[1], fulls.at[1], place.ring(axis, -1))

    def close():
        links.got(base + 2, fulls.at[0])
        links.got(base + 3, fulls.at[1])
        finish(part(0)[...].astype(F32) + fulls[0].astype(F32) + fulls[1].astype(F32))

    return start, relay, close


REDUCE_SEMS = 4 * (SIDE + 1)


def scatter_kernel(
    key_part, value_part, att_in, dq_in, assign,
    attended, query_grad, grad_keys, grad_values,
    halves, fulls, outgoing, column, tokens, send, recv, local, esem,
):
    place = Place()
    _, other_core, sibling = place.peer(0, 1)
    meet(place)
    links = Links(send, recv, sibling)
    locals_ = []
    token_base = HN * 2 * REDUCE_SEMS
    exchange_base = token_base + HN * 2 * len(PEERS)

    for which, (src, dst) in enumerate(((att_in, attended), (dq_in, query_grad))):
        for h in range(HN):
            cols = pl.ds(pl.multiple_of((place.core * HN + h) * HD, HD), HD)
            links.go(
                exchange_base + which * HN + h, src.at[other_core, h], dst.at[:, cols], sibling
            )
            copy = pltpu.make_async_copy(src.at[place.core, h], dst.at[:, cols], esem.at[which, h])
            copy.start()
            locals_.append(copy)

    outs = (grad_keys, grad_values)

    def cols_of(x, core, h):
        return pl.ds(pl.multiple_of((x * HEADS_X + core * HN + h) * HD, HD), HD)

    def expand(kv, h):
        def finish(total):
            for c in range(CORES):
                hot = slot_hot_of(assign[c, 0:1, :])
                counts = jnp.sum(hot, axis=1, keepdims=True)
                mean = (total[c * SLOTS : (c + 1) * SLOTS] / jnp.maximum(counts, 1.0)).astype(BF)
                tokens[h, kv, c] = lax.dot_general(
                    hot.astype(BF), mean, (((0,), (0,)), ((), ())), preferred_element_type=F32
                ).astype(BF)
            for j, (dx, dc) in enumerate(PEERS):
                x, core, target = place.peer(dx, dc)
                rows = pl.ds(pl.multiple_of(x * TOK_DEV, TOK_DEV), TOK_DEV)
                links.go(
                    token_base + (h * 2 + kv) * len(PEERS) + j,
                    tokens.at[h, kv, core, rows],
                    outs[kv].at[:, cols_of(place.x, place.core, h)],
                    target,
                )
            rows = pl.ds(pl.multiple_of(place.x * TOK_DEV, TOK_DEV), TOK_DEV)
            copy = pltpu.make_async_copy(
                tokens.at[h, kv, place.core, rows],
                outs[kv].at[:, cols_of(place.x, place.core, h)],
                local.at[h, kv],
            )
            copy.start()
            locals_.append(copy)

        return finish

    stages = []
    for h in range(HN):
        steps = [[] for _ in range(6)]
        for kv, (parts, first, second) in enumerate(
            ((key_part, "y", "z"), (value_part, "z", "y"))
        ):
            base = (h * 2 + kv) * REDUCE_SEMS

            def store(k, kv=kv, h=h):
                def finish(total):
                    column[h, kv, k] = total.astype(BF)

                return finish

            for k, s in reversed(list(enumerate(SPOTS))):

                def part(t, s=s, parts=parts, first=first, second=second, h=h):
                    return parts.at[h, place.chip(**{first: s, second: t})]

                three = bundle_steps(
                    place, links, base + 4 * k, second, part,
                    halves.at[h, kv, k], fulls.at[h, kv, k], outgoing.at[h, kv, k], store(k),
                )
                for tick, step in enumerate(three):
                    steps[tick].append(step)

            def column_part(t, kv=kv, h=h):
                return column.at[h, kv, SPOTS.index(t)]

            three = bundle_steps(
                place, links, base + 4 * SIDE, first, column_part,
                halves.at[h, kv, SIDE], fulls.at[h, kv, SIDE], outgoing.at[h, kv, SIDE],
                expand(kv, h),
            )
            for tick, step in enumerate(three):
                steps[3 + tick].append(step)
        stages.append([functools.partial(lambda group: [one() for one in group], group) for group in steps])
    run_rounds(stages, 1)

    for which, dst in enumerate((attended, query_grad)):
        for h in range(HN):
            cols = pl.ds(pl.multiple_of((other_core * HN + h) * HD, HD), HD)
            links.got(exchange_base + which * HN + h, dst.at[:, cols])
    for h in range(HN):
        for kv in range(2):
            for j, (dx, dc) in enumerate(PEERS):
                x, core, _ = place.peer(SIDE - dx, dc)
                links.got(
                    token_base + (h * 2 + kv) * len(PEERS) + j, outs[kv].at[:, cols_of(x, core, h)]
                )
    for copy in locals_:
        copy.wait()
    links.finish()


ANY = pl.BlockSpec(memory_space=pl.ANY)
VMEM = pl.BlockSpec(memory_space=pltpu.VMEM)
SMEM = pl.BlockSpec(memory_space=pltpu.SMEM)


def body(queries, keys_in, values_in, grad_out, assign, pattern, live_blocks):
    assign_rows = jnp.broadcast_to(assign[None, :], (8, TOK))
    shape = jax.ShapeDtypeStruct
    dma = pltpu.SemaphoreType.DMA
    n_gather = HN * 2 * (len(PEERS) + GATHER_SEMS) + 3 + 2 * HN
    every_key, every_value, query_two, upstream_two, assign_two = pl.pallas_call(
        gather_kernel,
        out_shape=(
            shape((HN, CHIPS, SHARD, HD), BF),
            shape((HN, CHIPS, SHARD, HD), BF),
            shape((CORES, HN, TOK, HD), BF),
            shape((CORES, HN, TOK, HD), BF),
            shape((CORES, 8, TOK), jnp.int32),
        ),
        in_specs=[ANY, ANY, ANY, ANY, VMEM],
        out_specs=(VMEM, VMEM, ANY, ANY, VMEM),
        scratch_shapes=[
            pltpu.VMEM((HN, CORES, TOK, HD), BF),
            pltpu.VMEM((HN, CORES, TOK, HD), BF),
            dma((n_gather,)),
            dma((n_gather,)),
            dma((HN, 2)),
            dma,
            dma((2, HN)),
        ],
        compiler_params=pltpu.CompilerParams(
            collective_id=0, has_side_effects=True, vmem_limit_bytes=VMEM_LIMIT
        ),
        name="gather",
    )(keys_in, values_in, queries, grad_out, assign_rows)

    def head_block():
        return pl.BlockSpec((1, BLOCKS, KB, HD), lambda h, c: (h, 0, 0, 0))

    def token_block():
        return pl.BlockSpec((1, 1, TOK, HD), lambda h, c: (c, h, 0, 0))

    att_two, dq_two, key_part, value_part = pl.pallas_call(
        attention_kernel,
        grid=(HN, CORES),
        out_shape=(
            shape((CORES, HN, TOK, HD), BF),
            shape((CORES, HN, TOK, HD), BF),
            shape((HN, BLOCKS, KB, HD), BF),
            shape((HN, BLOCKS, KB, HD), BF),
        ),
        in_specs=[SMEM, SMEM, head_block(), head_block(), token_block(), token_block()],
        out_specs=(token_block(), token_block(), head_block(), head_block()),
        scratch_shapes=[
            pltpu.VMEM((NSEL * KB, HD), BF),
            pltpu.VMEM((NSEL * KB, HD), BF),
            pltpu.VMEM((NSEL * KB, TOK), F32),
            pltpu.VMEM((NSEL * KB, HD), F32),
            pltpu.VMEM((NSEL * KB, HD), F32),
        ],
        compiler_params=pltpu.CompilerParams(vmem_limit_bytes=VMEM_LIMIT),
        name="attention",
    )(
        pattern, live_blocks,
        every_key.reshape(HN, BLOCKS, KB, HD), every_value.reshape(HN, BLOCKS, KB, HD),
        query_two, upstream_two,
    )

    n_reduce = HN * 2 * (REDUCE_SEMS + len(PEERS)) + 2 * HN
    return pl.pallas_call(
        scatter_kernel,
        out_shape=(
            shape(queries.shape, BF),
            shape(queries.shape, BF),
            shape(keys_in.shape, BF),
            shape(keys_in.shape, BF),
        ),
        in_specs=[VMEM, VMEM, ANY, ANY, VMEM],
        out_specs=(ANY, ANY, ANY, ANY),
        scratch_shapes=[
            pltpu.VMEM((HN, 2, SIDE + 1, 2, HALF, HD), BF),
            pltpu.VMEM((HN, 2, SIDE + 1, 2, SHARD, HD), BF),
            pltpu.VMEM((HN, 2, SIDE + 1, 2, SHARD, HD), BF),
            pltpu.VMEM((HN, 2, SIDE, SHARD, HD), BF),
            pltpu.VMEM((HN, 2, CORES, TOK, HD), BF),
            dma((n_reduce,)),
            dma((n_reduce,)),
            dma((HN, 2)),
            dma((2, HN)),
        ],
        compiler_params=pltpu.CompilerParams(
            collective_id=1, has_side_effects=True, vmem_limit_bytes=VMEM_LIMIT
        ),
        name="scatter",
    )(
        key_part.reshape(HN, CHIPS, SHARD, HD), value_part.reshape(HN, CHIPS, SHARD, HD),
        att_two, dq_two, assign_two,
    )


def solution(mesh):
    return jax.shard_map(
        body,
        mesh=mesh,
        in_specs=(
            P("frame", "head"),
            P(("frame", "head"), None),
            P(("frame", "head"), None),
            P("frame", "head"),
            P("frame"),
            P(),
            P(),
        ),
        out_specs=(
            P("frame", "head"),
            P("frame", "head"),
            P(("frame", "head"), None),
            P(("frame", "head"), None),
        ),
        check_vma=False,
    )
```

```python
import math

import jax
import jax.numpy as jnp
from jax import lax
from jax.experimental import pallas as pl
from jax.experimental.pallas import tpu as pltpu
from jax.sharding import PartitionSpec as P

HD = 128
KB = 64
NSEL = 16
SIDE = 4
CORES = 2
HEADS_X = 6
WIDTH = HEADS_X * HD
TOK = 512
TOK_DEV = TOK // SIDE
SLOTS = 128
UNITS = 6
CHUNK = 256
SCALE = 1.0 / math.sqrt(HD)
MESH = pl.DeviceIdType.MESH
BF = jnp.bfloat16
F32 = jnp.float32
VMEM_LIMIT = 56 * 1024 * 1024
STEPS = (1, -1, 2)
GROUPS = ((0, SIDE), (SIDE, HEADS_X - SIDE))
PARTS = ((0, 0), (1, 0), (0, 1), (1, 1))


class Place:
    def __init__(self):
        frame = lax.axis_index("frame")
        self.x = lax.axis_index("head")
        self.core = frame % CORES
        self.z = (frame // CORES) % SIDE
        self.y = frame // (CORES * SIDE)

    def device(self, y, z, core, x):
        return {"frame": (y * SIDE + z) * CORES + core, "head": x}

    def ring(self, axis, step):
        at = {"x": self.x, "y": self.y, "z": self.z}
        at[axis] = (at[axis] + step + SIDE) % SIDE
        return self.device(at["y"], at["z"], self.core, at["x"])

    def sibling(self):
        return self.device(self.y, self.z, 1 - self.core, self.x)

    def partner(self):
        return self.device(self.y, SIDE - 1 - self.z, self.core, self.x)


def shift(at, step):
    return (at + step + SIDE) % SIDE


def meet(place):
    partners = [place.sibling()]
    partners += [place.ring(axis, step) for axis in ("x", "z") for step in STEPS]
    partners += [place.ring("y", step) for step in (1, -1)]
    barrier = pltpu.get_barrier_semaphore()
    for target in partners:
        pl.semaphore_signal(barrier, inc=1, device_id=target, device_id_type=MESH)
    pl.semaphore_wait(barrier, len(partners))


class Links:
    def __init__(self, place, send, recv, local):
        self.send, self.recv, self.local = send, recv, local
        self.anyone = place.sibling()
        self.started = []
        self.names = {}
        self.local_names = {}

    def sem(self, name):
        return self.names.setdefault(name, len(self.names))

    def remote(self, name, src, dst, target):
        sem = self.sem(name)
        return pltpu.make_async_remote_copy(
            src_ref=src,
            dst_ref=dst,
            send_sem=self.send.at[sem],
            recv_sem=self.recv.at[sem],
            device_id=target,
            device_id_type=MESH,
        )

    def go(self, name, src, dst, target):
        copy = self.remote(name, src, dst, target)
        copy.start()
        self.started.append(copy)

    def got(self, name, region):
        self.remote(name, region, region, self.anyone).wait_recv()

    def here(self, name, src, dst):
        sem = self.local_names.setdefault(name, len(self.local_names))
        copy = pltpu.make_async_copy(src, dst, self.local.at[sem])
        copy.start()
        return copy

    def finish(self):
        for copy in self.started:
            copy.wait_send()


def low(ref):
    return ref.at[pl.ds(0, SIDE // 2)]


def high(ref):
    return ref.at[pl.ds(SIDE // 2, SIDE // 2)]


def cols(head, count=1):
    return pl.ds(pl.multiple_of(head * HD, HD), count * HD)


def token_rows(x):
    return pl.ds(pl.multiple_of(x * TOK_DEV, TOK_DEV), TOK_DEV)


def slot_hot_of(assign):
    slots = lax.broadcasted_iota(jnp.int32, (SLOTS, TOK), 0)
    return (slots == assign[0:1, :]).astype(F32)


def run_rounds(stages, stagger):
    ticks = {}
    for i, rounds in enumerate(stages):
        for r, step in enumerate(rounds):
            ticks.setdefault(i * stagger + r, []).append((-i, step))
    for tick in sorted(ticks):
        for _, step in sorted(ticks[tick], key=lambda item: item[0]):
            step()


GATHER_SEMS = len(PARTS) * 14 + 2 * 4
GATHER_LOCAL = len(PARTS) + 4


def gather_kernel(
    keys, values, queries, upstream, assign,
    every_key, every_value, query_out, upstream_out,
    tokens, merged, send, recv, local,
):
    place = Place()
    meet(place)
    links = Links(place, send, recv, local)
    sources = (keys, values)
    every = (every_key, every_value)
    own = {}

    def send_tokens(kv, slot):
        first, count = GROUPS[slot]
        for step in STEPS:
            links.go(
                ("x", kv, slot, step),
                sources[kv].at[:, cols(shift(place.x, step) * HEADS_X + first, count)],
                tokens.at[kv, token_rows(place.x), cols(first, count)],
                place.ring("x", step),
            )
        own[kv, slot] = links.here(
            ("x", kv, slot),
            sources[kv].at[:, cols(place.x * HEADS_X + first, count)],
            tokens.at[kv, token_rows(place.x), cols(first, count)],
        )

    def send_queries(which):
        src, dst = ((queries, query_out), (upstream, upstream_out))[which]
        for step in STEPS:
            links.go(
                ("q", which, step), src.at[:, cols(shift(place.z, step))], dst.at[place.z],
                place.ring("z", step),
            )
        mine = place.z // 2
        links.go(
            ("q", which, "partner"), src.at[:, cols(SIDE + 1 - mine)], dst.at[SIDE + 1],
            place.partner(),
        )
        own["q", which, 0] = links.here(("q", which, 0), src.at[:, cols(place.z)], dst.at[place.z])
        own["q", which, 1] = links.here(
            ("q", which, 1), src.at[:, cols(SIDE + mine)], dst.at[SIDE]
        )

    send_tokens(*PARTS[0])
    send_tokens(*PARTS[1])
    send_queries(0)
    send_tokens(*PARTS[2])
    send_tokens(*PARTS[3])
    hot = slot_hot_of(assign)
    divisor = jnp.maximum(jnp.sum(hot, axis=1, keepdims=True), 1.0)
    hot = hot.astype(BF)

    def stage(kv, slot):
        first, count = GROUPS[slot]
        out = every[kv]

        def region(step):
            return out.at[slot, shift(place.y, step), place.core]

        def pass_on(step):
            links.go(("s", kv, slot, step), region(step), region(step), place.sibling())

        def merge():
            own[kv, slot].wait()
            for step in STEPS:
                links.got(
                    ("x", kv, slot, step),
                    tokens.at[kv, token_rows(shift(place.x, -step)), cols(first, count)],
                )
            sums = jnp.dot(
                hot, tokens[kv, :, first * HD : (first + count) * HD], preferred_element_type=F32
            )
            mean = (sums / divisor).astype(BF)
            for i in range(count):
                merged[kv, first + i] = mean[:, i * HD : (i + 1) * HD]

            def head_of(z):
                return z if slot == 0 else SIDE + z // 2

            for step in STEPS:
                links.go(
                    ("z", kv, slot, step),
                    merged.at[kv, head_of(shift(place.z, step))],
                    out.at[slot, place.y, place.core, place.z],
                    place.ring("z", step),
                )
            out[slot, place.y, place.core, place.z] = merged[kv, head_of(place.z)]
            if (kv, slot) == PARTS[0]:
                send_queries(1)

        def row():
            for step in STEPS:
                links.got(
                    ("z", kv, slot, step),
                    out.at[slot, place.y, place.core, shift(place.z, -step)],
                )
            links.go(("y", kv, slot, 1), region(0), region(0), place.ring("y", 1))
            links.go(("y", kv, slot, -1), region(0), region(0), place.ring("y", -1))
            pass_on(0)

        def near():
            links.got(("y", kv, slot, 1), region(-1))
            links.go(("f", kv, slot, 1), low(region(-1)), low(region(-1)), place.ring("y", 1))
            pass_on(-1)
            links.got(("y", kv, slot, -1), region(1))
            links.go(("f", kv, slot, -1), high(region(1)), high(region(1)), place.ring("y", -1))
            pass_on(1)

        def far():
            links.got(("f", kv, slot, 1), low(region(2)))
            links.got(("f", kv, slot, -1), high(region(2)))
            pass_on(2)

        def close():
            for step in (0, -1, 1, 2):
                links.got(
                    ("s", kv, slot, step), out.at[slot, shift(place.y, step), 1 - place.core]
                )

        return [merge, row, near, far, close]

    run_rounds([stage(kv, slot) for kv, slot in PARTS], 1)
    for which, dst in enumerate((query_out, upstream_out)):
        for step in STEPS:
            links.got(("q", which, step), dst.at[shift(place.z, -step)])
        links.got(("q", which, "partner"), dst.at[SIDE + 1])
        own["q", which, 0].wait()
        own["q", which, 1].wait()
    links.finish()


def attention_kernel(
    pattern, live, keys, values, query, upstream,
    attended, query_grad, key_grad, value_grad,
    ksel, vsel, expo, kpart, vpart,
):
    place = Place()
    unit = pl.program_id(0)
    unit_z = jnp.where(unit < SIDE, unit, jnp.where(unit == SIDE, place.z, SIDE - 1 - place.z))
    frame = (place.y * SIDE + unit_z) * CORES + place.core
    count = live[frame]
    chunks = (count * KB + CHUNK - 1) // CHUNK
    rows_live = count * KB

    def spot_of(block):
        owner = block // 2
        y, z, core = owner // (CORES * SIDE), (owner // CORES) % SIDE, owner % CORES
        return ((y * CORES + core) * SIDE + z) * 2 + block % 2

    @pl.when((unit == 0) | (unit == SIDE))
    def _():
        key_grad[...] = jnp.zeros_like(key_grad)
        value_grad[...] = jnp.zeros_like(value_grad)

    for j in range(NSEL):
        spot = spot_of(pattern[frame, j])
        ksel[pl.ds(j * KB, KB), :] = keys[0, spot]
        vsel[pl.ds(j * KB, KB), :] = values[0, spot]
    q = query[0]
    g = upstream[0]
    q_t = q.T
    g_t = g.T

    def rows_of(c):
        return pl.ds(pl.multiple_of(c * CHUNK, CHUNK), CHUNK)

    def score_step(c, top):
        scores = jnp.dot(ksel[rows_of(c), :], q_t, preferred_element_type=F32) * SCALE
        ids = lax.broadcasted_iota(jnp.int32, (CHUNK, TOK), 0) + c * CHUNK
        scores = jnp.where(ids < rows_live, scores, -jnp.inf)
        expo[rows_of(c), :] = scores
        return jnp.maximum(top, jnp.max(scores, axis=0, keepdims=True))

    top = lax.fori_loop(0, chunks, score_step, jnp.full((1, TOK), -jnp.inf, F32))

    def value_step(c, state):
        total, weighted = state
        weights = jnp.exp(expo[rows_of(c), :] - top)
        expo[rows_of(c), :] = weights
        total = total + jnp.sum(weights, axis=0, keepdims=True)
        weighted = weighted + lax.dot_general(
            vsel[rows_of(c), :], weights.astype(BF), (((0,), (0,)), ((), ())),
            preferred_element_type=F32,
        )
        return total, weighted

    total, weighted = lax.fori_loop(
        0, chunks, value_step, (jnp.zeros((1, TOK), F32), jnp.zeros((HD, TOK), F32))
    )
    att_t = (weighted / total).astype(BF)
    attended[0] = att_t.T
    delta = jnp.sum(g_t.astype(F32) * att_t.astype(F32), axis=0, keepdims=True)
    inverse = 1.0 / total

    def grad_step(c, dq):
        probs = expo[rows_of(c), :] * inverse
        prob_grad = jnp.dot(vsel[rows_of(c), :], g_t, preferred_element_type=F32)
        score_grad = (probs * (prob_grad - delta)).astype(BF)
        kpart[rows_of(c), :] = jnp.dot(score_grad, q, preferred_element_type=F32) * SCALE
        vpart[rows_of(c), :] = jnp.dot(probs.astype(BF), g, preferred_element_type=F32)
        return dq + lax.dot_general(
            ksel[rows_of(c), :], score_grad, (((0,), (0,)), ((), ())), preferred_element_type=F32
        )

    dq = lax.fori_loop(0, chunks, grad_step, jnp.zeros((HD, TOK), F32))
    query_grad[0] = (dq * SCALE).astype(BF).T

    for j in range(NSEL):

        @pl.when(j < count)
        def _():
            spot = spot_of(pattern[frame, j])
            for out, part in ((key_grad, kpart), (value_grad, vpart)):
                piece = part[pl.ds(j * KB, KB), :].astype(BF).astype(F32)
                out[0, spot] = (out[0, spot].astype(F32) + piece).astype(BF)


SCATTER_SEMS = len(PARTS) * 14 + 2 * 4
SCATTER_LOCAL = len(PARTS) + 4


def scatter_kernel(
    key_part, value_part, att_in, dq_in, assign,
    attended, query_grad, grad_keys, grad_values,
    twin, halves, fulls, outgoing, column, pieces, tokens, send, recv, local,
):
    place = Place()
    meet(place)
    links = Links(place, send, recv, local)
    parts = (key_part, value_part)
    outs = (grad_keys, grad_values)
    own = []

    def send_twin(kv, slot):
        for step in (2, 1, -1, 0):
            y = shift(place.y, step)
            links.go(
                ("s", kv, slot, step), parts[kv].at[slot, y, 1 - place.core],
                twin.at[kv, slot, y], place.sibling(),
            )

    for kv, slot in PARTS:
        send_twin(kv, slot)
    mine = place.z // 2
    for which, (src, dst) in enumerate(((att_in, attended), (dq_in, query_grad))):
        for step in STEPS:
            links.go(
                ("q", which, step), src.at[shift(place.z, step)], dst.at[:, cols(place.z)],
                place.ring("z", step),
            )
        links.go(
            ("q", which, "partner"), src.at[SIDE + 1], dst.at[:, cols(SIDE + mine)],
            place.partner(),
        )
        own.append(links.here(("q", which, 0), src.at[place.z], dst.at[:, cols(place.z)]))
        own.append(links.here(("q", which, 1), src.at[SIDE], dst.at[:, cols(SIDE + mine)]))
    hot = slot_hot_of(assign)
    divisor = jnp.maximum(jnp.sum(hot, axis=1, keepdims=True), 1.0)
    hot = hot.astype(BF)

    def stage(kv, slot):
        first, count = GROUPS[slot]
        half_in, full_in, out = halves.at[kv, slot], fulls.at[kv, slot], outgoing.at[kv, slot]

        def term(step):
            y = shift(place.y, step)
            links.got(("s", kv, slot, step), twin.at[kv, slot, y])
            return parts[kv][slot, y, place.core].astype(F32) + twin[kv, slot, y].astype(F32)

        def start():
            out[2] = term(2).astype(BF)
            links.go(("h", kv, slot, 1), low(out.at[2]), half_in.at[0], place.ring("y", 1))
            links.go(("h", kv, slot, -1), high(out.at[2]), half_in.at[1], place.ring("y", -1))

        def relay():
            ahead = term(1)
            behind = term(-1)
            half = SIDE // 2
            links.got(("h", kv, slot, 1), half_in.at[0])
            out[0, 0:half] = (ahead[0:half] + half_in[0].astype(F32)).astype(BF)
            out[0, half:SIDE] = ahead[half:SIDE].astype(BF)
            links.go(("y", kv, slot, 1), out.at[0], full_in.at[0], place.ring("y", 1))
            links.got(("h", kv, slot, -1), half_in.at[1])
            out[1, 0:half] = behind[0:half].astype(BF)
            out[1, half:SIDE] = (behind[half:SIDE] + half_in[1].astype(F32)).astype(BF)
            links.go(("y", kv, slot, -1), out.at[1], full_in.at[1], place.ring("y", -1))

        def row():
            total = term(0)
            links.got(("y", kv, slot, 1), full_in.at[0])
            links.got(("y", kv, slot, -1), full_in.at[1])
            total = total + full_in[0].astype(F32) + full_in[1].astype(F32)
            column[kv, slot] = total.astype(BF)
            for step in STEPS:
                links.go(
                    ("z", kv, slot, step), column.at[kv, slot, shift(place.z, step)],
                    pieces.at[kv, slot, place.z], place.ring("z", step),
                )
            pieces[kv, slot, place.z] = column[kv, slot, place.z]

        def expand():
            for step in STEPS:
                links.got(("z", kv, slot, step), pieces.at[kv, slot, shift(place.z, -step)])
            ready = [pieces[kv, slot, z].astype(F32) for z in range(SIDE)]
            if slot == 1:
                ready = [ready[0] + ready[1], ready[2] + ready[3]]
            mean = jnp.concatenate([(one / divisor).astype(BF) for one in ready], axis=1)
            tokens[kv, :, first * HD : (first + count) * HD] = lax.dot_general(
                hot, mean, (((0,), (0,)), ((), ())), preferred_element_type=F32
            ).astype(BF)
            to = cols(place.x * HEADS_X + first, count)
            for step in STEPS:
                links.go(
                    ("x", kv, slot, step),
                    tokens.at[kv, token_rows(shift(place.x, step)), cols(first, count)],
                    outs[kv].at[:, to],
                    place.ring("x", step),
                )
            own.append(
                links.here(
                    ("x", kv, slot),
                    tokens.at[kv, token_rows(place.x), cols(first, count)],
                    outs[kv].at[:, to],
                )
            )

        return [start, relay, row, expand]

    run_rounds([stage(kv, slot) for kv, slot in PARTS], 1)

    for which, dst in enumerate((attended, query_grad)):
        for step in STEPS:
            links.got(("q", which, step), dst.at[:, cols(shift(place.z, -step))])
        links.got(("q", which, "partner"), dst.at[:, cols(SIDE + 1 - mine)])
    for kv, slot in PARTS:
        first, count = GROUPS[slot]
        for step in STEPS:
            links.got(
                ("x", kv, slot, step),
                outs[kv].at[:, cols(shift(place.x, -step) * HEADS_X + first, count)],
            )
    for copy in own:
        copy.wait()
    links.finish()


ANY = pl.BlockSpec(memory_space=pl.ANY)
VMEM = pl.BlockSpec(memory_space=pltpu.VMEM)
SMEM = pl.BlockSpec(memory_space=pltpu.SMEM)
ALL_FRAMES = SIDE * SIDE * CORES


def body(queries, keys_in, values_in, grad_out, assign, pattern, live_blocks):
    assign_rows = jnp.broadcast_to(assign[None, :], (8, TOK))
    shape = jax.ShapeDtypeStruct
    dma = pltpu.SemaphoreType.DMA
    spread = (2, SIDE, CORES, SIDE, SLOTS, HD)
    every_key, every_value, query_units, upstream_units = pl.pallas_call(
        gather_kernel,
        out_shape=(
            shape(spread, BF),
            shape(spread, BF),
            shape((UNITS, TOK, HD), BF),
            shape((UNITS, TOK, HD), BF),
        ),
        in_specs=[ANY, ANY, ANY, ANY, VMEM],
        out_specs=(VMEM, VMEM, ANY, ANY),
        scratch_shapes=[
            pltpu.VMEM((2, TOK, WIDTH), BF),
            pltpu.VMEM((2, HEADS_X, SLOTS, HD), BF),
            dma((GATHER_SEMS,)),
            dma((GATHER_SEMS,)),
            dma((GATHER_LOCAL,)),
        ],
        compiler_params=pltpu.CompilerParams(
            collective_id=0, has_side_effects=True, vmem_limit_bytes=VMEM_LIMIT
        ),
        name="gather",
    )(keys_in, values_in, queries, grad_out, assign_rows)

    blocks = (2, ALL_FRAMES * SLOTS // KB, KB, HD)

    def head_block():
        return pl.BlockSpec((1,) + blocks[1:], lambda u: (u // SIDE, 0, 0, 0))

    def token_block():
        return pl.BlockSpec((1, TOK, HD), lambda u: (u, 0, 0))

    att_units, dq_units, key_part, value_part = pl.pallas_call(
        attention_kernel,
        grid=(UNITS,),
        out_shape=(
            shape((UNITS, TOK, HD), BF),
            shape((UNITS, TOK, HD), BF),
            shape(blocks, BF),
            shape(blocks, BF),
        ),
        in_specs=[SMEM, SMEM, head_block(), head_block(), token_block(), token_block()],
        out_specs=(token_block(), token_block(), head_block(), head_block()),
        scratch_shapes=[
            pltpu.VMEM((NSEL * KB, HD), BF),
            pltpu.VMEM((NSEL * KB, HD), BF),
            pltpu.VMEM((NSEL * KB, TOK), F32),
            pltpu.VMEM((NSEL * KB, HD), F32),
            pltpu.VMEM((NSEL * KB, HD), F32),
        ],
        compiler_params=pltpu.CompilerParams(vmem_limit_bytes=VMEM_LIMIT),
        name="attention",
    )(
        pattern, live_blocks, every_key.reshape(blocks), every_value.reshape(blocks),
        query_units, upstream_units,
    )

    return pl.pallas_call(
        scatter_kernel,
        out_shape=(
            shape(queries.shape, BF),
            shape(queries.shape, BF),
            shape(keys_in.shape, BF),
            shape(keys_in.shape, BF),
        ),
        in_specs=[VMEM, VMEM, ANY, ANY, VMEM],
        out_specs=(ANY, ANY, ANY, ANY),
        scratch_shapes=[
            pltpu.VMEM((2, 2, SIDE, SIDE, SLOTS, HD), BF),
            pltpu.VMEM((2, 2, 2, SIDE // 2, SLOTS, HD), BF),
            pltpu.VMEM((2, 2, 2, SIDE, SLOTS, HD), BF),
            pltpu.VMEM((2, 2, 3, SIDE, SLOTS, HD), BF),
            pltpu.VMEM((2, 2, SIDE, SLOTS, HD), BF),
            pltpu.VMEM((2, 2, SIDE, SLOTS, HD), BF),
            pltpu.VMEM((2, TOK, WIDTH), BF),
            dma((SCATTER_SEMS,)),
            dma((SCATTER_SEMS,)),
            dma((SCATTER_LOCAL,)),
        ],
        compiler_params=pltpu.CompilerParams(
            collective_id=1, has_side_effects=True, vmem_limit_bytes=VMEM_LIMIT
        ),
        name="scatter",
    )(key_part.reshape(spread), value_part.reshape(spread), att_units, dq_units, assign_rows)


def solution(mesh):
    return jax.shard_map(
        body,
        mesh=mesh,
        in_specs=(
            P("frame", "head"),
            P(("frame", "head"), None),
            P(("frame", "head"), None),
            P("frame", "head"),
            P("frame"),
            P(),
            P(),
        ),
        out_specs=(
            P("frame", "head"),
            P("frame", "head"),
            P(("frame", "head"), None),
            P(("frame", "head"), None),
        ),
        check_vma=False,
    )
```

```python
import functools
import math

import jax
import jax.numpy as jnp
from jax import lax
from jax.experimental import pallas as pl
from jax.experimental.pallas import tpu as pltpu
from jax.sharding import PartitionSpec as P

HD = 128
KB = 64
NSEL = 16
SIZES = (256, 512, 768, 1024)
SIDE = 4
CORES = 2
HEADS_X = 6
WIDTH = HEADS_X * HD
TOK = 512
TOK_DEV = TOK // SIDE
SLOTS = 128
UNITS = 6
CHUNK = 512
SCALE = 1.0 / math.sqrt(HD)
MESH = pl.DeviceIdType.MESH
BF = jnp.bfloat16
F32 = jnp.float32
VMEM_LIMIT = 20 * 1024 * 1024
LOG2_E = math.log2(math.e)
STEPS = (1, -1, 2)
GROUPS = ((0, SIDE), (SIDE, HEADS_X - SIDE))
GATHER_PARTS = ((0, 1), (1, 1), (0, 0), (1, 0))
SCATTER_PARTS = ((1, 0), (0, 0), (1, 1), (0, 1))
GATHER_STRAIGHT = GATHER_PARTS[2:]
SCATTER_STRAIGHT = SCATTER_PARTS[:1]


class Place:
    def __init__(self):
        frame = lax.axis_index("frame")
        self.x = lax.axis_index("head")
        self.core = frame % CORES
        self.z = (frame // CORES) % SIDE
        self.y = frame // (CORES * SIDE)

    def device(self, y, z, core, x):
        return {"frame": (y * SIDE + z) * CORES + core, "head": x}

    def ring(self, axis, step):
        at = {"x": self.x, "y": self.y, "z": self.z}
        at[axis] = (at[axis] + step + SIDE) % SIDE
        return self.device(at["y"], at["z"], self.core, at["x"])

    def sibling(self):
        return self.device(self.y, self.z, 1 - self.core, self.x)

    def partner(self):
        return self.device(self.y, SIDE - 1 - self.z, self.core, self.x)


def shift(at, step):
    return (at + step + SIDE) % SIDE


def meet(place):
    partners = [place.sibling()]
    partners += [place.ring(axis, step) for axis in ("x", "y", "z") for step in STEPS]
    barrier = pltpu.get_barrier_semaphore()
    for target in partners:
        pl.semaphore_signal(barrier, inc=1, device_id=target, device_id_type=MESH)
    pl.semaphore_wait(barrier, len(partners))


class Links:
    def __init__(self, place, send, recv, local):
        self.send, self.recv, self.local = send, recv, local
        self.anyone = place.sibling()
        self.started = []
        self.names = {}
        self.local_names = {}

    def sem(self, name):
        return self.names.setdefault(name, len(self.names))

    def remote(self, name, src, dst, target):
        sem = self.sem(name)
        return pltpu.make_async_remote_copy(
            src_ref=src,
            dst_ref=dst,
            send_sem=self.send.at[sem],
            recv_sem=self.recv.at[sem],
            device_id=target,
            device_id_type=MESH,
        )

    def go(self, name, src, dst, target):
        copy = self.remote(name, src, dst, target)
        copy.start()
        self.started.append(copy)

    def got(self, name, region):
        self.remote(name, region, region, self.anyone).wait_recv()

    def here(self, name, src, dst):
        sem = self.local_names.setdefault(name, len(self.local_names))
        copy = pltpu.make_async_copy(src, dst, self.local.at[sem])
        copy.start()
        return copy

    def finish(self):
        for copy in self.started:
            copy.wait_send()


def low(ref):
    return ref.at[pl.ds(0, SIDE // 2)]


def high(ref):
    return ref.at[pl.ds(SIDE // 2, SIDE // 2)]


def cols(head, count=1):
    return pl.ds(pl.multiple_of(head * HD, HD), count * HD)


def token_rows(x):
    return pl.ds(pl.multiple_of(x * TOK_DEV, TOK_DEV), TOK_DEV)


def slot_hot_of(assign):
    slots = lax.broadcasted_iota(jnp.int32, (SLOTS, TOK), 0)
    return (slots == assign[0:1, :]).astype(F32)


def run_rounds(stages, stagger):
    ticks = {}
    for i, rounds in enumerate(stages):
        for r, step in enumerate(rounds):
            ticks.setdefault(i * stagger + r, []).append((-i, step))
    for tick in sorted(ticks):
        for _, step in sorted(ticks[tick], key=lambda item: item[0]):
            step()


GATHER_SEMS = len(GATHER_PARTS) * 14 + 2 * 4
GATHER_LOCAL = len(GATHER_PARTS) + 4


def gather_kernel(
    keys, values, queries, upstream, assign,
    every_key, every_value, query_out, upstream_out,
    tokens, merged, send, recv, local,
):
    place = Place()
    meet(place)
    links = Links(place, send, recv, local)
    sources = (keys, values)
    every = (every_key, every_value)
    own = {}

    def send_tokens(kv, slot):
        first, count = GROUPS[slot]
        for step in STEPS:
            links.go(
                ("x", kv, slot, step),
                sources[kv].at[:, cols(shift(place.x, step) * HEADS_X + first, count)],
                tokens.at[kv, token_rows(place.x), cols(first, count)],
                place.ring("x", step),
            )
        own[kv, slot] = links.here(
            ("x", kv, slot),
            sources[kv].at[:, cols(place.x * HEADS_X + first, count)],
            tokens.at[kv, token_rows(place.x), cols(first, count)],
        )

    def send_queries(which):
        src, dst = ((queries, query_out), (upstream, upstream_out))[which]
        for step in STEPS:
            links.go(
                ("q", which, step), src.at[:, cols(shift(place.z, step))], dst.at[place.z],
                place.ring("z", step),
            )
        mine = place.z // 2
        links.go(
            ("q", which, "partner"), src.at[:, cols(SIDE + 1 - mine)], dst.at[SIDE + 1],
            place.partner(),
        )
        own["q", which, 0] = links.here(("q", which, 0), src.at[:, cols(place.z)], dst.at[place.z])
        own["q", which, 1] = links.here(
            ("q", which, 1), src.at[:, cols(SIDE + mine)], dst.at[SIDE]
        )

    send_tokens(*GATHER_PARTS[0])
    send_tokens(*GATHER_PARTS[1])
    send_queries(0)
    send_tokens(*GATHER_PARTS[2])
    send_tokens(*GATHER_PARTS[3])
    hot = slot_hot_of(assign)
    divisor = jnp.maximum(jnp.sum(hot, axis=1, keepdims=True), 1.0)
    hot = hot.astype(BF)

    def stage(kv, slot):
        first, count = GROUPS[slot]
        out = every[kv]
        straight = (kv, slot) in GATHER_STRAIGHT

        def region(step):
            return out.at[slot, shift(place.y, step), place.core]

        def pass_on(step):
            links.go(("s", kv, slot, step), region(step), region(step), place.sibling())

        def merge():
            own[kv, slot].wait()
            for step in STEPS:
                links.got(
                    ("x", kv, slot, step),
                    tokens.at[kv, token_rows(shift(place.x, -step)), cols(first, count)],
                )
            sums = jnp.dot(
                hot, tokens[kv, :, first * HD : (first + count) * HD], preferred_element_type=F32
            )
            mean = (sums / divisor).astype(BF)
            for i in range(count):
                merged[kv, first + i] = mean[:, i * HD : (i + 1) * HD]

            def head_of(z):
                return z if slot == 0 else SIDE + z // 2

            for step in STEPS:
                links.go(
                    ("z", kv, slot, step),
                    merged.at[kv, head_of(shift(place.z, step))],
                    out.at[slot, place.y, place.core, place.z],
                    place.ring("z", step),
                )
            out[slot, place.y, place.core, place.z] = merged[kv, head_of(place.z)]
            if (kv, slot) == GATHER_PARTS[0]:
                send_queries(1)

        def row():
            for step in STEPS:
                links.got(
                    ("z", kv, slot, step),
                    out.at[slot, place.y, place.core, shift(place.z, -step)],
                )
            for step in STEPS if straight else STEPS[:2]:
                links.go(("y", kv, slot, step), region(0), region(0), place.ring("y", step))
            pass_on(0)

        def near():
            links.got(("y", kv, slot, 1), region(-1))
            if not straight:
                links.go(("f", kv, slot, 1), low(region(-1)), low(region(-1)), place.ring("y", 1))
            pass_on(-1)
            links.got(("y", kv, slot, -1), region(1))
            if not straight:
                links.go(("f", kv, slot, -1), high(region(1)), high(region(1)), place.ring("y", -1))
            pass_on(1)

        def far():
            if straight:
                links.got(("y", kv, slot, 2), region(2))
            else:
                links.got(("f", kv, slot, 1), low(region(2)))
                links.got(("f", kv, slot, -1), high(region(2)))
            pass_on(2)

        def close():
            for step in (0, -1, 1, 2):
                links.got(
                    ("s", kv, slot, step), out.at[slot, shift(place.y, step), 1 - place.core]
                )

        return [merge, row, near, far, close]

    run_rounds([stage(kv, slot) for kv, slot in GATHER_PARTS], 1)
    for which, dst in enumerate((query_out, upstream_out)):
        for step in STEPS:
            links.got(("q", which, step), dst.at[shift(place.z, -step)])
        links.got(("q", which, "partner"), dst.at[SIDE + 1])
        own["q", which, 0].wait()
        own["q", which, 1].wait()
    links.finish()


def attention_kernel(
    pattern, live, keys, values, query, upstream,
    attended, query_grad, key_grad, value_grad,
    ksel, vsel, expo, prob_grad, kpart, vpart,
):
    place = Place()
    key_grad[...] = jnp.zeros_like(key_grad)
    value_grad[...] = jnp.zeros_like(value_grad)

    def spot_of(block):
        owner = block // 2
        y, z, core = owner // (CORES * SIDE), (owner // CORES) % SIDE, owner % CORES
        return ((y * CORES + core) * SIDE + z) * 2 + block % 2

    def unit_step(unit, carry):
        slot = unit // SIDE
        unit_z = jnp.where(unit < SIDE, unit, jnp.where(unit == SIDE, place.z, SIDE - 1 - place.z))
        frame = (place.y * SIDE + unit_z) * CORES + place.core
        count = live[frame]
        rows_live = count * KB

        def attend(least, rows):
            for j in range(rows // KB):
                spot = spot_of(pattern[j, frame])
                ksel[j * KB : (j + 1) * KB, :] = keys[slot, spot]
                vsel[j * KB : (j + 1) * KB, :] = values[slot, spot]
            q, g = query[unit], upstream[unit]
            q_t, g_t = q.T, g.T
            spans = [(a, min(a + CHUNK, rows)) for a in range(0, rows, CHUNK)]
            top = jnp.full((1, TOK), -jnp.inf, F32)
            for a, b in spans:
                scores = jnp.dot(ksel[a:b, :], q_t, preferred_element_type=F32)
                if b > least:
                    ids = lax.broadcasted_iota(jnp.int32, (b - a, TOK), 0) + a
                    scores = jnp.where(ids < rows_live, scores, -jnp.inf)
                expo[a:b, :] = scores
                top = jnp.maximum(top, jnp.max(scores, axis=0, keepdims=True))
                prob_grad[a:b, :] = jnp.dot(vsel[a:b, :], g_t, preferred_element_type=F32)
            top = top * (SCALE * LOG2_E)
            total = jnp.zeros((1, TOK), F32)
            weighted = jnp.zeros((HD, TOK), F32)
            for a, b in spans:
                weights = jnp.exp2(expo[a:b, :] * (SCALE * LOG2_E) - top)
                expo[a:b, :] = weights
                total = total + jnp.sum(weights, axis=0, keepdims=True)
                weighted = weighted + lax.dot_general(
                    vsel[a:b, :], weights.astype(BF), (((0,), (0,)), ((), ())),
                    preferred_element_type=F32,
                )
            inverse = 1.0 / total
            att_t = (weighted * inverse).astype(BF)
            attended[unit] = att_t.T
            delta = jnp.sum(g_t.astype(F32) * att_t.astype(F32), axis=0, keepdims=True)
            dq = jnp.zeros((HD, TOK), F32)
            for a, b in spans:
                probs = expo[a:b, :] * inverse
                score_grad = (probs * (prob_grad[a:b, :] - delta)).astype(BF)
                kpart[a:b, :] = (
                    jnp.dot(score_grad, q, preferred_element_type=F32) * SCALE
                ).astype(BF)
                vpart[a:b, :] = jnp.dot(
                    probs.astype(BF), g, preferred_element_type=F32
                ).astype(BF)
                dq = dq + lax.dot_general(
                    ksel[a:b, :], score_grad, (((0,), (0,)), ((), ())), preferred_element_type=F32
                )
            query_grad[unit] = (dq * SCALE).astype(BF).T
            for j in range(rows // KB):

                def add(j=j):
                    spot = spot_of(pattern[j, frame])
                    for out, part in ((key_grad, kpart), (value_grad, vpart)):
                        piece = part[j * KB : (j + 1) * KB, :].astype(F32)
                        out[slot, spot] = (out[slot, spot].astype(F32) + piece).astype(BF)

                if j * KB < least:
                    add()
                else:
                    pl.when(j < count)(add)

        least = 0
        for rows in SIZES:
            pl.when((rows_live > least) & (rows_live <= rows))(
                functools.partial(attend, least, rows)
            )
            least = rows
        return carry

    lax.fori_loop(0, UNITS, unit_step, 0)


SCATTER_SEMS = len(SCATTER_PARTS) * 14 + 2 * 4
SCATTER_LOCAL = len(SCATTER_PARTS) + 4


def scatter_kernel(
    key_part, value_part, att_in, dq_in, assign,
    attended, query_grad, grad_keys, grad_values,
    twin, halves, fulls, outgoing, column, pieces, tokens, send, recv, local,
):
    place = Place()
    meet(place)
    links = Links(place, send, recv, local)
    parts = (key_part, value_part)
    outs = (grad_keys, grad_values)
    own = []

    def send_twin(kv, slot):
        for step in (2, 1, -1, 0):
            y = shift(place.y, step)
            links.go(
                ("s", kv, slot, step), parts[kv].at[slot, y, 1 - place.core],
                twin.at[kv, slot, y], place.sibling(),
            )

    for kv, slot in SCATTER_PARTS:
        send_twin(kv, slot)
    mine = place.z // 2
    for which, (src, dst) in enumerate(((att_in, attended), (dq_in, query_grad))):
        for step in STEPS:
            links.go(
                ("q", which, step), src.at[shift(place.z, step)], dst.at[:, cols(place.z)],
                place.ring("z", step),
            )
        links.go(
            ("q", which, "partner"), src.at[SIDE + 1], dst.at[:, cols(SIDE + mine)],
            place.partner(),
        )
        own.append(links.here(("q", which, 0), src.at[place.z], dst.at[:, cols(place.z)]))
        own.append(links.here(("q", which, 1), src.at[SIDE], dst.at[:, cols(SIDE + mine)]))
    hot = slot_hot_of(assign)
    divisor = jnp.maximum(jnp.sum(hot, axis=1, keepdims=True), 1.0)
    hot = hot.astype(BF)

    def stage(kv, slot):
        first, count = GROUPS[slot]
        straight = (kv, slot) in SCATTER_STRAIGHT
        half_in, full_in, out = halves.at[kv, slot], fulls.at[kv, slot], outgoing.at[kv, slot]

        def term(step):
            y = shift(place.y, step)
            links.got(("s", kv, slot, step), twin.at[kv, slot, y])
            return parts[kv][slot, y, place.core].astype(F32) + twin[kv, slot, y].astype(F32)

        def start():
            out[2] = term(2).astype(BF)
            if straight:
                links.go(("y", kv, slot, 2), out.at[2], full_in.at[2], place.ring("y", 2))
                return
            links.go(("h", kv, slot, 1), low(out.at[2]), half_in.at[0], place.ring("y", 1))
            links.go(("h", kv, slot, -1), high(out.at[2]), half_in.at[1], place.ring("y", -1))

        def relay():
            ahead = term(1)
            behind = term(-1)
            half = SIDE // 2
            if straight:
                for at, step, value in ((0, 1, ahead), (1, -1, behind)):
                    out[at] = value.astype(BF)
                    links.go(
                        ("y", kv, slot, step), out.at[at], full_in.at[at], place.ring("y", step)
                    )
                return
            links.got(("h", kv, slot, 1), half_in.at[0])
            out[0, 0:half] = (ahead[0:half] + half_in[0].astype(F32)).astype(BF)
            out[0, half:SIDE] = ahead[half:SIDE].astype(BF)
            links.go(("y", kv, slot, 1), out.at[0], full_in.at[0], place.ring("y", 1))
            links.got(("h", kv, slot, -1), half_in.at[1])
            out[1, 0:half] = behind[0:half].astype(BF)
            out[1, half:SIDE] = (behind[half:SIDE] + half_in[1].astype(F32)).astype(BF)
            links.go(("y", kv, slot, -1), out.at[1], full_in.at[1], place.ring("y", -1))

        def row():
            total = term(0)
            links.got(("y", kv, slot, 1), full_in.at[0])
            links.got(("y", kv, slot, -1), full_in.at[1])
            total = total + full_in[0].astype(F32) + full_in[1].astype(F32)
            if straight:
                links.got(("y", kv, slot, 2), full_in.at[2])
                total = total + full_in[2].astype(F32)
            column[kv, slot] = total.astype(BF)
            for step in STEPS:
                links.go(
                    ("z", kv, slot, step), column.at[kv, slot, shift(place.z, step)],
                    pieces.at[kv, slot, place.z], place.ring("z", step),
                )
            pieces[kv, slot, place.z] = column[kv, slot, place.z]

        def expand():
            for step in STEPS:
                links.got(("z", kv, slot, step), pieces.at[kv, slot, shift(place.z, -step)])
            ready = [pieces[kv, slot, z].astype(F32) for z in range(SIDE)]
            if slot == 1:
                ready = [ready[0] + ready[1], ready[2] + ready[3]]
            mean = jnp.concatenate([(one / divisor).astype(BF) for one in ready], axis=1)
            tokens[kv, :, first * HD : (first + count) * HD] = lax.dot_general(
                hot, mean, (((0,), (0,)), ((), ())), preferred_element_type=F32
            ).astype(BF)
            to = cols(place.x * HEADS_X + first, count)
            for step in STEPS:
                links.go(
                    ("x", kv, slot, step),
                    tokens.at[kv, token_rows(shift(place.x, step)), cols(first, count)],
                    outs[kv].at[:, to],
                    place.ring("x", step),
                )
            own.append(
                links.here(
                    ("x", kv, slot),
                    tokens.at[kv, token_rows(place.x), cols(first, count)],
                    outs[kv].at[:, to],
                )
            )

        return [start, relay, row, expand]

    run_rounds([stage(kv, slot) for kv, slot in SCATTER_PARTS], 1)

    for which, dst in enumerate((attended, query_grad)):
        for step in STEPS:
            links.got(("q", which, step), dst.at[:, cols(shift(place.z, -step))])
        links.got(("q", which, "partner"), dst.at[:, cols(SIDE + 1 - mine)])
    for kv, slot in SCATTER_PARTS:
        first, count = GROUPS[slot]
        for step in STEPS:
            links.got(
                ("x", kv, slot, step),
                outs[kv].at[:, cols(shift(place.x, -step) * HEADS_X + first, count)],
            )
    for copy in own:
        copy.wait()
    links.finish()


ANY = pl.BlockSpec(memory_space=pl.ANY)
HBM = pl.BlockSpec(memory_space=pltpu.HBM)
VMEM = pl.BlockSpec(memory_space=pltpu.VMEM)
SMEM = pl.BlockSpec(memory_space=pltpu.SMEM)
ALL_FRAMES = SIDE * SIDE * CORES


def body(queries, keys_in, values_in, grad_out, assign, pattern, live_blocks):
    assign_rows = assign.reshape(1, TOK)
    shape = jax.ShapeDtypeStruct
    dma = pltpu.SemaphoreType.DMA
    spread = (2, SIDE, CORES, SIDE, SLOTS, HD)
    every_key, every_value, query_units, upstream_units = pl.pallas_call(
        gather_kernel,
        out_shape=(
            shape(spread, BF),
            shape(spread, BF),
            shape((UNITS, TOK, HD), BF),
            shape((UNITS, TOK, HD), BF),
        ),
        in_specs=[HBM, HBM, HBM, HBM, VMEM],
        out_specs=(VMEM, VMEM, VMEM, VMEM),
        scratch_shapes=[
            pltpu.VMEM((2, TOK, WIDTH), BF),
            pltpu.VMEM((2, HEADS_X, SLOTS, HD), BF),
            dma((GATHER_SEMS,)),
            dma((GATHER_SEMS,)),
            dma((GATHER_LOCAL,)),
        ],
        compiler_params=pltpu.CompilerParams(
            collective_id=0, has_side_effects=True, vmem_limit_bytes=VMEM_LIMIT
        ),
        name="gather",
    )(keys_in, values_in, queries, grad_out, assign_rows)

    blocks = (2, ALL_FRAMES * SLOTS // KB, KB, HD)

    att_units, dq_units, key_part, value_part = pl.pallas_call(
        attention_kernel,
        out_shape=(
            shape((UNITS, TOK, HD), BF),
            shape((UNITS, TOK, HD), BF),
            shape(blocks, BF),
            shape(blocks, BF),
        ),
        in_specs=[SMEM, SMEM, VMEM, VMEM, VMEM, VMEM],
        out_specs=(VMEM, VMEM, VMEM, VMEM),
        scratch_shapes=[
            pltpu.VMEM((NSEL * KB, HD), BF),
            pltpu.VMEM((NSEL * KB, HD), BF),
            pltpu.VMEM((NSEL * KB, TOK), F32),
            pltpu.VMEM((NSEL * KB, TOK), F32),
            pltpu.VMEM((NSEL * KB, HD), BF),
            pltpu.VMEM((NSEL * KB, HD), BF),
        ],
        compiler_params=pltpu.CompilerParams(vmem_limit_bytes=VMEM_LIMIT),
        name="attention",
    )(
        pattern.T, live_blocks, every_key.reshape(blocks), every_value.reshape(blocks),
        query_units, upstream_units,
    )

    return pl.pallas_call(
        scatter_kernel,
        out_shape=(
            shape(queries.shape, BF),
            shape(queries.shape, BF),
            shape(keys_in.shape, BF),
            shape(keys_in.shape, BF),
        ),
        in_specs=[VMEM, VMEM, VMEM, VMEM, VMEM],
        out_specs=(ANY, ANY, ANY, ANY),
        scratch_shapes=[
            pltpu.VMEM((2, 2, SIDE, SIDE, SLOTS, HD), BF),
            pltpu.VMEM((2, 2, 2, SIDE // 2, SLOTS, HD), BF),
            pltpu.VMEM((2, 2, 3, SIDE, SLOTS, HD), BF),
            pltpu.VMEM((2, 2, 3, SIDE, SLOTS, HD), BF),
            pltpu.VMEM((2, 2, SIDE, SLOTS, HD), BF),
            pltpu.VMEM((2, 2, SIDE, SLOTS, HD), BF),
            pltpu.VMEM((2, TOK, WIDTH), BF),
            dma((SCATTER_SEMS,)),
            dma((SCATTER_SEMS,)),
            dma((SCATTER_LOCAL,)),
        ],
        compiler_params=pltpu.CompilerParams(
            collective_id=1, has_side_effects=True, vmem_limit_bytes=VMEM_LIMIT
        ),
        name="scatter",
    )(key_part.reshape(spread), value_part.reshape(spread), att_units, dq_units, assign_rows)


def solution(mesh):
    return jax.shard_map(
        body,
        mesh=mesh,
        in_specs=(
            P("frame", "head"),
            P(("frame", "head"), None),
            P(("frame", "head"), None),
            P("frame", "head"),
            P("frame"),
            P(),
            P(),
        ),
        out_specs=(
            P("frame", "head"),
            P("frame", "head"),
            P(("frame", "head"), None),
            P(("frame", "head"), None),
        ),
        check_vma=False,
    )
```

```python
import functools
import math

import jax
import jax.numpy as jnp
from jax import lax
from jax.experimental import pallas as pl
from jax.experimental.pallas import tpu as pltpu
from jax.sharding import PartitionSpec as P

HD = 128
KB = 64
NSEL = 16
SIZES = (256, 512, 768, 1024)
SIDE = 4
CORES = 2
HEADS_X = 6
WIDTH = HEADS_X * HD
TOK = 512
TOK_DEV = TOK // SIDE
SLOTS = 128
UNITS = 6
CHUNK = 512
SCALE = 1.0 / math.sqrt(HD)
MESH = pl.DeviceIdType.MESH
BF = jnp.bfloat16
F32 = jnp.float32
VMEM_LIMIT = 20 * 1024 * 1024
LOG2_E = math.log2(math.e)
STEPS = (1, -1, 2)
GROUPS = ((0, SIDE), (SIDE, HEADS_X - SIDE))
GATHER_PARTS = ((0, 1), (1, 1), (0, 0), (1, 0))
SCATTER_PARTS = ((1, 0), (0, 0), (1, 1), (0, 1))
GATHER_STRAIGHT = GATHER_PARTS[3:]
SCATTER_STRAIGHT = SCATTER_PARTS[:1]


class Place:
    def __init__(self):
        frame = lax.axis_index("frame")
        self.x = lax.axis_index("head")
        self.core = frame % CORES
        self.z = (frame // CORES) % SIDE
        self.y = frame // (CORES * SIDE)

    def device(self, y, z, core, x):
        return {"frame": (y * SIDE + z) * CORES + core, "head": x}

    def ring(self, axis, step):
        at = {"x": self.x, "y": self.y, "z": self.z}
        at[axis] = (at[axis] + step + SIDE) % SIDE
        return self.device(at["y"], at["z"], self.core, at["x"])

    def sibling(self):
        return self.device(self.y, self.z, 1 - self.core, self.x)

    def partner_z(self):
        return jnp.where(self.core == 0, self.z + 1 - 2 * (self.z % 2), SIDE - 1 - self.z)

    def partner(self):
        return self.device(self.y, self.partner_z(), self.core, self.x)


def shift(at, step):
    return (at + step + SIDE) % SIDE


def meet(place):
    partners = [place.sibling()]
    partners += [place.ring(axis, step) for axis in ("x", "y", "z") for step in STEPS]
    barrier = pltpu.get_barrier_semaphore()
    for target in partners:
        pl.semaphore_signal(barrier, inc=1, device_id=target, device_id_type=MESH)
    pl.semaphore_wait(barrier, len(partners))


class Links:
    def __init__(self, place, send, recv, local):
        self.send, self.recv, self.local = send, recv, local
        self.anyone = place.sibling()
        self.started = []
        self.names = {}
        self.local_names = {}

    def sem(self, name):
        return self.names.setdefault(name, len(self.names))

    def remote(self, name, src, dst, target):
        sem = self.sem(name)
        return pltpu.make_async_remote_copy(
            src_ref=src,
            dst_ref=dst,
            send_sem=self.send.at[sem],
            recv_sem=self.recv.at[sem],
            device_id=target,
            device_id_type=MESH,
        )

    def go(self, name, src, dst, target):
        copy = self.remote(name, src, dst, target)
        copy.start()
        self.started.append(copy)

    def got(self, name, region):
        self.remote(name, region, region, self.anyone).wait_recv()

    def here(self, name, src, dst):
        sem = self.local_names.setdefault(name, len(self.local_names))
        copy = pltpu.make_async_copy(src, dst, self.local.at[sem])
        copy.start()
        return copy

    def finish(self):
        for copy in self.started:
            copy.wait_send()


def low(ref):
    return ref.at[pl.ds(0, SIDE // 2)]


def high(ref):
    return ref.at[pl.ds(SIDE // 2, SIDE // 2)]


def cols(head, count=1):
    return pl.ds(pl.multiple_of(head * HD, HD), count * HD)


def token_rows(x):
    return pl.ds(pl.multiple_of(x * TOK_DEV, TOK_DEV), TOK_DEV)


def slot_hot_of(assign):
    slots = lax.broadcasted_iota(jnp.int32, (SLOTS, TOK), 0)
    return (slots == assign[0:1, :]).astype(F32)


MERGE, ROW, NEAR, FAR, CLOSE = range(5)
GATHER_ORDER = (
    (0, MERGE), (1, MERGE), (0, ROW), (1, ROW), (2, MERGE), (0, NEAR), (1, NEAR), (2, ROW), (0, FAR),
    (3, MERGE), (1, FAR), (3, ROW), (2, NEAR), (2, FAR), (3, NEAR), (3, FAR),
    (0, CLOSE), (1, CLOSE), (2, CLOSE), (3, CLOSE),
)
START, RELAY, TOTAL, EXPAND = range(4)
SCATTER_ORDER = (
    (0, START), (1, START), (2, START), (3, START), (0, RELAY), (1, RELAY), (2, RELAY), (3, RELAY),
    (0, TOTAL), (0, EXPAND), (1, TOTAL), (1, EXPAND), (2, TOTAL), (2, EXPAND), (3, TOTAL), (3, EXPAND),
)


GATHER_SEMS = len(GATHER_PARTS) * 14 + 2 * 4
GATHER_LOCAL = len(GATHER_PARTS) + 5


def gather_kernel(
    keys, values, queries, upstream, assign,
    every_key, every_value, query_out, upstream_out,
    tokens, merged, assign_own, send, recv, local,
):
    place = Place()
    meet(place)
    links = Links(place, send, recv, local)
    sources = (keys, values)
    every = (every_key, every_value)
    own = {}

    def send_tokens(kv, slot):
        first, count = GROUPS[slot]
        for step in STEPS:
            links.go(
                ("x", kv, slot, step),
                sources[kv].at[:, cols(shift(place.x, step) * HEADS_X + first, count)],
                tokens.at[kv, token_rows(place.x), cols(first, count)],
                place.ring("x", step),
            )
        own[kv, slot] = links.here(
            ("x", kv, slot),
            sources[kv].at[:, cols(place.x * HEADS_X + first, count)],
            tokens.at[kv, token_rows(place.x), cols(first, count)],
        )

    def send_queries(which):
        src, dst = ((queries, query_out), (upstream, upstream_out))[which]
        for step in STEPS:
            links.go(
                ("q", which, step), src.at[:, cols(shift(place.z, step))], dst.at[place.z],
                place.ring("z", step),
            )
        mine = place.z % 2
        links.go(
            ("q", which, "partner"), src.at[:, cols(SIDE + 1 - mine)], dst.at[SIDE + 1],
            place.partner(),
        )
        own["q", which, 0] = links.here(("q", which, 0), src.at[:, cols(place.z)], dst.at[place.z])
        own["q", which, 1] = links.here(
            ("q", which, 1), src.at[:, cols(SIDE + mine)], dst.at[SIDE]
        )

    send_tokens(*GATHER_PARTS[0])
    send_tokens(*GATHER_PARTS[1])
    send_queries(0)
    send_tokens(*GATHER_PARTS[2])
    send_tokens(*GATHER_PARTS[3])
    links.here("assign", assign, assign_own).wait()
    hot = slot_hot_of(assign_own)
    divisor = jnp.maximum(jnp.sum(hot, axis=1, keepdims=True), 1.0)
    hot = hot.astype(BF)

    def stage(kv, slot):
        first, count = GROUPS[slot]
        out = every[kv]
        straight = (kv, slot) in GATHER_STRAIGHT

        def region(step):
            return out.at[slot, shift(place.y, step), place.core]

        def pass_on(step):
            links.go(("s", kv, slot, step), region(step), region(step), place.sibling())

        def merge():
            own[kv, slot].wait()
            for step in STEPS:
                links.got(
                    ("x", kv, slot, step),
                    tokens.at[kv, token_rows(shift(place.x, -step)), cols(first, count)],
                )
            sums = jnp.dot(
                hot, tokens[kv, :, first * HD : (first + count) * HD], preferred_element_type=F32
            )
            mean = (sums / divisor).astype(BF)
            for i in range(count):
                merged[kv, first + i] = mean[:, i * HD : (i + 1) * HD]

            def head_of(z):
                return z if slot == 0 else SIDE + z % 2

            for step in STEPS:
                links.go(
                    ("z", kv, slot, step),
                    merged.at[kv, head_of(shift(place.z, step))],
                    out.at[slot, place.y, place.core, place.z],
                    place.ring("z", step),
                )
            out[slot, place.y, place.core, place.z] = merged[kv, head_of(place.z)]
            if (kv, slot) == GATHER_PARTS[0]:
                send_queries(1)

        def row():
            for step in STEPS:
                links.got(
                    ("z", kv, slot, step),
                    out.at[slot, place.y, place.core, shift(place.z, -step)],
                )
            for step in STEPS if straight else STEPS[:2]:
                links.go(("y", kv, slot, step), region(0), region(0), place.ring("y", step))
            pass_on(0)

        def near():
            links.got(("y", kv, slot, 1), region(-1))
            if not straight:
                links.go(("f", kv, slot, 1), low(region(-1)), low(region(-1)), place.ring("y", 1))
            pass_on(-1)
            links.got(("y", kv, slot, -1), region(1))
            if not straight:
                links.go(("f", kv, slot, -1), high(region(1)), high(region(1)), place.ring("y", -1))
            pass_on(1)

        def far():
            if straight:
                links.got(("y", kv, slot, 2), region(2))
            else:
                links.got(("f", kv, slot, 1), low(region(2)))
                links.got(("f", kv, slot, -1), high(region(2)))
            pass_on(2)

        def close():
            for step in (0, -1, 1, 2):
                links.got(
                    ("s", kv, slot, step), out.at[slot, shift(place.y, step), 1 - place.core]
                )

        return [merge, row, near, far, close]

    stages = [stage(kv, slot) for kv, slot in GATHER_PARTS]
    for part, step in GATHER_ORDER:
        stages[part][step]()
    for which, dst in enumerate((query_out, upstream_out)):
        for step in STEPS:
            links.got(("q", which, step), dst.at[shift(place.z, -step)])
        links.got(("q", which, "partner"), dst.at[SIDE + 1])
        own["q", which, 0].wait()
        own["q", which, 1].wait()
    links.finish()


def attention_kernel(
    pattern, live, keys, values, query, upstream,
    attended, query_grad, key_grad, value_grad,
    ksel, vsel, expo, prob_grad, kpart, vpart,
):
    place = Place()
    key_grad[...] = jnp.zeros_like(key_grad)
    value_grad[...] = jnp.zeros_like(value_grad)

    def spot_of(block):
        owner = block // 2
        y, z, core = owner // (CORES * SIDE), (owner // CORES) % SIDE, owner % CORES
        return ((y * CORES + core) * SIDE + z) * 2 + block % 2

    def unit_step(unit, carry):
        slot = unit // SIDE
        unit_z = jnp.where(unit < SIDE, unit, jnp.where(unit == SIDE, place.z, place.partner_z()))
        frame = (place.y * SIDE + unit_z) * CORES + place.core
        count = live[frame]
        rows_live = count * KB

        def attend(least, rows):
            for j in range(rows // KB):
                spot = spot_of(pattern[j, frame])
                ksel[j * KB : (j + 1) * KB, :] = keys[slot, spot]
                vsel[j * KB : (j + 1) * KB, :] = values[slot, spot]
            q, g = query[unit], upstream[unit]
            q_t, g_t = q.T, g.T
            spans = [(a, min(a + CHUNK, rows)) for a in range(0, rows, CHUNK)]
            top = jnp.full((1, TOK), -jnp.inf, F32)
            for a, b in spans:
                scores = jnp.dot(ksel[a:b, :], q_t, preferred_element_type=F32)
                if b > least:
                    ids = lax.broadcasted_iota(jnp.int32, (b - a, TOK), 0) + a
                    scores = jnp.where(ids < rows_live, scores, -jnp.inf)
                expo[a:b, :] = scores
                top = jnp.maximum(top, jnp.max(scores, axis=0, keepdims=True))
                prob_grad[a:b, :] = jnp.dot(vsel[a:b, :], g_t, preferred_element_type=F32)
            top = top * (SCALE * LOG2_E)
            total = jnp.zeros((1, TOK), F32)
            weighted = jnp.zeros((HD, TOK), F32)
            for a, b in spans:
                weights = jnp.exp2(expo[a:b, :] * (SCALE * LOG2_E) - top)
                expo[a:b, :] = weights
                total = total + jnp.sum(weights, axis=0, keepdims=True)
                weighted = weighted + lax.dot_general(
                    vsel[a:b, :], weights.astype(BF), (((0,), (0,)), ((), ())),
                    preferred_element_type=F32,
                )
            inverse = 1.0 / total
            att_t = (weighted * inverse).astype(BF)
            attended[unit] = att_t.T
            delta = jnp.sum(g_t.astype(F32) * att_t.astype(F32), axis=0, keepdims=True)
            dq = jnp.zeros((HD, TOK), F32)
            for a, b in spans:
                probs = expo[a:b, :] * inverse
                score_grad = (probs * (prob_grad[a:b, :] - delta)).astype(BF)
                kpart[a:b, :] = (
                    jnp.dot(score_grad, q, preferred_element_type=F32) * SCALE
                ).astype(BF)
                vpart[a:b, :] = jnp.dot(
                    probs.astype(BF), g, preferred_element_type=F32
                ).astype(BF)
                dq = dq + lax.dot_general(
                    ksel[a:b, :], score_grad, (((0,), (0,)), ((), ())), preferred_element_type=F32
                )
            query_grad[unit] = (dq * SCALE).astype(BF).T
            for j in range(rows // KB):

                def add(j=j):
                    spot = spot_of(pattern[j, frame])
                    for out, part in ((key_grad, kpart), (value_grad, vpart)):
                        piece = part[j * KB : (j + 1) * KB, :].astype(F32)
                        out[slot, spot] = (out[slot, spot].astype(F32) + piece).astype(BF)

                if j * KB < least:
                    add()
                else:
                    pl.when(j < count)(add)

        least = 0
        for rows in SIZES:
            pl.when((rows_live > least) & (rows_live <= rows))(
                functools.partial(attend, least, rows)
            )
            least = rows
        return carry

    lax.fori_loop(0, UNITS, unit_step, 0)


SCATTER_SEMS = len(SCATTER_PARTS) * 14 + 2 * 4
SCATTER_LOCAL = len(SCATTER_PARTS) + 5


def scatter_kernel(
    key_part, value_part, att_in, dq_in, assign,
    attended, query_grad, grad_keys, grad_values,
    twin, halves, fulls, outgoing, column, pieces, tokens, assign_own, send, recv, local,
):
    place = Place()
    meet(place)
    links = Links(place, send, recv, local)
    parts = (key_part, value_part)
    outs = (grad_keys, grad_values)
    own = []

    def send_twin(kv, slot):
        for step in (2, 1, -1, 0):
            y = shift(place.y, step)
            links.go(
                ("s", kv, slot, step), parts[kv].at[slot, y, 1 - place.core],
                twin.at[kv, slot, y], place.sibling(),
            )

    for kv, slot in SCATTER_PARTS:
        send_twin(kv, slot)
    mine = place.z % 2
    for which, (src, dst) in enumerate(((att_in, attended), (dq_in, query_grad))):
        for step in STEPS:
            links.go(
                ("q", which, step), src.at[shift(place.z, step)], dst.at[:, cols(place.z)],
                place.ring("z", step),
            )
        links.go(
            ("q", which, "partner"), src.at[SIDE + 1], dst.at[:, cols(SIDE + mine)],
            place.partner(),
        )
        own.append(links.here(("q", which, 0), src.at[place.z], dst.at[:, cols(place.z)]))
        own.append(links.here(("q", which, 1), src.at[SIDE], dst.at[:, cols(SIDE + mine)]))
    links.here("assign", assign, assign_own).wait()
    hot = slot_hot_of(assign_own)
    divisor = jnp.maximum(jnp.sum(hot, axis=1, keepdims=True), 1.0)
    hot = hot.astype(BF)

    def stage(kv, slot):
        first, count = GROUPS[slot]
        straight = (kv, slot) in SCATTER_STRAIGHT
        half_in, full_in, out = halves.at[kv, slot], fulls.at[kv, slot], outgoing.at[kv, slot]

        def term(step):
            y = shift(place.y, step)
            links.got(("s", kv, slot, step), twin.at[kv, slot, y])
            return parts[kv][slot, y, place.core].astype(F32) + twin[kv, slot, y].astype(F32)

        def start():
            out[2] = term(2).astype(BF)
            if straight:
                links.go(("y", kv, slot, 2), out.at[2], full_in.at[2], place.ring("y", 2))
                return
            links.go(("h", kv, slot, 1), low(out.at[2]), half_in.at[0], place.ring("y", 1))
            links.go(("h", kv, slot, -1), high(out.at[2]), half_in.at[1], place.ring("y", -1))

        def relay():
            ahead = term(1)
            behind = term(-1)
            half = SIDE // 2
            if straight:
                for at, step, value in ((0, 1, ahead), (1, -1, behind)):
                    out[at] = value.astype(BF)
                    links.go(
                        ("y", kv, slot, step), out.at[at], full_in.at[at], place.ring("y", step)
                    )
                return
            links.got(("h", kv, slot, 1), half_in.at[0])
            out[0, 0:half] = (ahead[0:half] + half_in[0].astype(F32)).astype(BF)
            out[0, half:SIDE] = ahead[half:SIDE].astype(BF)
            links.go(("y", kv, slot, 1), out.at[0], full_in.at[0], place.ring("y", 1))
            links.got(("h", kv, slot, -1), half_in.at[1])
            out[1, 0:half] = behind[0:half].astype(BF)
            out[1, half:SIDE] = (behind[half:SIDE] + half_in[1].astype(F32)).astype(BF)
            links.go(("y", kv, slot, -1), out.at[1], full_in.at[1], place.ring("y", -1))

        def row():
            total = term(0)
            links.got(("y", kv, slot, 1), full_in.at[0])
            links.got(("y", kv, slot, -1), full_in.at[1])
            total = total + full_in[0].astype(F32) + full_in[1].astype(F32)
            if straight:
                links.got(("y", kv, slot, 2), full_in.at[2])
                total = total + full_in[2].astype(F32)
            column[kv, slot] = total.astype(BF)
            for step in STEPS:
                links.go(
                    ("z", kv, slot, step), column.at[kv, slot, shift(place.z, step)],
                    pieces.at[kv, slot, place.z], place.ring("z", step),
                )
            pieces[kv, slot, place.z] = column[kv, slot, place.z]

        def expand():
            for step in STEPS:
                links.got(("z", kv, slot, step), pieces.at[kv, slot, shift(place.z, -step)])
            ready = [pieces[kv, slot, z].astype(F32) for z in range(SIDE)]
            if slot == 1:
                ready = [ready[0] + ready[2], ready[1] + ready[3]]
            mean = jnp.concatenate([(one / divisor).astype(BF) for one in ready], axis=1)
            tokens[kv, :, first * HD : (first + count) * HD] = lax.dot_general(
                hot, mean, (((0,), (0,)), ((), ())), preferred_element_type=F32
            ).astype(BF)
            to = cols(place.x * HEADS_X + first, count)
            for step in STEPS:
                links.go(
                    ("x", kv, slot, step),
                    tokens.at[kv, token_rows(shift(place.x, step)), cols(first, count)],
                    outs[kv].at[:, to],
                    place.ring("x", step),
                )
            own.append(
                links.here(
                    ("x", kv, slot),
                    tokens.at[kv, token_rows(place.x), cols(first, count)],
                    outs[kv].at[:, to],
                )
            )

        return [start, relay, row, expand]

    stages = [stage(kv, slot) for kv, slot in SCATTER_PARTS]
    for part, step in SCATTER_ORDER:
        stages[part][step]()

    for which, dst in enumerate((attended, query_grad)):
        for step in STEPS:
            links.got(("q", which, step), dst.at[:, cols(shift(place.z, -step))])
        links.got(("q", which, "partner"), dst.at[:, cols(SIDE + 1 - mine)])
    for kv, slot in SCATTER_PARTS:
        first, count = GROUPS[slot]
        for step in STEPS:
            links.got(
                ("x", kv, slot, step),
                outs[kv].at[:, cols(shift(place.x, -step) * HEADS_X + first, count)],
            )
    for copy in own:
        copy.wait()
    links.finish()


def store_kernel(*refs):
    sems = refs[-1]
    copies = [pltpu.make_async_copy(refs[i], refs[4 + i], sems.at[i]) for i in range(4)]
    for copy in copies:
        copy.start()
    for copy in copies:
        copy.wait()


ANY = pl.BlockSpec(memory_space=pl.ANY)
HBM = pl.BlockSpec(memory_space=pltpu.HBM)
VMEM = pl.BlockSpec(memory_space=pltpu.VMEM)
SMEM = pl.BlockSpec(memory_space=pltpu.SMEM)
ALL_FRAMES = SIDE * SIDE * CORES


def body(queries, keys_in, values_in, grad_out, assign, pattern, live_blocks):
    keys_in, values_in, queries, grad_out, assign_rows = (
        pltpu.with_memory_space_constraint(one, pltpu.HBM)
        for one in (keys_in, values_in, queries, grad_out, assign.reshape(1, TOK))
    )
    shape = jax.ShapeDtypeStruct
    dma = pltpu.SemaphoreType.DMA
    spread = (2, SIDE, CORES, SIDE, SLOTS, HD)
    every_key, every_value, query_units, upstream_units = pl.pallas_call(
        gather_kernel,
        out_shape=(
            shape(spread, BF),
            shape(spread, BF),
            shape((UNITS, TOK, HD), BF),
            shape((UNITS, TOK, HD), BF),
        ),
        in_specs=[HBM, HBM, HBM, HBM, HBM],
        out_specs=(VMEM, VMEM, VMEM, VMEM),
        scratch_shapes=[
            pltpu.VMEM((2, TOK, WIDTH), BF),
            pltpu.VMEM((2, HEADS_X, SLOTS, HD), BF),
            pltpu.VMEM((1, TOK), jnp.int32),
            dma((GATHER_SEMS,)),
            dma((GATHER_SEMS,)),
            dma((GATHER_LOCAL,)),
        ],
        compiler_params=pltpu.CompilerParams(
            collective_id=0, has_side_effects=True, vmem_limit_bytes=VMEM_LIMIT
        ),
        name="gather",
    )(keys_in, values_in, queries, grad_out, assign_rows)

    blocks = (2, ALL_FRAMES * SLOTS // KB, KB, HD)

    att_units, dq_units, key_part, value_part = pl.pallas_call(
        attention_kernel,
        out_shape=(
            shape((UNITS, TOK, HD), BF),
            shape((UNITS, TOK, HD), BF),
            shape(blocks, BF),
            shape(blocks, BF),
        ),
        in_specs=[SMEM, SMEM, VMEM, VMEM, VMEM, VMEM],
        out_specs=(VMEM, VMEM, VMEM, VMEM),
        scratch_shapes=[
            pltpu.VMEM((NSEL * KB, HD), BF),
            pltpu.VMEM((NSEL * KB, HD), BF),
            pltpu.VMEM((NSEL * KB, TOK), F32),
            pltpu.VMEM((NSEL * KB, TOK), F32),
            pltpu.VMEM((NSEL * KB, HD), BF),
            pltpu.VMEM((NSEL * KB, HD), BF),
        ],
        compiler_params=pltpu.CompilerParams(vmem_limit_bytes=VMEM_LIMIT),
        name="attention",
    )(
        pattern.T, live_blocks, every_key.reshape(blocks), every_value.reshape(blocks),
        query_units, upstream_units,
    )

    results = pl.pallas_call(
        scatter_kernel,
        out_shape=(
            shape(queries.shape, BF),
            shape(queries.shape, BF),
            shape(keys_in.shape, BF),
            shape(keys_in.shape, BF),
        ),
        in_specs=[VMEM, VMEM, VMEM, VMEM, HBM],
        out_specs=(ANY, ANY, ANY, ANY),
        scratch_shapes=[
            pltpu.VMEM((2, 2, SIDE, SIDE, SLOTS, HD), BF),
            pltpu.VMEM((2, 2, 2, SIDE // 2, SLOTS, HD), BF),
            pltpu.VMEM((2, 2, 3, SIDE, SLOTS, HD), BF),
            pltpu.VMEM((2, 2, 3, SIDE, SLOTS, HD), BF),
            pltpu.VMEM((2, 2, SIDE, SLOTS, HD), BF),
            pltpu.VMEM((2, 2, SIDE, SLOTS, HD), BF),
            pltpu.VMEM((2, TOK, WIDTH), BF),
            pltpu.VMEM((1, TOK), jnp.int32),
            dma((SCATTER_SEMS,)),
            dma((SCATTER_SEMS,)),
            dma((SCATTER_LOCAL,)),
        ],
        compiler_params=pltpu.CompilerParams(
            collective_id=1, has_side_effects=True, vmem_limit_bytes=VMEM_LIMIT
        ),
        name="scatter",
    )(key_part.reshape(spread), value_part.reshape(spread), att_units, dq_units, assign_rows)
    return pl.pallas_call(
        store_kernel,
        out_shape=tuple(shape(one.shape, BF) for one in results),
        in_specs=[ANY] * 4,
        out_specs=(HBM,) * 4,
        scratch_shapes=[dma((4,))],
        name="store",
    )(*results)


def solution(mesh):
    return jax.shard_map(
        body,
        mesh=mesh,
        in_specs=(
            P("frame", "head"),
            P(("frame", "head"), None),
            P(("frame", "head"), None),
            P("frame", "head"),
            P("frame"),
            P(),
            P(),
        ),
        out_specs=(
            P("frame", "head"),
            P("frame", "head"),
            P(("frame", "head"), None),
            P(("frame", "head"), None),
        ),
        check_vma=False,
    )
```

```python
import functools
import math

import jax
import jax.numpy as jnp
from jax import lax
from jax.experimental import pallas as pl
from jax.experimental.pallas import tpu as pltpu
from jax.sharding import PartitionSpec as P

HD = 128
KB = 64
NSEL = 16
SIZES = (256, 512, 768, 1024)
SIDE = 4
CORES = 2
HEADS_X = 6
WIDTH = HEADS_X * HD
TOK = 512
TOK_DEV = TOK // SIDE
SLOTS = 128
UNITS = 6
CHUNK = 512
SCALE = 1.0 / math.sqrt(HD)
MESH = pl.DeviceIdType.MESH
BF = jnp.bfloat16
F32 = jnp.float32
VMEM_LIMIT = 20 * 1024 * 1024
LOG2_E = math.log2(math.e)
STEPS = (1, -1, 2)
GROUPS = ((0, SIDE), (SIDE, HEADS_X - SIDE))
GATHER_PARTS = ((0, 1), (1, 1), (0, 0), (1, 0))
SCATTER_PARTS = ((1, 0), (0, 0), (1, 1), (0, 1))
GATHER_STRAIGHT = GATHER_PARTS[3:]
SCATTER_STRAIGHT = SCATTER_PARTS[:1]


class Place:
    def __init__(self):
        frame = lax.axis_index("frame")
        self.x = lax.axis_index("head")
        self.core = frame % CORES
        self.z = (frame // CORES) % SIDE
        self.y = frame // (CORES * SIDE)

    def device(self, y, z, core, x):
        return {"frame": (y * SIDE + z) * CORES + core, "head": x}

    def ring(self, axis, step):
        at = {"x": self.x, "y": self.y, "z": self.z}
        at[axis] = (at[axis] + step + SIDE) % SIDE
        return self.device(at["y"], at["z"], self.core, at["x"])

    def sibling(self):
        return self.device(self.y, self.z, 1 - self.core, self.x)

    def partner_z(self):
        return jnp.where(self.core == 0, self.z + 1 - 2 * (self.z % 2), SIDE - 1 - self.z)

    def partner(self):
        return self.device(self.y, self.partner_z(), self.core, self.x)


def shift(at, step):
    return (at + step + SIDE) % SIDE


def meet(place):
    partners = [place.sibling()]
    partners += [place.ring(axis, step) for axis in ("x", "y", "z") for step in STEPS]
    barrier = pltpu.get_barrier_semaphore()
    for target in partners:
        pl.semaphore_signal(barrier, inc=1, device_id=target, device_id_type=MESH)
    pl.semaphore_wait(barrier, len(partners))


class Links:
    def __init__(self, place, send, recv, local):
        self.send, self.recv, self.local = send, recv, local
        self.anyone = place.sibling()
        self.started = []
        self.names = {}
        self.local_names = {}

    def sem(self, name):
        return self.names.setdefault(name, len(self.names))

    def remote(self, name, src, dst, target):
        sem = self.sem(name)
        return pltpu.make_async_remote_copy(
            src_ref=src,
            dst_ref=dst,
            send_sem=self.send.at[sem],
            recv_sem=self.recv.at[sem],
            device_id=target,
            device_id_type=MESH,
        )

    def go(self, name, src, dst, target):
        copy = self.remote(name, src, dst, target)
        copy.start()
        self.started.append(copy)

    def got(self, name, region):
        self.remote(name, region, region, self.anyone).wait_recv()

    def here(self, name, src, dst):
        sem = self.local_names.setdefault(name, len(self.local_names))
        copy = pltpu.make_async_copy(src, dst, self.local.at[sem])
        copy.start()
        return copy

    def finish(self):
        for copy in self.started:
            copy.wait_send()


def low(ref):
    return ref.at[pl.ds(0, SIDE // 2)]


def high(ref):
    return ref.at[pl.ds(SIDE // 2, SIDE // 2)]


def cols(head, count=1):
    return pl.ds(pl.multiple_of(head * HD, HD), count * HD)


def token_rows(x):
    return pl.ds(pl.multiple_of(x * TOK_DEV, TOK_DEV), TOK_DEV)


def slot_hot_of(assign):
    slots = lax.broadcasted_iota(jnp.int32, (SLOTS, TOK), 0)
    return (slots == assign[0:1, :]).astype(F32)


MERGE, ROW, NEAR, FAR, CLOSE = range(5)
GATHER_ORDER = (
    (0, MERGE), (1, MERGE), (0, ROW), (1, ROW), (2, MERGE), (0, NEAR), (1, NEAR), (2, ROW), (0, FAR),
    (3, MERGE), (1, FAR), (3, ROW), (2, NEAR), (2, FAR), (3, NEAR), (3, FAR),
    (0, CLOSE), (1, CLOSE), (2, CLOSE), (3, CLOSE),
)
START, RELAY, TOTAL, EXPAND = range(4)
SCATTER_ORDER = (
    (0, START), (1, START), (2, START), (3, START), (0, RELAY), (1, RELAY), (2, RELAY), (3, RELAY),
    (0, TOTAL), (0, EXPAND), (1, TOTAL), (1, EXPAND), (2, TOTAL), (2, EXPAND), (3, TOTAL), (3, EXPAND),
)


GATHER_SEMS = len(GATHER_PARTS) * 14 + 2 * 4
GATHER_LOCAL = len(GATHER_PARTS) + 5


def gather_kernel(
    keys, values, queries, upstream, assign,
    every_key, every_value, query_out, upstream_out,
    tokens, merged, assign_own, send, recv, local,
):
    place = Place()
    meet(place)
    links = Links(place, send, recv, local)
    sources = (keys, values)
    every = (every_key, every_value)
    own = {}

    def send_tokens(kv, slot):
        first, count = GROUPS[slot]
        for step in STEPS:
            links.go(
                ("x", kv, slot, step),
                sources[kv].at[:, cols(shift(place.x, step) * HEADS_X + first, count)],
                tokens.at[kv, token_rows(place.x), cols(first, count)],
                place.ring("x", step),
            )
        own[kv, slot] = links.here(
            ("x", kv, slot),
            sources[kv].at[:, cols(place.x * HEADS_X + first, count)],
            tokens.at[kv, token_rows(place.x), cols(first, count)],
        )

    def send_queries(which):
        src, dst = ((queries, query_out), (upstream, upstream_out))[which]
        for step in STEPS:
            links.go(
                ("q", which, step), src.at[:, cols(shift(place.z, step))], dst.at[place.z],
                place.ring("z", step),
            )
        mine = place.z % 2
        links.go(
            ("q", which, "partner"), src.at[:, cols(SIDE + 1 - mine)], dst.at[SIDE + 1],
            place.partner(),
        )
        own["q", which, 0] = links.here(("q", which, 0), src.at[:, cols(place.z)], dst.at[place.z])
        own["q", which, 1] = links.here(
            ("q", which, 1), src.at[:, cols(SIDE + mine)], dst.at[SIDE]
        )

    send_tokens(*GATHER_PARTS[0])
    send_tokens(*GATHER_PARTS[1])
    send_queries(0)
    send_tokens(*GATHER_PARTS[2])
    send_tokens(*GATHER_PARTS[3])
    links.here("assign", assign, assign_own).wait()
    hot = slot_hot_of(assign_own)
    divisor = jnp.maximum(jnp.sum(hot, axis=1, keepdims=True), 1.0)
    hot = hot.astype(BF)

    def stage(kv, slot):
        first, count = GROUPS[slot]
        out = every[kv]
        straight = (kv, slot) in GATHER_STRAIGHT

        def region(step):
            return out.at[slot, shift(place.y, step), place.core]

        def pass_on(step):
            links.go(("s", kv, slot, step), region(step), region(step), place.sibling())

        def merge():
            own[kv, slot].wait()
            for step in STEPS:
                links.got(
                    ("x", kv, slot, step),
                    tokens.at[kv, token_rows(shift(place.x, -step)), cols(first, count)],
                )
            sums = jnp.dot(
                hot, tokens[kv, :, first * HD : (first + count) * HD], preferred_element_type=F32
            )
            mean = (sums / divisor).astype(BF)
            for i in range(count):
                merged[kv, first + i] = mean[:, i * HD : (i + 1) * HD]

            def head_of(z):
                return z if slot == 0 else SIDE + z % 2

            for step in STEPS:
                links.go(
                    ("z", kv, slot, step),
                    merged.at[kv, head_of(shift(place.z, step))],
                    out.at[slot, place.y, place.core, place.z],
                    place.ring("z", step),
                )
            out[slot, place.y, place.core, place.z] = merged[kv, head_of(place.z)]
            if (kv, slot) == GATHER_PARTS[0]:
                send_queries(1)

        def row():
            for step in STEPS:
                links.got(
                    ("z", kv, slot, step),
                    out.at[slot, place.y, place.core, shift(place.z, -step)],
                )
            for step in STEPS if straight else STEPS[:2]:
                links.go(("y", kv, slot, step), region(0), region(0), place.ring("y", step))
            pass_on(0)

        def near():
            links.got(("y", kv, slot, 1), region(-1))
            if not straight:
                links.go(("f", kv, slot, 1), low(region(-1)), low(region(-1)), place.ring("y", 1))
            pass_on(-1)
            links.got(("y", kv, slot, -1), region(1))
            if not straight:
                links.go(("f", kv, slot, -1), high(region(1)), high(region(1)), place.ring("y", -1))
            pass_on(1)

        def far():
            if straight:
                links.got(("y", kv, slot, 2), region(2))
            else:
                links.got(("f", kv, slot, 1), low(region(2)))
                links.got(("f", kv, slot, -1), high(region(2)))
            pass_on(2)

        def close():
            for step in (0, -1, 1, 2):
                links.got(
                    ("s", kv, slot, step), out.at[slot, shift(place.y, step), 1 - place.core]
                )

        return [merge, row, near, far, close]

    stages = [stage(kv, slot) for kv, slot in GATHER_PARTS]
    for part, step in GATHER_ORDER:
        stages[part][step]()
    for which, dst in enumerate((query_out, upstream_out)):
        for step in STEPS:
            links.got(("q", which, step), dst.at[shift(place.z, -step)])
        links.got(("q", which, "partner"), dst.at[SIDE + 1])
        own["q", which, 0].wait()
        own["q", which, 1].wait()
    links.finish()


def attention_kernel(
    pattern, live, keys, values, query, upstream,
    attended, query_grad, key_grad, value_grad,
    ksel, vsel, expo, prob_grad, kpart, vpart,
):
    place = Place()
    key_grad[...] = jnp.zeros_like(key_grad)
    value_grad[...] = jnp.zeros_like(value_grad)

    def spot_of(block):
        owner = block // 2
        y, z, core = owner // (CORES * SIDE), (owner // CORES) % SIDE, owner % CORES
        return ((y * CORES + core) * SIDE + z) * 2 + block % 2

    def unit_step(unit, carry):
        slot = unit // SIDE
        unit_z = jnp.where(unit < SIDE, unit, jnp.where(unit == SIDE, place.z, place.partner_z()))
        frame = (place.y * SIDE + unit_z) * CORES + place.core
        count = live[frame]
        rows_live = count * KB

        def attend(least, rows):
            for j in range(rows // KB):
                spot = spot_of(pattern[j, frame])
                ksel[j * KB : (j + 1) * KB, :] = keys[slot, spot]
                vsel[j * KB : (j + 1) * KB, :] = values[slot, spot]
            q, g = query[unit], upstream[unit]
            q_t, g_t = q.T, g.T
            spans = [(a, min(a + CHUNK, rows)) for a in range(0, rows, CHUNK)]
            top = jnp.full((1, TOK), -jnp.inf, F32)
            for a, b in spans:
                scores = jnp.dot(ksel[a:b, :], q_t, preferred_element_type=F32)
                if b > least:
                    ids = lax.broadcasted_iota(jnp.int32, (b - a, TOK), 0) + a
                    scores = jnp.where(ids < rows_live, scores, -jnp.inf)
                expo[a:b, :] = scores
                top = jnp.maximum(top, jnp.max(scores, axis=0, keepdims=True))
                prob_grad[a:b, :] = jnp.dot(vsel[a:b, :], g_t, preferred_element_type=F32)
            top = top * (SCALE * LOG2_E)
            total = jnp.zeros((1, TOK), F32)
            weighted = jnp.zeros((HD, TOK), F32)
            for a, b in spans:
                weights = jnp.exp2(expo[a:b, :] * (SCALE * LOG2_E) - top)
                expo[a:b, :] = weights
                total = total + jnp.sum(weights, axis=0, keepdims=True)
                weighted = weighted + lax.dot_general(
                    vsel[a:b, :], weights.astype(BF), (((0,), (0,)), ((), ())),
                    preferred_element_type=F32,
                )
            inverse = 1.0 / total
            att_t = (weighted * inverse).astype(BF)
            attended[unit] = att_t.T
            delta = jnp.sum(g_t.astype(F32) * att_t.astype(F32), axis=0, keepdims=True)
            dq = jnp.zeros((HD, TOK), F32)
            for a, b in spans:
                probs = expo[a:b, :] * inverse
                score_grad = (probs * (prob_grad[a:b, :] - delta)).astype(BF)
                kpart[a:b, :] = (
                    jnp.dot(score_grad, q, preferred_element_type=F32) * SCALE
                ).astype(BF)
                vpart[a:b, :] = jnp.dot(
                    probs.astype(BF), g, preferred_element_type=F32
                ).astype(BF)
                dq = dq + lax.dot_general(
                    ksel[a:b, :], score_grad, (((0,), (0,)), ((), ())), preferred_element_type=F32
                )
            query_grad[unit] = (dq * SCALE).astype(BF).T
            for j in range(rows // KB):

                def add(j=j):
                    spot = spot_of(pattern[j, frame])
                    for out, part in ((key_grad, kpart), (value_grad, vpart)):
                        piece = part[j * KB : (j + 1) * KB, :].astype(F32)
                        out[slot, spot] = (out[slot, spot].astype(F32) + piece).astype(BF)

                if j * KB < least:
                    add()
                else:
                    pl.when(j < count)(add)

        least = 0
        for rows in SIZES:
            pl.when((rows_live > least) & (rows_live <= rows))(
                functools.partial(attend, least, rows)
            )
            least = rows
        return carry

    lax.fori_loop(0, UNITS, unit_step, 0)


SCATTER_SEMS = len(SCATTER_PARTS) * 14 + 2 * 4
SCATTER_LOCAL = len(SCATTER_PARTS) + 5


def scatter_kernel(
    key_part, value_part, att_in, dq_in, assign,
    attended, query_grad, grad_keys, grad_values,
    twin, halves, fulls, outgoing, column, pieces, tokens, assign_own, send, recv, local,
):
    place = Place()
    meet(place)
    links = Links(place, send, recv, local)
    parts = (key_part, value_part)
    outs = (grad_keys, grad_values)
    own = []

    def send_twin(kv, slot):
        for step in (2, 1, -1, 0):
            y = shift(place.y, step)
            links.go(
                ("s", kv, slot, step), parts[kv].at[slot, y, 1 - place.core],
                twin.at[kv, slot, y], place.sibling(),
            )

    for kv, slot in SCATTER_PARTS:
        send_twin(kv, slot)
    mine = place.z % 2
    for which, (src, dst) in enumerate(((att_in, attended), (dq_in, query_grad))):
        for step in STEPS:
            links.go(
                ("q", which, step), src.at[shift(place.z, step)], dst.at[:, cols(place.z)],
                place.ring("z", step),
            )
        links.go(
            ("q", which, "partner"), src.at[SIDE + 1], dst.at[:, cols(SIDE + mine)],
            place.partner(),
        )
        own.append(links.here(("q", which, 0), src.at[place.z], dst.at[:, cols(place.z)]))
        own.append(links.here(("q", which, 1), src.at[SIDE], dst.at[:, cols(SIDE + mine)]))
    links.here("assign", assign, assign_own).wait()
    hot = slot_hot_of(assign_own)
    divisor = jnp.maximum(jnp.sum(hot, axis=1, keepdims=True), 1.0)
    hot = hot.astype(BF)

    def stage(kv, slot):
        first, count = GROUPS[slot]
        straight = (kv, slot) in SCATTER_STRAIGHT
        half_in, full_in, out = halves.at[kv, slot], fulls.at[kv, slot], outgoing.at[kv, slot]

        def term(step):
            y = shift(place.y, step)
            links.got(("s", kv, slot, step), twin.at[kv, slot, y])
            return parts[kv][slot, y, place.core].astype(F32) + twin[kv, slot, y].astype(F32)

        def start():
            out[2] = term(2).astype(BF)
            if straight:
                links.go(("y", kv, slot, 2), out.at[2], full_in.at[2], place.ring("y", 2))
                return
            links.go(("h", kv, slot, 1), low(out.at[2]), half_in.at[0], place.ring("y", 1))
            links.go(("h", kv, slot, -1), high(out.at[2]), half_in.at[1], place.ring("y", -1))

        def relay():
            ahead = term(1)
            behind = term(-1)
            half = SIDE // 2
            if straight:
                for at, step, value in ((0, 1, ahead), (1, -1, behind)):
                    out[at] = value.astype(BF)
                    links.go(
                        ("y", kv, slot, step), out.at[at], full_in.at[at], place.ring("y", step)
                    )
                return
            links.got(("h", kv, slot, 1), half_in.at[0])
            out[0, 0:half] = (ahead[0:half] + half_in[0].astype(F32)).astype(BF)
            out[0, half:SIDE] = ahead[half:SIDE].astype(BF)
            links.go(("y", kv, slot, 1), out.at[0], full_in.at[0], place.ring("y", 1))
            links.got(("h", kv, slot, -1), half_in.at[1])
            out[1, 0:half] = behind[0:half].astype(BF)
            out[1, half:SIDE] = (behind[half:SIDE] + half_in[1].astype(F32)).astype(BF)
            links.go(("y", kv, slot, -1), out.at[1], full_in.at[1], place.ring("y", -1))

        def row():
            total = term(0)
            links.got(("y", kv, slot, 1), full_in.at[0])
            links.got(("y", kv, slot, -1), full_in.at[1])
            total = total + full_in[0].astype(F32) + full_in[1].astype(F32)
            if straight:
                links.got(("y", kv, slot, 2), full_in.at[2])
                total = total + full_in[2].astype(F32)
            column[kv, slot] = total.astype(BF)
            for step in STEPS:
                links.go(
                    ("z", kv, slot, step), column.at[kv, slot, shift(place.z, step)],
                    pieces.at[kv, slot, place.z], place.ring("z", step),
                )
            pieces[kv, slot, place.z] = column[kv, slot, place.z]

        def expand():
            for step in STEPS:
                links.got(("z", kv, slot, step), pieces.at[kv, slot, shift(place.z, -step)])
            ready = [pieces[kv, slot, z].astype(F32) for z in range(SIDE)]
            if slot == 1:
                ready = [ready[0] + ready[2], ready[1] + ready[3]]
            mean = jnp.concatenate([(one / divisor).astype(BF) for one in ready], axis=1)
            tokens[kv, :, first * HD : (first + count) * HD] = lax.dot_general(
                hot, mean, (((0,), (0,)), ((), ())), preferred_element_type=F32
            ).astype(BF)
            to = cols(place.x * HEADS_X + first, count)
            for step in STEPS:
                links.go(
                    ("x", kv, slot, step),
                    tokens.at[kv, token_rows(shift(place.x, step)), cols(first, count)],
                    outs[kv].at[:, to],
                    place.ring("x", step),
                )
            own.append(
                links.here(
                    ("x", kv, slot),
                    tokens.at[kv, token_rows(place.x), cols(first, count)],
                    outs[kv].at[:, to],
                )
            )

        return [start, relay, row, expand]

    stages = [stage(kv, slot) for kv, slot in SCATTER_PARTS]
    for part, step in SCATTER_ORDER:
        stages[part][step]()

    for which, dst in enumerate((attended, query_grad)):
        for step in STEPS:
            links.got(("q", which, step), dst.at[:, cols(shift(place.z, -step))])
        links.got(("q", which, "partner"), dst.at[:, cols(SIDE + 1 - mine)])
    for kv, slot in SCATTER_PARTS:
        first, count = GROUPS[slot]
        for step in STEPS:
            links.got(
                ("x", kv, slot, step),
                outs[kv].at[:, cols(shift(place.x, -step) * HEADS_X + first, count)],
            )
    for copy in own:
        copy.wait()
    links.finish()


def store_kernel(*refs):
    sems = refs[-1]
    copies = [pltpu.make_async_copy(refs[i], refs[4 + i], sems.at[i]) for i in range(4)]
    for copy in copies:
        copy.start()
    for copy in copies:
        copy.wait()


ANY = pl.BlockSpec(memory_space=pl.ANY)
HBM = pl.BlockSpec(memory_space=pltpu.HBM)
VMEM = pl.BlockSpec(memory_space=pltpu.VMEM)
SMEM = pl.BlockSpec(memory_space=pltpu.SMEM)
ALL_FRAMES = SIDE * SIDE * CORES


def body(queries, keys_in, values_in, grad_out, assign, pattern, live_blocks):
    keys_in, values_in, queries, grad_out, assign_rows = (
        pltpu.with_memory_space_constraint(one, pltpu.HBM)
        for one in (keys_in, values_in, queries, grad_out, assign.reshape(1, TOK))
    )
    shape = jax.ShapeDtypeStruct
    dma = pltpu.SemaphoreType.DMA
    spread = (2, SIDE, CORES, SIDE, SLOTS, HD)
    every_key, every_value, query_units, upstream_units = pl.pallas_call(
        gather_kernel,
        out_shape=(
            shape(spread, BF),
            shape(spread, BF),
            shape((UNITS, TOK, HD), BF),
            shape((UNITS, TOK, HD), BF),
        ),
        in_specs=[HBM, HBM, HBM, HBM, HBM],
        out_specs=(VMEM, VMEM, VMEM, VMEM),
        scratch_shapes=[
            pltpu.VMEM((2, TOK, WIDTH), BF),
            pltpu.VMEM((2, HEADS_X, SLOTS, HD), BF),
            pltpu.VMEM((1, TOK), jnp.int32),
            dma((GATHER_SEMS,)),
            dma((GATHER_SEMS,)),
            dma((GATHER_LOCAL,)),
        ],
        compiler_params=pltpu.CompilerParams(
            collective_id=0, has_side_effects=True, vmem_limit_bytes=VMEM_LIMIT
        ),
        name="gather",
    )(keys_in, values_in, queries, grad_out, assign_rows)

    blocks = (2, ALL_FRAMES * SLOTS // KB, KB, HD)

    att_units, dq_units, key_part, value_part = pl.pallas_call(
        attention_kernel,
        out_shape=(
            shape((UNITS, TOK, HD), BF),
            shape((UNITS, TOK, HD), BF),
            shape(blocks, BF),
            shape(blocks, BF),
        ),
        in_specs=[SMEM, SMEM, VMEM, VMEM, VMEM, VMEM],
        out_specs=(VMEM, VMEM, VMEM, VMEM),
        scratch_shapes=[
            pltpu.VMEM((NSEL * KB, HD), BF),
            pltpu.VMEM((NSEL * KB, HD), BF),
            pltpu.VMEM((NSEL * KB, TOK), F32),
            pltpu.VMEM((NSEL * KB, TOK), F32),
            pltpu.VMEM((NSEL * KB, HD), BF),
            pltpu.VMEM((NSEL * KB, HD), BF),
        ],
        compiler_params=pltpu.CompilerParams(vmem_limit_bytes=VMEM_LIMIT),
        name="attention",
    )(
        pattern.T, live_blocks, every_key.reshape(blocks), every_value.reshape(blocks),
        query_units, upstream_units,
    )

    results = pl.pallas_call(
        scatter_kernel,
        out_shape=(
            shape(queries.shape, BF),
            shape(queries.shape, BF),
            shape(keys_in.shape, BF),
            shape(keys_in.shape, BF),
        ),
        in_specs=[VMEM, VMEM, VMEM, VMEM, HBM],
        out_specs=(ANY, ANY, ANY, ANY),
        scratch_shapes=[
            pltpu.VMEM((2, 2, SIDE, SIDE, SLOTS, HD), BF),
            pltpu.VMEM((2, 2, 2, SIDE // 2, SLOTS, HD), BF),
            pltpu.VMEM((2, 2, 3, SIDE, SLOTS, HD), BF),
            pltpu.VMEM((2, 2, 3, SIDE, SLOTS, HD), BF),
            pltpu.VMEM((2, 2, SIDE, SLOTS, HD), BF),
            pltpu.VMEM((2, 2, SIDE, SLOTS, HD), BF),
            pltpu.VMEM((2, TOK, WIDTH), BF),
            pltpu.VMEM((1, TOK), jnp.int32),
            dma((SCATTER_SEMS,)),
            dma((SCATTER_SEMS,)),
            dma((SCATTER_LOCAL,)),
        ],
        compiler_params=pltpu.CompilerParams(
            collective_id=1, has_side_effects=True, vmem_limit_bytes=VMEM_LIMIT
        ),
        name="scatter",
    )(key_part.reshape(spread), value_part.reshape(spread), att_units, dq_units, assign_rows)
    return pl.pallas_call(
        store_kernel,
        out_shape=tuple(shape(one.shape, BF) for one in results),
        in_specs=[VMEM] * 4,
        out_specs=(HBM,) * 4,
        scratch_shapes=[dma((4,))],
        compiler_params=pltpu.CompilerParams(vmem_limit_bytes=VMEM_LIMIT),
        name="store",
    )(*results)


def solution(mesh):
    return jax.shard_map(
        body,
        mesh=mesh,
        in_specs=(
            P("frame", "head"),
            P(("frame", "head"), None),
            P(("frame", "head"), None),
            P("frame", "head"),
            P("frame"),
            P(),
            P(),
        ),
        out_specs=(
            P("frame", "head"),
            P("frame", "head"),
            P(("frame", "head"), None),
            P(("frame", "head"), None),
        ),
        check_vma=False,
    )
```

```python
import functools
import math

import jax
import jax.numpy as jnp
from jax import lax
from jax.experimental import pallas as pl
from jax.experimental.pallas import tpu as pltpu
from jax.sharding import PartitionSpec as P

HD = 128
KB = 64
NSEL = 16
SIZES = (256, 512, 768, 1024)
SIDE = 4
CORES = 2
HEADS_X = 6
WIDTH = HEADS_X * HD
TOK = 512
TOK_DEV = TOK // SIDE
SLOTS = 128
UNITS = 6
CHUNK = 512
SCALE = 1.0 / math.sqrt(HD)
MESH = pl.DeviceIdType.MESH
BF = jnp.bfloat16
F32 = jnp.float32
VMEM_LIMIT = 20 * 1024 * 1024
LOG2_E = math.log2(math.e)
STEPS = (1, -1, 2)
GROUPS = ((0, SIDE), (SIDE, HEADS_X - SIDE))
GATHER_PARTS = ((0, 1), (1, 1), (0, 0), (1, 0))
SCATTER_PARTS = ((1, 0), (0, 0), (1, 1), (0, 1))
GATHER_STRAIGHT = GATHER_PARTS[3:]
SCATTER_STRAIGHT = SCATTER_PARTS[:1]


class Place:
    def __init__(self):
        frame = lax.axis_index("frame")
        self.x = lax.axis_index("head")
        self.core = frame % CORES
        self.z = (frame // CORES) % SIDE
        self.y = frame // (CORES * SIDE)

    def device(self, y, z, core, x):
        return {"frame": (y * SIDE + z) * CORES + core, "head": x}

    def ring(self, axis, step):
        at = {"x": self.x, "y": self.y, "z": self.z}
        at[axis] = (at[axis] + step + SIDE) % SIDE
        return self.device(at["y"], at["z"], self.core, at["x"])

    def sibling(self):
        return self.device(self.y, self.z, 1 - self.core, self.x)

    def partner_z(self):
        return jnp.where(self.core == 0, self.z + 1 - 2 * (self.z % 2), SIDE - 1 - self.z)

    def partner(self):
        return self.device(self.y, self.partner_z(), self.core, self.x)


def shift(at, step):
    return (at + step + SIDE) % SIDE


def meet(place):
    partners = [place.sibling()]
    partners += [place.ring(axis, step) for axis in ("x", "y", "z") for step in STEPS]
    barrier = pltpu.get_barrier_semaphore()
    for target in partners:
        pl.semaphore_signal(barrier, inc=1, device_id=target, device_id_type=MESH)
    pl.semaphore_wait(barrier, len(partners))


class Links:
    def __init__(self, place, send, recv, local):
        self.send, self.recv, self.local = send, recv, local
        self.anyone = place.sibling()
        self.started = []
        self.names = {}
        self.local_names = {}

    def sem(self, name):
        return self.names.setdefault(name, len(self.names))

    def remote(self, name, src, dst, target):
        sem = self.sem(name)
        return pltpu.make_async_remote_copy(
            src_ref=src,
            dst_ref=dst,
            send_sem=self.send.at[sem],
            recv_sem=self.recv.at[sem],
            device_id=target,
            device_id_type=MESH,
        )

    def go(self, name, src, dst, target):
        copy = self.remote(name, src, dst, target)
        copy.start()
        self.started.append(copy)

    def got(self, name, region):
        self.remote(name, region, region, self.anyone).wait_recv()

    def here(self, name, src, dst):
        sem = self.local_names.setdefault(name, len(self.local_names))
        copy = pltpu.make_async_copy(src, dst, self.local.at[sem])
        copy.start()
        return copy

    def finish(self):
        for copy in self.started:
            copy.wait_send()


def low(ref):
    return ref.at[pl.ds(0, SIDE // 2)]


def high(ref):
    return ref.at[pl.ds(SIDE // 2, SIDE // 2)]


def cols(head, count=1):
    return pl.ds(pl.multiple_of(head * HD, HD), count * HD)


def token_rows(x):
    return pl.ds(pl.multiple_of(x * TOK_DEV, TOK_DEV), TOK_DEV)


def slot_hot_of(assign):
    slots = lax.broadcasted_iota(jnp.int32, (SLOTS, TOK), 0)
    return (slots == assign[0:1, :]).astype(F32)


MERGE, ROW, NEAR, FAR, CLOSE = range(5)
GATHER_ORDER = (
    (0, MERGE), (1, MERGE), (0, ROW), (1, ROW), (2, MERGE), (0, NEAR), (1, NEAR), (2, ROW), (0, FAR),
    (3, MERGE), (1, FAR), (3, ROW), (2, NEAR), (2, FAR), (3, NEAR), (3, FAR),
    (0, CLOSE), (1, CLOSE), (2, CLOSE), (3, CLOSE),
)
START, RELAY, TOTAL, EXPAND = range(4)
SCATTER_ORDER = (
    (0, START), (1, START), (2, START), (3, START), (0, RELAY), (1, RELAY), (2, RELAY), (3, RELAY),
    (0, TOTAL), (0, EXPAND), (1, TOTAL), (1, EXPAND), (2, TOTAL), (2, EXPAND), (3, TOTAL), (3, EXPAND),
)


GATHER_SEMS = len(GATHER_PARTS) * 14 + 2 * 4
GATHER_LOCAL = len(GATHER_PARTS) + 5


def gather_kernel(
    keys, values, queries, upstream, assign,
    every_key, every_value, query_out, upstream_out,
    tokens, merged, assign_own, send, recv, local,
):
    place = Place()
    meet(place)
    links = Links(place, send, recv, local)
    sources = (keys, values)
    every = (every_key, every_value)
    own = {}

    def send_tokens(kv, slot):
        first, count = GROUPS[slot]
        for step in STEPS:
            links.go(
                ("x", kv, slot, step),
                sources[kv].at[:, cols(shift(place.x, step) * HEADS_X + first, count)],
                tokens.at[kv, token_rows(place.x), cols(first, count)],
                place.ring("x", step),
            )
        own[kv, slot] = links.here(
            ("x", kv, slot),
            sources[kv].at[:, cols(place.x * HEADS_X + first, count)],
            tokens.at[kv, token_rows(place.x), cols(first, count)],
        )

    def send_queries(which):
        src, dst = ((queries, query_out), (upstream, upstream_out))[which]
        for step in STEPS:
            links.go(
                ("q", which, step), src.at[:, cols(shift(place.z, step))], dst.at[place.z],
                place.ring("z", step),
            )
        mine = place.z % 2
        links.go(
            ("q", which, "partner"), src.at[:, cols(SIDE + 1 - mine)], dst.at[SIDE + 1],
            place.partner(),
        )
        own["q", which, 0] = links.here(("q", which, 0), src.at[:, cols(place.z)], dst.at[place.z])
        own["q", which, 1] = links.here(
            ("q", which, 1), src.at[:, cols(SIDE + mine)], dst.at[SIDE]
        )

    send_tokens(*GATHER_PARTS[0])
    send_tokens(*GATHER_PARTS[1])
    send_queries(0)
    send_tokens(*GATHER_PARTS[2])
    send_tokens(*GATHER_PARTS[3])
    links.here("assign", assign, assign_own).wait()
    hot = slot_hot_of(assign_own)
    divisor = jnp.maximum(jnp.sum(hot, axis=1, keepdims=True), 1.0)
    hot = hot.astype(BF)

    def stage(kv, slot):
        first, count = GROUPS[slot]
        out = every[kv]
        straight = (kv, slot) in GATHER_STRAIGHT

        def region(step):
            return out.at[slot, shift(place.y, step), place.core]

        def pass_on(step):
            links.go(("s", kv, slot, step), region(step), region(step), place.sibling())

        def merge():
            own[kv, slot].wait()
            for step in STEPS:
                links.got(
                    ("x", kv, slot, step),
                    tokens.at[kv, token_rows(shift(place.x, -step)), cols(first, count)],
                )
            sums = jnp.dot(
                hot, tokens[kv, :, first * HD : (first + count) * HD], preferred_element_type=F32
            )
            mean = (sums / divisor).astype(BF)
            for i in range(count):
                merged[kv, first + i] = mean[:, i * HD : (i + 1) * HD]

            def head_of(z):
                return z if slot == 0 else SIDE + z % 2

            for step in STEPS:
                links.go(
                    ("z", kv, slot, step),
                    merged.at[kv, head_of(shift(place.z, step))],
                    out.at[slot, place.y, place.core, place.z],
                    place.ring("z", step),
                )
            out[slot, place.y, place.core, place.z] = merged[kv, head_of(place.z)]
            if (kv, slot) == GATHER_PARTS[3]:
                send_queries(1)

        def row():
            for step in STEPS:
                links.got(
                    ("z", kv, slot, step),
                    out.at[slot, place.y, place.core, shift(place.z, -step)],
                )
            for step in STEPS if straight else STEPS[:2]:
                links.go(("y", kv, slot, step), region(0), region(0), place.ring("y", step))
            pass_on(0)

        def near():
            links.got(("y", kv, slot, 1), region(-1))
            if not straight:
                links.go(("f", kv, slot, 1), low(region(-1)), low(region(-1)), place.ring("y", 1))
            pass_on(-1)
            links.got(("y", kv, slot, -1), region(1))
            if not straight:
                links.go(("f", kv, slot, -1), high(region(1)), high(region(1)), place.ring("y", -1))
            pass_on(1)

        def far():
            if straight:
                links.got(("y", kv, slot, 2), region(2))
            else:
                links.got(("f", kv, slot, 1), low(region(2)))
                links.got(("f", kv, slot, -1), high(region(2)))
            pass_on(2)

        def close():
            for step in (0, -1, 1, 2):
                links.got(
                    ("s", kv, slot, step), out.at[slot, shift(place.y, step), 1 - place.core]
                )

        return [merge, row, near, far, close]

    stages = [stage(kv, slot) for kv, slot in GATHER_PARTS]
    for part, step in GATHER_ORDER:
        stages[part][step]()
    for which, dst in enumerate((query_out, upstream_out)):
        for step in STEPS:
            links.got(("q", which, step), dst.at[shift(place.z, -step)])
        links.got(("q", which, "partner"), dst.at[SIDE + 1])
        own["q", which, 0].wait()
        own["q", which, 1].wait()
    links.finish()


def attention_kernel(
    pattern, live, keys, values, query, upstream,
    attended, query_grad, key_grad, value_grad,
    ksel, vsel, expo, prob_grad, kpart, vpart,
):
    place = Place()
    key_grad[...] = jnp.zeros_like(key_grad)
    value_grad[...] = jnp.zeros_like(value_grad)

    def spot_of(block):
        owner = block // 2
        y, z, core = owner // (CORES * SIDE), (owner // CORES) % SIDE, owner % CORES
        return ((y * CORES + core) * SIDE + z) * 2 + block % 2

    def unit_step(unit, carry):
        slot = unit // SIDE
        unit_z = jnp.where(unit < SIDE, unit, jnp.where(unit == SIDE, place.z, place.partner_z()))
        frame = (place.y * SIDE + unit_z) * CORES + place.core
        count = live[frame]
        rows_live = count * KB

        def attend(least, rows):
            for j in range(rows // KB):
                spot = spot_of(pattern[j, frame])
                ksel[j * KB : (j + 1) * KB, :] = keys[slot, spot]
                vsel[j * KB : (j + 1) * KB, :] = values[slot, spot]
            q, g = query[unit], upstream[unit]
            q_t, g_t = q.T, g.T
            spans = [(a, min(a + CHUNK, rows)) for a in range(0, rows, CHUNK)]
            top = jnp.full((1, TOK), -jnp.inf, F32)
            for a, b in spans:
                scores = jnp.dot(ksel[a:b, :], q_t, preferred_element_type=F32)
                if b > least:
                    ids = lax.broadcasted_iota(jnp.int32, (b - a, TOK), 0) + a
                    scores = jnp.where(ids < rows_live, scores, -jnp.inf)
                expo[a:b, :] = scores
                top = jnp.maximum(top, jnp.max(scores, axis=0, keepdims=True))
                prob_grad[a:b, :] = jnp.dot(vsel[a:b, :], g_t, preferred_element_type=F32)
            top = top * (SCALE * LOG2_E)
            total = jnp.zeros((1, TOK), F32)
            weighted = jnp.zeros((HD, TOK), F32)
            for a, b in spans:
                weights = jnp.exp2(expo[a:b, :] * (SCALE * LOG2_E) - top)
                expo[a:b, :] = weights
                total = total + jnp.sum(weights, axis=0, keepdims=True)
                weighted = weighted + lax.dot_general(
                    vsel[a:b, :], weights.astype(BF), (((0,), (0,)), ((), ())),
                    preferred_element_type=F32,
                )
            inverse = 1.0 / total
            att_t = (weighted * inverse).astype(BF)
            attended[unit] = att_t.T
            delta = jnp.sum(g_t.astype(F32) * att_t.astype(F32), axis=0, keepdims=True)
            dq = jnp.zeros((HD, TOK), F32)
            for a, b in spans:
                probs = expo[a:b, :] * inverse
                score_grad = (probs * (prob_grad[a:b, :] - delta)).astype(BF)
                kpart[a:b, :] = (
                    jnp.dot(score_grad, q, preferred_element_type=F32) * SCALE
                ).astype(BF)
                vpart[a:b, :] = jnp.dot(
                    probs.astype(BF), g, preferred_element_type=F32
                ).astype(BF)
                dq = dq + lax.dot_general(
                    ksel[a:b, :], score_grad, (((0,), (0,)), ((), ())), preferred_element_type=F32
                )
            query_grad[unit] = (dq * SCALE).astype(BF).T
            for j in range(rows // KB):

                def add(j=j):
                    spot = spot_of(pattern[j, frame])
                    for out, part in ((key_grad, kpart), (value_grad, vpart)):
                        piece = part[j * KB : (j + 1) * KB, :].astype(F32)
                        out[slot, spot] = (out[slot, spot].astype(F32) + piece).astype(BF)

                if j * KB < least:
                    add()
                else:
                    pl.when(j < count)(add)

        least = 0
        for rows in SIZES:
            pl.when((rows_live > least) & (rows_live <= rows))(
                functools.partial(attend, least, rows)
            )
            least = rows
        return carry

    lax.fori_loop(0, UNITS, unit_step, 0)


SCATTER_SEMS = len(SCATTER_PARTS) * 14 + 2 * 4
SCATTER_LOCAL = len(SCATTER_PARTS) + 5


def scatter_kernel(
    key_part, value_part, att_in, dq_in, assign,
    attended, query_grad, grad_keys, grad_values,
    twin, halves, fulls, outgoing, column, pieces, tokens, assign_own, send, recv, local,
):
    place = Place()
    meet(place)
    links = Links(place, send, recv, local)
    parts = (key_part, value_part)
    outs = (grad_keys, grad_values)
    own = []

    def send_twin(kv, slot):
        for step in (2, 1, -1, 0):
            y = shift(place.y, step)
            links.go(
                ("s", kv, slot, step), parts[kv].at[slot, y, 1 - place.core],
                twin.at[kv, slot, y], place.sibling(),
            )

    for kv, slot in SCATTER_PARTS:
        send_twin(kv, slot)
    mine = place.z % 2
    for which, (src, dst) in enumerate(((att_in, attended), (dq_in, query_grad))):
        for step in STEPS:
            links.go(
                ("q", which, step), src.at[shift(place.z, step)], dst.at[:, cols(place.z)],
                place.ring("z", step),
            )
        links.go(
            ("q", which, "partner"), src.at[SIDE + 1], dst.at[:, cols(SIDE + mine)],
            place.partner(),
        )
        own.append(links.here(("q", which, 0), src.at[place.z], dst.at[:, cols(place.z)]))
        own.append(links.here(("q", which, 1), src.at[SIDE], dst.at[:, cols(SIDE + mine)]))
    links.here("assign", assign, assign_own).wait()
    hot = slot_hot_of(assign_own)
    divisor = jnp.maximum(jnp.sum(hot, axis=1, keepdims=True), 1.0)
    hot = hot.astype(BF)

    def stage(kv, slot):
        first, count = GROUPS[slot]
        straight = (kv, slot) in SCATTER_STRAIGHT
        half_in, full_in, out = halves.at[kv, slot], fulls.at[kv, slot], outgoing.at[kv, slot]

        def term(step):
            y = shift(place.y, step)
            links.got(("s", kv, slot, step), twin.at[kv, slot, y])
            return parts[kv][slot, y, place.core].astype(F32) + twin[kv, slot, y].astype(F32)

        def start():
            out[2] = term(2).astype(BF)
            if straight:
                links.go(("y", kv, slot, 2), out.at[2], full_in.at[2], place.ring("y", 2))
                return
            links.go(("h", kv, slot, 1), low(out.at[2]), half_in.at[0], place.ring("y", 1))
            links.go(("h", kv, slot, -1), high(out.at[2]), half_in.at[1], place.ring("y", -1))

        def relay():
            ahead = term(1)
            behind = term(-1)
            half = SIDE // 2
            if straight:
                for at, step, value in ((0, 1, ahead), (1, -1, behind)):
                    out[at] = value.astype(BF)
                    links.go(
                        ("y", kv, slot, step), out.at[at], full_in.at[at], place.ring("y", step)
                    )
                return
            links.got(("h", kv, slot, 1), half_in.at[0])
            out[0, 0:half] = (ahead[0:half] + half_in[0].astype(F32)).astype(BF)
            out[0, half:SIDE] = ahead[half:SIDE].astype(BF)
            links.go(("y", kv, slot, 1), out.at[0], full_in.at[0], place.ring("y", 1))
            links.got(("h", kv, slot, -1), half_in.at[1])
            out[1, 0:half] = behind[0:half].astype(BF)
            out[1, half:SIDE] = (behind[half:SIDE] + half_in[1].astype(F32)).astype(BF)
            links.go(("y", kv, slot, -1), out.at[1], full_in.at[1], place.ring("y", -1))

        def row():
            total = term(0)
            links.got(("y", kv, slot, 1), full_in.at[0])
            links.got(("y", kv, slot, -1), full_in.at[1])
            total = total + full_in[0].astype(F32) + full_in[1].astype(F32)
            if straight:
                links.got(("y", kv, slot, 2), full_in.at[2])
                total = total + full_in[2].astype(F32)
            column[kv, slot] = total.astype(BF)
            for step in STEPS:
                links.go(
                    ("z", kv, slot, step), column.at[kv, slot, shift(place.z, step)],
                    pieces.at[kv, slot, place.z], place.ring("z", step),
                )
            pieces[kv, slot, place.z] = column[kv, slot, place.z]

        def expand():
            for step in STEPS:
                links.got(("z", kv, slot, step), pieces.at[kv, slot, shift(place.z, -step)])
            ready = [pieces[kv, slot, z].astype(F32) for z in range(SIDE)]
            if slot == 1:
                ready = [ready[0] + ready[2], ready[1] + ready[3]]
            mean = jnp.concatenate([(one / divisor).astype(BF) for one in ready], axis=1)
            tokens[kv, :, first * HD : (first + count) * HD] = lax.dot_general(
                hot, mean, (((0,), (0,)), ((), ())), preferred_element_type=F32
            ).astype(BF)
            to = cols(place.x * HEADS_X + first, count)
            for step in STEPS:
                links.go(
                    ("x", kv, slot, step),
                    tokens.at[kv, token_rows(shift(place.x, step)), cols(first, count)],
                    outs[kv].at[:, to],
                    place.ring("x", step),
                )
            own.append(
                links.here(
                    ("x", kv, slot),
                    tokens.at[kv, token_rows(place.x), cols(first, count)],
                    outs[kv].at[:, to],
                )
            )

        return [start, relay, row, expand]

    stages = [stage(kv, slot) for kv, slot in SCATTER_PARTS]
    for part, step in SCATTER_ORDER:
        stages[part][step]()

    for which, dst in enumerate((attended, query_grad)):
        for step in STEPS:
            links.got(("q", which, step), dst.at[:, cols(shift(place.z, -step))])
        links.got(("q", which, "partner"), dst.at[:, cols(SIDE + 1 - mine)])
    for kv, slot in SCATTER_PARTS:
        first, count = GROUPS[slot]
        for step in STEPS:
            links.got(
                ("x", kv, slot, step),
                outs[kv].at[:, cols(shift(place.x, -step) * HEADS_X + first, count)],
            )
    for copy in own:
        copy.wait()
    links.finish()


def store_kernel(*refs):
    sems = refs[-1]
    copies = [pltpu.make_async_copy(refs[i], refs[4 + i], sems.at[i]) for i in range(4)]
    for copy in copies:
        copy.start()
    for copy in copies:
        copy.wait()


ANY = pl.BlockSpec(memory_space=pl.ANY)
HBM = pl.BlockSpec(memory_space=pltpu.HBM)
VMEM = pl.BlockSpec(memory_space=pltpu.VMEM)
SMEM = pl.BlockSpec(memory_space=pltpu.SMEM)
ALL_FRAMES = SIDE * SIDE * CORES


def body(queries, keys_in, values_in, grad_out, assign, pattern, live_blocks):
    keys_in, values_in, queries, grad_out, assign_rows = (
        pltpu.with_memory_space_constraint(one, pltpu.HBM)
        for one in (keys_in, values_in, queries, grad_out, assign.reshape(1, TOK))
    )
    shape = jax.ShapeDtypeStruct
    dma = pltpu.SemaphoreType.DMA
    spread = (2, SIDE, CORES, SIDE, SLOTS, HD)
    every_key, every_value, query_units, upstream_units = pl.pallas_call(
        gather_kernel,
        out_shape=(
            shape(spread, BF),
            shape(spread, BF),
            shape((UNITS, TOK, HD), BF),
            shape((UNITS, TOK, HD), BF),
        ),
        in_specs=[HBM, HBM, HBM, HBM, HBM],
        out_specs=(VMEM, VMEM, VMEM, VMEM),
        scratch_shapes=[
            pltpu.VMEM((2, TOK, WIDTH), BF),
            pltpu.VMEM((2, HEADS_X, SLOTS, HD), BF),
            pltpu.VMEM((1, TOK), jnp.int32),
            dma((GATHER_SEMS,)),
            dma((GATHER_SEMS,)),
            dma((GATHER_LOCAL,)),
        ],
        compiler_params=pltpu.CompilerParams(
            collective_id=0, has_side_effects=True, vmem_limit_bytes=VMEM_LIMIT
        ),
        name="gather",
    )(keys_in, values_in, queries, grad_out, assign_rows)

    blocks = (2, ALL_FRAMES * SLOTS // KB, KB, HD)

    att_units, dq_units, key_part, value_part = pl.pallas_call(
        attention_kernel,
        out_shape=(
            shape((UNITS, TOK, HD), BF),
            shape((UNITS, TOK, HD), BF),
            shape(blocks, BF),
            shape(blocks, BF),
        ),
        in_specs=[SMEM, SMEM, VMEM, VMEM, VMEM, VMEM],
        out_specs=(VMEM, VMEM, VMEM, VMEM),
        scratch_shapes=[
            pltpu.VMEM((NSEL * KB, HD), BF),
            pltpu.VMEM((NSEL * KB, HD), BF),
            pltpu.VMEM((NSEL * KB, TOK), F32),
            pltpu.VMEM((NSEL * KB, TOK), F32),
            pltpu.VMEM((NSEL * KB, HD), BF),
            pltpu.VMEM((NSEL * KB, HD), BF),
        ],
        compiler_params=pltpu.CompilerParams(vmem_limit_bytes=VMEM_LIMIT),
        name="attention",
    )(
        pattern.T, live_blocks, every_key.reshape(blocks), every_value.reshape(blocks),
        query_units, upstream_units,
    )

    results = pl.pallas_call(
        scatter_kernel,
        out_shape=(
            shape(queries.shape, BF),
            shape(queries.shape, BF),
            shape(keys_in.shape, BF),
            shape(keys_in.shape, BF),
        ),
        in_specs=[VMEM, VMEM, VMEM, VMEM, HBM],
        out_specs=(ANY, ANY, ANY, ANY),
        scratch_shapes=[
            pltpu.VMEM((2, 2, SIDE, SIDE, SLOTS, HD), BF),
            pltpu.VMEM((2, 2, 2, SIDE // 2, SLOTS, HD), BF),
            pltpu.VMEM((2, 2, 3, SIDE, SLOTS, HD), BF),
            pltpu.VMEM((2, 2, 3, SIDE, SLOTS, HD), BF),
            pltpu.VMEM((2, 2, SIDE, SLOTS, HD), BF),
            pltpu.VMEM((2, 2, SIDE, SLOTS, HD), BF),
            pltpu.VMEM((2, TOK, WIDTH), BF),
            pltpu.VMEM((1, TOK), jnp.int32),
            dma((SCATTER_SEMS,)),
            dma((SCATTER_SEMS,)),
            dma((SCATTER_LOCAL,)),
        ],
        compiler_params=pltpu.CompilerParams(
            collective_id=1, has_side_effects=True, vmem_limit_bytes=VMEM_LIMIT
        ),
        name="scatter",
    )(key_part.reshape(spread), value_part.reshape(spread), att_units, dq_units, assign_rows)
    return pl.pallas_call(
        store_kernel,
        out_shape=tuple(shape(one.shape, BF) for one in results),
        in_specs=[VMEM] * 4,
        out_specs=(HBM,) * 4,
        scratch_shapes=[dma((4,))],
        compiler_params=pltpu.CompilerParams(vmem_limit_bytes=VMEM_LIMIT),
        name="store",
    )(*results)


def solution(mesh):
    return jax.shard_map(
        body,
        mesh=mesh,
        in_specs=(
            P("frame", "head"),
            P(("frame", "head"), None),
            P(("frame", "head"), None),
            P("frame", "head"),
            P("frame"),
            P(),
            P(),
        ),
        out_specs=(
            P("frame", "head"),
            P("frame", "head"),
            P(("frame", "head"), None),
            P(("frame", "head"), None),
        ),
        check_vma=False,
    )
```

```python
import math

import jax
import jax.numpy as jnp
from jax import lax
from jax.experimental import pallas as pl
from jax.experimental.pallas import tpu as pltpu
from jax.sharding import PartitionSpec as P

HD = 128
KB = 64
NSEL = 16
SIDE = 4
CORES = 2
HEADS_X = 6
WIDTH = HEADS_X * HD
TOK = 512
TOK_DEV = TOK // SIDE
SLOTS = 128
SLOT_UNITS = (4, 2)
CHUNK = 512
SCALE = 1.0 / math.sqrt(HD)
MESH = pl.DeviceIdType.MESH
BF = jnp.bfloat16
F32 = jnp.float32
VMEM_LIMIT = 44 * 1024 * 1024
STORE_LIMIT = 8 * 1024 * 1024
GROUP = SIDE * SLOTS // KB
LOG2_E = math.log2(math.e)
STEPS = (1, -1, 2)
GROUPS = ((0, SIDE), (SIDE, HEADS_X - SIDE))
GATHER_PARTS = ((0, 1), (1, 1), (0, 0), (1, 0))
GATHER_STRAIGHT = GATHER_PARTS[3:]
SCATTER_STRAIGHT = ((1, 0),)


class Place:
    def __init__(self):
        frame = lax.axis_index("frame")
        self.x = lax.axis_index("head")
        self.core = frame % CORES
        self.z = (frame // CORES) % SIDE
        self.y = frame // (CORES * SIDE)

    def device(self, y, z, core, x):
        return {"frame": (y * SIDE + z) * CORES + core, "head": x}

    def ring(self, axis, step):
        at = {"x": self.x, "y": self.y, "z": self.z}
        at[axis] = (at[axis] + step + SIDE) % SIDE
        return self.device(at["y"], at["z"], self.core, at["x"])

    def sibling(self):
        return self.device(self.y, self.z, 1 - self.core, self.x)

    def partner_z(self):
        return jnp.where(self.core == 0, self.z + 1 - 2 * (self.z % 2), SIDE - 1 - self.z)

    def partner(self):
        return self.device(self.y, self.partner_z(), self.core, self.x)


def shift(at, step):
    return (at + step + SIDE) % SIDE


def meet(place):
    partners = [place.sibling()]
    partners += [place.ring(axis, step) for axis in ("x", "y", "z") for step in STEPS]
    barrier = pltpu.get_barrier_semaphore()
    for target in partners:
        pl.semaphore_signal(barrier, inc=1, device_id=target, device_id_type=MESH)
    pl.semaphore_wait(barrier, len(partners))


class Links:
    def __init__(self, place, send, recv, local):
        self.send, self.recv, self.local = send, recv, local
        self.anyone = place.sibling()
        self.started = []
        self.names = {}
        self.local_names = {}

    def sem(self, name):
        return self.names.setdefault(name, len(self.names))

    def remote(self, name, src, dst, target):
        sem = self.sem(name)
        return pltpu.make_async_remote_copy(
            src_ref=src,
            dst_ref=dst,
            send_sem=self.send.at[sem],
            recv_sem=self.recv.at[sem],
            device_id=target,
            device_id_type=MESH,
        )

    def go(self, name, src, dst, target):
        copy = self.remote(name, src, dst, target)
        copy.start()
        self.started.append(copy)

    def got(self, name, region):
        self.remote(name, region, region, self.anyone).wait_recv()

    def here(self, name, src, dst):
        sem = self.local_names.setdefault(name, len(self.local_names))
        copy = pltpu.make_async_copy(src, dst, self.local.at[sem])
        copy.start()
        return copy

    def finish(self):
        for copy in self.started:
            copy.wait_send()


def low(ref):
    return ref.at[pl.ds(0, GROUP // 2)]


def high(ref):
    return ref.at[pl.ds(GROUP // 2, GROUP // 2)]


def spot_of(block):
    owner = block // 2
    y, z, core = owner // (CORES * SIDE), (owner // CORES) % SIDE, owner % CORES
    return ((y * CORES + core) * SIDE + z) * 2 + block % 2


def cols(head, count=1):
    return pl.ds(pl.multiple_of(head * HD, HD), count * HD)


def token_rows(x):
    return pl.ds(pl.multiple_of(x * TOK_DEV, TOK_DEV), TOK_DEV)


def slot_hot_of(assign):
    slots = lax.broadcasted_iota(jnp.int32, (SLOTS, TOK), 0)
    return (slots == assign[0:1, :]).astype(F32)


SEMS = 4 * 14 + 2 * 4 + 4 * 14 + 2 * 4
LOCAL = 4 + 4 + 1 + 4 + 4
ALL_FRAMES = SIDE * SIDE * CORES
ALL_SPOTS = ALL_FRAMES * SLOTS // KB
DEAD = NSEL
ENTRIES = NSEL + 1


def layer_kernel(
    keys, values, queries, upstream, assign, spots, entries, biases,
    attended, query_grad, grad_keys, grad_values,
    keys0, keys1, values0, values1, tokens, merged, assign_own, query_in, upstream_in,
    ksel, vsel, expo, prob_grad, key_part0, key_part1, value_part0, value_part1, att_out, dq_out, dense,
    twin, halves, fulls, outgoing, column, pieces, token_out, send, recv, local,
):
    place = Place()
    meet(place)
    links = Links(place, send, recv, local)
    sources = (keys, values)
    every = ((keys0, keys1), (values0, values1))
    parts = ((key_part0, key_part1), (value_part0, value_part1))
    outs = (grad_keys, grad_values)
    own = {}
    mine = place.z % 2

    def send_tokens(kv, slot):
        first, count = GROUPS[slot]
        for step in STEPS:
            links.go(
                ("x", kv, slot, step),
                sources[kv].at[:, cols(shift(place.x, step) * HEADS_X + first, count)],
                tokens.at[kv, token_rows(place.x), cols(first, count)],
                place.ring("x", step),
            )
        own[kv, slot] = links.here(
            ("x", kv, slot),
            sources[kv].at[:, cols(place.x * HEADS_X + first, count)],
            tokens.at[kv, token_rows(place.x), cols(first, count)],
        )

    moved = ((queries, query_in), (upstream, upstream_in))

    def send_rows(which):
        src, dst = moved[which]
        for step in STEPS:
            links.go(
                ("q", which, step), src.at[:, cols(shift(place.z, step))], dst.at[place.z],
                place.ring("z", step),
            )
        own["q", which, 0] = links.here(("q", which, 0), src.at[:, cols(place.z)], dst.at[place.z])

    def send_pair(which):
        src, dst = moved[which]
        links.go(
            ("q", which, "partner"), src.at[:, cols(SIDE + 1 - mine)], dst.at[SIDE + 1],
            place.partner(),
        )
        own["q", which, 1] = links.here(
            ("q", which, 1), src.at[:, cols(SIDE + mine)], dst.at[SIDE]
        )

    def rows_arrived():
        for which, (_, dst) in enumerate(moved):
            for step in STEPS:
                links.got(("q", which, step), dst.at[shift(place.z, -step)])
            own["q", which, 0].wait()

    def pair_arrived():
        for which, (_, dst) in enumerate(moved):
            links.got(("q", which, "partner"), dst.at[SIDE + 1])
            own["q", which, 1].wait()

    send_tokens(*GATHER_PARTS[0])
    send_tokens(*GATHER_PARTS[1])
    send_pair(0)
    send_pair(1)
    send_rows(0)
    send_tokens(*GATHER_PARTS[2])
    send_tokens(*GATHER_PARTS[3])
    links.here("assign", assign, assign_own).wait()
    hot = slot_hot_of(assign_own)
    divisor = jnp.maximum(jnp.sum(hot, axis=1, keepdims=True), 1.0)
    hot = hot.astype(BF)
    for kv in range(2):
        for slot, count in enumerate(SLOT_UNITS):
            for at in range(count):
                parts[kv][slot][at * ENTRIES + DEAD] = jnp.zeros((KB, HD), BF)

    def group(y, core):
        return pl.ds((y * CORES + core) * GROUP, GROUP)

    def gather_stage(kv, slot):
        first, count = GROUPS[slot]
        out = every[kv][slot]
        straight = (kv, slot) in GATHER_STRAIGHT

        def region(step):
            return out.at[group(shift(place.y, step), place.core)]

        def cell(z):
            return pl.ds((place.y * CORES + place.core) * GROUP + z * 2, 2)

        def pass_on(step):
            links.go(("s", kv, slot, step), region(step), region(step), place.sibling())

        def merge():
            own[kv, slot].wait()
            for step in STEPS:
                links.got(
                    ("x", kv, slot, step),
                    tokens.at[kv, token_rows(shift(place.x, -step)), cols(first, count)],
                )
            sums = jnp.dot(
                hot, tokens[kv, :, first * HD : (first + count) * HD], preferred_element_type=F32
            )
            mean = (sums / divisor).astype(BF)
            for i in range(count):
                merged[kv, first + i] = mean[:, i * HD : (i + 1) * HD].reshape(2, KB, HD)

            def head_of(z):
                return z if slot == 0 else SIDE + z % 2

            for step in STEPS:
                links.go(
                    ("z", kv, slot, step),
                    merged.at[kv, head_of(shift(place.z, step))],
                    out.at[cell(place.z)],
                    place.ring("z", step),
                )
            out[cell(place.z)] = merged[kv, head_of(place.z)]
            if (kv, slot) == GATHER_PARTS[3]:
                send_rows(1)

        def row():
            for step in STEPS:
                links.got(("z", kv, slot, step), out.at[cell(shift(place.z, -step))])
            for step in STEPS if straight else STEPS[:2]:
                links.go(("y", kv, slot, step), region(0), region(0), place.ring("y", step))
            pass_on(0)

        def near():
            links.got(("y", kv, slot, 1), region(-1))
            if not straight:
                links.go(("f", kv, slot, 1), low(region(-1)), low(region(-1)), place.ring("y", 1))
            pass_on(-1)
            links.got(("y", kv, slot, -1), region(1))
            if not straight:
                links.go(("f", kv, slot, -1), high(region(1)), high(region(1)), place.ring("y", -1))
            pass_on(1)

        def far():
            if straight:
                links.got(("y", kv, slot, 2), region(2))
            else:
                links.got(("f", kv, slot, 1), low(region(2)))
                links.got(("f", kv, slot, -1), high(region(2)))
            pass_on(2)

        def close():
            for step in (0, -1, 1, 2):
                links.got(
                    ("s", kv, slot, step),
                    out.at[group(shift(place.y, step), 1 - place.core)],
                )

        return merge, row, near, far, close

    def attend(slot, unit):
        every_key, every_value = every[0][slot], every[1][slot]
        at = unit - slot * SIDE
        rows = NSEL * KB
        for j in range(NSEL):
            spot = spots[unit * NSEL + j]
            ksel[j * KB : (j + 1) * KB, :] = every_key[spot]
            vsel[j * KB : (j + 1) * KB, :] = every_value[spot]
        q, g = query_in[unit], upstream_in[unit]
        q_t, g_t = q.T, g.T
        spans = [(a, a + CHUNK) for a in range(0, rows, CHUNK)]
        top = jnp.full((1, TOK), -jnp.inf, F32)
        for a, b in spans:
            scores = jnp.dot(ksel[a:b, :], q_t, preferred_element_type=F32)
            for c in range(a, b, KB):
                block = scores[c - a : c - a + KB] + biases[unit * NSEL + c // KB]
                expo[c : c + KB, :] = block
                top = jnp.maximum(top, jnp.max(block, axis=0, keepdims=True))
            prob_grad[a:b, :] = jnp.dot(vsel[a:b, :], g_t, preferred_element_type=F32)
        top = top * (SCALE * LOG2_E)
        total = jnp.zeros((1, TOK), F32)
        weighted = jnp.zeros((HD, TOK), F32)
        for a, b in spans:
            weights = jnp.exp2(expo[a:b, :] * (SCALE * LOG2_E) - top)
            expo[a:b, :] = weights
            total = total + jnp.sum(weights, axis=0, keepdims=True)
            weighted = weighted + lax.dot_general(
                vsel[a:b, :], weights.astype(BF), (((0,), (0,)), ((), ())),
                preferred_element_type=F32,
            )
        inverse = 1.0 / total
        att_t = (weighted * inverse).astype(BF)
        att_out[unit] = att_t.T
        delta = jnp.sum(g_t.astype(F32) * att_t.astype(F32), axis=0, keepdims=True)
        dq = jnp.zeros((HD, TOK), F32)
        blocks = CHUNK // KB
        for a, b in spans:
            probs = expo[a:b, :] * inverse
            score_grad = (probs * (prob_grad[a:b, :] - delta)).astype(BF)
            dk = jnp.dot(score_grad, q, preferred_element_type=F32) * SCALE
            dv = jnp.dot(probs.astype(BF), g, preferred_element_type=F32)
            for kv, grads in enumerate((dk, dv)):
                into = pl.ds(at * ENTRIES + a // KB, blocks)
                parts[kv][slot][into] = grads.astype(BF).reshape(blocks, KB, HD)
            dq = dq + lax.dot_general(
                ksel[a:b, :], score_grad, (((0,), (0,)), ((), ())), preferred_element_type=F32
            )
        dq_out[unit] = (dq * SCALE).astype(BF).T

    results = ((att_out, attended), (dq_out, query_grad))

    def send_result(unit, step):
        for which, (src, dst) in enumerate(results):
            if step:
                links.go(
                    ("r", which, step), src.at[unit], dst.at[:, cols(place.z)], place.ring("z", step)
                )
            else:
                own["r", which, 0] = links.here(
                    ("r", which, 0), src.at[unit], dst.at[:, cols(place.z)]
                )

    def send_pair_result():
        for which, (src, dst) in enumerate(results):
            links.go(
                ("r", which, "partner"), src.at[SIDE + 1], dst.at[:, cols(SIDE + mine)],
                place.partner(),
            )
            own["r", which, 1] = links.here(
                ("r", which, 1), src.at[SIDE], dst.at[:, cols(SIDE + mine)]
            )

    def spread(kv, slot):
        def region(y, core):
            def one(i, carry):
                spot = (y * CORES + core) * GROUP + i
                total = jnp.zeros((KB, HD), F32)
                for at in range(SLOT_UNITS[slot]):
                    entry = entries[(slot * SIDE + at) * ALL_SPOTS + spot]
                    total = total + parts[kv][slot][entry].astype(F32)
                dense[kv, slot, spot] = total.astype(BF)
                return carry

            lax.fori_loop(0, GROUP, one, 0)

        for step in (2, 1, -1, 0):
            y = shift(place.y, step)
            region(y, 1 - place.core)
            links.go(
                ("t", kv, slot, step), dense.at[kv, slot, group(y, 1 - place.core)],
                twin.at[kv, slot, y], place.sibling(),
            )
        for step in (2, 1, -1, 0):
            region(shift(place.y, step), place.core)

    def scatter_stage(kv, slot):
        first, count = GROUPS[slot]
        straight = (kv, slot) in SCATTER_STRAIGHT
        half_in, full_in, out = halves.at[kv, slot], fulls.at[kv, slot], outgoing.at[kv, slot]

        def term(step):
            y = shift(place.y, step)
            links.got(("t", kv, slot, step), twin.at[kv, slot, y])
            here = dense[kv, slot, group(y, place.core)]
            return here.astype(F32) + twin[kv, slot, y].astype(F32)

        def start():
            out[2] = term(2).astype(BF)
            if straight:
                links.go(("w", kv, slot, 2), out.at[2], full_in.at[2], place.ring("y", 2))
                return
            links.go(("h", kv, slot, 1), low(out.at[2]), half_in.at[0], place.ring("y", 1))
            links.go(("h", kv, slot, -1), high(out.at[2]), half_in.at[1], place.ring("y", -1))

        def relay():
            ahead = term(1)
            behind = term(-1)
            half = GROUP // 2
            if straight:
                for at, step, value in ((0, 1, ahead), (1, -1, behind)):
                    out[at] = value.astype(BF)
                    links.go(
                        ("w", kv, slot, step), out.at[at], full_in.at[at], place.ring("y", step)
                    )
                return
            links.got(("h", kv, slot, 1), half_in.at[0])
            out[0, 0:half] = (ahead[0:half] + half_in[0].astype(F32)).astype(BF)
            out[0, half:GROUP] = ahead[half:GROUP].astype(BF)
            links.go(("w", kv, slot, 1), out.at[0], full_in.at[0], place.ring("y", 1))
            links.got(("h", kv, slot, -1), half_in.at[1])
            out[1, 0:half] = behind[0:half].astype(BF)
            out[1, half:GROUP] = (behind[half:GROUP] + half_in[1].astype(F32)).astype(BF)
            links.go(("w", kv, slot, -1), out.at[1], full_in.at[1], place.ring("y", -1))

        def total():
            value = term(0)
            links.got(("w", kv, slot, 1), full_in.at[0])
            links.got(("w", kv, slot, -1), full_in.at[1])
            value = value + full_in[0].astype(F32) + full_in[1].astype(F32)
            if straight:
                links.got(("w", kv, slot, 2), full_in.at[2])
                value = value + full_in[2].astype(F32)
            column[kv, slot] = value.astype(BF)
            for step in STEPS:
                links.go(
                    ("v", kv, slot, step),
                    column.at[kv, slot, pl.ds(shift(place.z, step) * 2, 2)],
                    pieces.at[kv, slot, place.z], place.ring("z", step),
                )
            pieces[kv, slot, place.z] = column[kv, slot, pl.ds(place.z * 2, 2)]

        def expand():
            for step in STEPS:
                links.got(("v", kv, slot, step), pieces.at[kv, slot, shift(place.z, -step)])
            ready = [pieces[kv, slot, z].astype(F32).reshape(SLOTS, HD) for z in range(SIDE)]
            if slot == 1:
                ready = [ready[0] + ready[2], ready[1] + ready[3]]
            mean = jnp.concatenate([(one / divisor).astype(BF) for one in ready], axis=1)
            token_out[kv, :, first * HD : (first + count) * HD] = lax.dot_general(
                hot, mean, (((0,), (0,)), ((), ())), preferred_element_type=F32
            ).astype(BF)
            to = cols(place.x * HEADS_X + first, count)
            for step in STEPS:
                links.go(
                    ("u", kv, slot, step),
                    token_out.at[kv, token_rows(shift(place.x, step)), cols(first, count)],
                    outs[kv].at[:, to],
                    place.ring("x", step),
                )
            own["u", kv, slot] = links.here(
                ("u", kv, slot),
                token_out.at[kv, token_rows(place.x), cols(first, count)],
                outs[kv].at[:, to],
            )

        return start, relay, total, expand

    (merge0, row0, near0, far0, close0), (merge1, row1, near1, far1, close1), (
        merge2, row2, near2, far2, close2,
    ), (merge3, row3, near3, far3, close3) = [gather_stage(kv, slot) for kv, slot in GATHER_PARTS]
    for step in (
        merge0, merge1, row0, row1, merge2, near0, near1, row2, far0, merge3, far1, row3, near2, far2,
        close0, close1, pair_arrived,
    ):
        step()

    def pair_step(i, carry):
        attend(1, SIDE + i)
        return carry

    lax.fori_loop(0, SLOT_UNITS[1], pair_step, 0)
    near3()
    far3()
    send_pair_result()
    spread(1, 1)
    spread(0, 1)
    close2()
    close3()
    rows_arrived()

    def ahead_step(i, carry):
        attend(0, shift(place.z, 1 + 2 * i))
        return carry

    def rest_step(i, carry):
        attend(0, shift(place.z, 2 + 2 * i))
        return carry

    value0, key0, value1, key1 = [
        scatter_stage(kv, slot) for kv, slot in ((1, 0), (0, 0), (1, 1), (0, 1))
    ]
    start, relay, total, expand = range(4)
    value1[start]()
    key1[start]()
    lax.fori_loop(0, 2, ahead_step, 0)
    send_result(shift(place.z, 1), 1)
    send_result(shift(place.z, -1), -1)
    value1[relay]()
    key1[relay]()
    lax.fori_loop(0, 2, rest_step, 0)
    send_result(shift(place.z, 2), 2)
    send_result(place.z, 0)
    value1[total]()
    key1[total]()
    spread(1, 0)
    value0[start]()
    value0[relay]()
    value1[expand]()
    key1[expand]()
    spread(0, 0)
    key0[start]()
    key0[relay]()
    value0[total]()
    value0[expand]()
    key0[total]()
    key0[expand]()

    for which, (_, dst) in enumerate(results):
        for step in STEPS:
            links.got(("r", which, step), dst.at[:, cols(shift(place.z, -step))])
        links.got(("r", which, "partner"), dst.at[:, cols(SIDE + 1 - mine)])
        own["r", which, 0].wait()
        own["r", which, 1].wait()
    for slot, (first, count) in enumerate(GROUPS):
        for kv in range(2):
            for step in STEPS:
                links.got(
                    ("u", kv, slot, step),
                    outs[kv].at[:, cols(shift(place.x, -step) * HEADS_X + first, count)],
                )
            own["u", kv, slot].wait()
    links.finish()


def prepare_kernel(pattern, live, spots, entries, biases):
    place = Place()
    for unit in range(sum(SLOT_UNITS)):
        z = unit if unit < SIDE else place.z if unit == SIDE else place.partner_z()
        frame = (place.y * SIDE + z) * CORES + place.core
        base = unit % SIDE * ENTRIES

        def clear(i, carry, unit=unit, base=base):
            entries[unit * ALL_SPOTS + i] = base + DEAD
            return carry

        lax.fori_loop(0, ALL_SPOTS, clear, 0, unroll=8)

        def note(j, carry, unit=unit, base=base, frame=frame):
            spot = spot_of(pattern[j, frame])
            alive = j < live[frame]
            spots[unit * NSEL + j] = spot
            biases[unit * NSEL + j] = jnp.where(alive, 0.0, -jnp.inf).astype(F32)
            entries[unit * ALL_SPOTS + spot] = jnp.where(alive, base + j, base + DEAD)
            return carry

        lax.fori_loop(0, NSEL, note, 0, unroll=4)


def store_kernel(*refs):
    sems = refs[-1]
    copies = [pltpu.make_async_copy(refs[i], refs[4 + i], sems.at[i]) for i in range(4)]
    for copy in copies:
        copy.start()
    for copy in copies:
        copy.wait()


ANY = pl.BlockSpec(memory_space=pl.ANY)
HBM = pl.BlockSpec(memory_space=pltpu.HBM)
VMEM = pl.BlockSpec(memory_space=pltpu.VMEM)
SMEM = pl.BlockSpec(memory_space=pltpu.SMEM)


def body(queries, keys_in, values_in, grad_out, assign, pattern, live_blocks):
    inputs = [
        pltpu.with_memory_space_constraint(one, pltpu.HBM)
        for one in (keys_in, values_in, queries, grad_out, assign.reshape(1, TOK))
    ]
    shape = jax.ShapeDtypeStruct
    dma = pltpu.SemaphoreType.DMA
    units = sum(SLOT_UNITS)
    lists = pl.pallas_call(
        prepare_kernel,
        out_shape=(
            shape((units * NSEL,), jnp.int32),
            shape((units * ALL_SPOTS,), jnp.int32),
            shape((units * NSEL,), F32),
        ),
        in_specs=[SMEM] * 2,
        out_specs=(SMEM,) * 3,
        compiler_params=pltpu.CompilerParams(vmem_limit_bytes=STORE_LIMIT),
        name="prepare",
    )(pattern.T, live_blocks)

    def half(*dims):
        return pltpu.VMEM(dims, BF)

    results = pl.pallas_call(
        layer_kernel,
        out_shape=(
            shape(queries.shape, BF),
            shape(queries.shape, BF),
            shape(keys_in.shape, BF),
            shape(keys_in.shape, BF),
        ),
        in_specs=[HBM] * 5 + [SMEM] * 3,
        out_specs=(ANY,) * 4,
        scratch_shapes=[
            half(ALL_SPOTS, KB, HD),
            half(ALL_SPOTS, KB, HD),
            half(ALL_SPOTS, KB, HD),
            half(ALL_SPOTS, KB, HD),
            half(2, TOK, WIDTH),
            half(2, HEADS_X, 2, KB, HD),
            pltpu.VMEM((1, TOK), jnp.int32),
            half(units, TOK, HD),
            half(units, TOK, HD),
            half(NSEL * KB, HD),
            half(NSEL * KB, HD),
            pltpu.VMEM((NSEL * KB, TOK), F32),
            pltpu.VMEM((NSEL * KB, TOK), F32),
            half(SLOT_UNITS[0] * ENTRIES, KB, HD),
            half(SLOT_UNITS[1] * ENTRIES, KB, HD),
            half(SLOT_UNITS[0] * ENTRIES, KB, HD),
            half(SLOT_UNITS[1] * ENTRIES, KB, HD),
            half(units, TOK, HD),
            half(units, TOK, HD),
            half(2, 2, ALL_SPOTS, KB, HD),
            half(2, 2, SIDE, GROUP, KB, HD),
            half(2, 2, 2, GROUP // 2, KB, HD),
            half(2, 2, 3, GROUP, KB, HD),
            half(2, 2, 3, GROUP, KB, HD),
            half(2, 2, GROUP, KB, HD),
            half(2, 2, SIDE, 2, KB, HD),
            half(2, TOK, WIDTH),
            dma((SEMS,)),
            dma((SEMS,)),
            dma((LOCAL,)),
        ],
        compiler_params=pltpu.CompilerParams(
            collective_id=0, has_side_effects=True, vmem_limit_bytes=VMEM_LIMIT
        ),
        name="layer",
    )(*inputs, *lists)
    return pl.pallas_call(
        store_kernel,
        out_shape=tuple(shape(one.shape, BF) for one in results),
        in_specs=[VMEM] * 4,
        out_specs=(HBM,) * 4,
        scratch_shapes=[dma((4,))],
        compiler_params=pltpu.CompilerParams(vmem_limit_bytes=STORE_LIMIT),
        name="store",
    )(*results)


def solution(mesh):
    return jax.shard_map(
        body,
        mesh=mesh,
        in_specs=(
            P("frame", "head"),
            P(("frame", "head"), None),
            P(("frame", "head"), None),
            P("frame", "head"),
            P("frame"),
            P(),
            P(),
        ),
        out_specs=(
            P("frame", "head"),
            P("frame", "head"),
            P(("frame", "head"), None),
            P(("frame", "head"), None),
        ),
        check_vma=False,
    )
```

```python
import math

import jax
import jax.numpy as jnp
from jax import lax
from jax.experimental import pallas as pl
from jax.experimental.pallas import tpu as pltpu
from jax.sharding import PartitionSpec as P

HD = 128
KB = 64
NSEL = 16
SIDE = 4
CORES = 2
HEADS_X = 6
WIDTH = HEADS_X * HD
TOK = 512
TOK_DEV = TOK // SIDE
SLOTS = 128
SLOT_UNITS = (4, 2)
CHUNK = 512
SCALE = 1.0 / math.sqrt(HD)
MESH = pl.DeviceIdType.MESH
BF = jnp.bfloat16
F32 = jnp.float32
VMEM_LIMIT = 50 * 1024 * 1024
STORE_LIMIT = 8 * 1024 * 1024
GROUP = SIDE * SLOTS // KB
LOG2_E = math.log2(math.e)
STEPS = (1, -1, 2)
GROUPS = ((0, SIDE), (SIDE, HEADS_X - SIDE))
GATHER_PARTS = ((0, 1), (0, 0), (1, 0), (1, 1))
GATHER_STRAIGHT = (GATHER_PARTS[0], GATHER_PARTS[3])
SCATTER_STRAIGHT = ()


class Place:
    def __init__(self):
        frame = lax.axis_index("frame")
        self.x = lax.axis_index("head")
        self.core = frame % CORES
        self.z = (frame // CORES) % SIDE
        self.y = frame // (CORES * SIDE)

    def device(self, y, z, core, x):
        return {"frame": (y * SIDE + z) * CORES + core, "head": x}

    def ring(self, axis, step):
        at = {"x": self.x, "y": self.y, "z": self.z}
        at[axis] = (at[axis] + step + SIDE) % SIDE
        return self.device(at["y"], at["z"], self.core, at["x"])

    def sibling(self):
        return self.device(self.y, self.z, 1 - self.core, self.x)

    def partner_z(self):
        return jnp.where(self.core == 0, self.z + 1 - 2 * (self.z % 2), SIDE - 1 - self.z)

    def partner(self):
        return self.device(self.y, self.partner_z(), self.core, self.x)


def shift(at, step):
    return (at + step + SIDE) % SIDE


def meet(place):
    partners = [place.sibling()]
    partners += [place.ring(axis, step) for axis in ("x", "y", "z") for step in STEPS]
    barrier = pltpu.get_barrier_semaphore()
    for target in partners:
        pl.semaphore_signal(barrier, inc=1, device_id=target, device_id_type=MESH)
    pl.semaphore_wait(barrier, len(partners))


class Links:
    def __init__(self, place, send, recv, local):
        self.send, self.recv, self.local = send, recv, local
        self.anyone = place.sibling()
        self.started = []
        self.names = {}
        self.local_names = {}

    def sem(self, name):
        return self.names.setdefault(name, len(self.names))

    def remote(self, name, src, dst, target):
        sem = self.sem(name)
        return pltpu.make_async_remote_copy(
            src_ref=src,
            dst_ref=dst,
            send_sem=self.send.at[sem],
            recv_sem=self.recv.at[sem],
            device_id=target,
            device_id_type=MESH,
        )

    def go(self, name, src, dst, target):
        copy = self.remote(name, src, dst, target)
        copy.start()
        self.started.append(copy)

    def got(self, name, region):
        self.remote(name, region, region, self.anyone).wait_recv()

    def here(self, name, src, dst):
        sem = self.local_names.setdefault(name, len(self.local_names))
        copy = pltpu.make_async_copy(src, dst, self.local.at[sem])
        copy.start()
        return copy

    def finish(self):
        for copy in self.started:
            copy.wait_send()


def low(ref):
    return ref.at[pl.ds(0, GROUP // 2)]


def high(ref):
    return ref.at[pl.ds(GROUP // 2, GROUP // 2)]


def spot_of(block):
    y, z, core, half = block >> 4, (block >> 2) & 3, (block >> 1) & 1, block & 1
    return (y << 4) + (core << 3) + (z << 1) + half


def cols(head, count=1):
    return pl.ds(pl.multiple_of(head * HD, HD), count * HD)


def token_rows(x):
    return pl.ds(pl.multiple_of(x * TOK_DEV, TOK_DEV), TOK_DEV)


def slot_hot_of(assign):
    slots = lax.broadcasted_iota(jnp.int32, (SLOTS, TOK), 0)
    return (slots == assign[0:1, :]).astype(F32)


SEMS = 4 * 14 + 2 * 4 + 4 * 14 + 2 * 4
LOCAL = 4 + 4 + 4 + 4 + 4
ALL_FRAMES = SIDE * SIDE * CORES
ALL_SPOTS = ALL_FRAMES * SLOTS // KB
DEAD = NSEL
ENTRIES = NSEL + 1


def layer_kernel(
    keys, values, queries, upstream, assign, pattern_in, live_in,
    attended, query_grad, grad_keys, grad_values,
    keys0, keys1, values0, values1, tokens, merged, assign_own, query_in, upstream_in,
    listed, expo, inverses, prob_grad, key_part0, key_part1, value_part0, value_part1, att_out, dq_out, dense,
    twin, halves, fulls, outgoing, column, pieces, token_out, pattern, live, entries_out, entries, send, recv, local,
):
    place = Place()
    links = Links(place, send, recv, local)
    lists = [links.here("pattern", pattern_in, pattern), links.here("live", live_in, live)]
    meet(place)
    sources = (keys, values)
    every = ((keys0, keys1), (values0, values1))
    parts = ((key_part0, key_part1), (value_part0, value_part1))
    outs = (grad_keys, grad_values)
    own = {}
    mine = place.z % 2

    def send_tokens(kv, slot):
        first, count = GROUPS[slot]
        for step in STEPS:
            links.go(
                ("x", kv, slot, step),
                sources[kv].at[:, cols(shift(place.x, step) * HEADS_X + first, count)],
                tokens.at[kv, token_rows(place.x), cols(first, count)],
                place.ring("x", step),
            )
        own[kv, slot] = links.here(
            ("x", kv, slot),
            sources[kv].at[:, cols(place.x * HEADS_X + first, count)],
            tokens.at[kv, token_rows(place.x), cols(first, count)],
        )

    moved = ((queries, query_in), (upstream, upstream_in))

    def send_rows(which):
        src, dst = moved[which]
        for step in STEPS:
            links.go(
                ("q", which, step), src.at[:, cols(shift(place.z, step))], dst.at[place.z],
                place.ring("z", step),
            )
        own["q", which, 0] = links.here(("q", which, 0), src.at[:, cols(place.z)], dst.at[place.z])

    def send_pair(which):
        src, dst = moved[which]
        links.go(
            ("q", which, "partner"), src.at[:, cols(SIDE + 1 - mine)], dst.at[SIDE + 1],
            place.partner(),
        )
        own["q", which, 1] = links.here(
            ("q", which, 1), src.at[:, cols(SIDE + mine)], dst.at[SIDE]
        )

    def rows_arrived():
        for which, (_, dst) in enumerate(moved):
            for step in STEPS:
                links.got(("q", which, step), dst.at[shift(place.z, -step)])
            own["q", which, 0].wait()

    def pair_arrived():
        for which, (_, dst) in enumerate(moved):
            links.got(("q", which, "partner"), dst.at[SIDE + 1])
            own["q", which, 1].wait()

    send_tokens(*GATHER_PARTS[0])
    send_tokens(*GATHER_PARTS[1])
    send_rows(0)
    send_tokens(*GATHER_PARTS[2])
    send_tokens(*GATHER_PARTS[3])
    for one in lists:
        one.wait()
    links.here("assign", assign, assign_own).wait()
    hot = slot_hot_of(assign_own)
    divisor = jnp.maximum(jnp.sum(hot, axis=1, keepdims=True), 1.0)
    hot = hot.astype(BF)
    for kv in range(2):
        for slot, count in enumerate(SLOT_UNITS):
            for at in range(count):
                parts[kv][slot][at * ENTRIES + DEAD] = jnp.zeros((KB, HD), BF)

    def group(y, core):
        return pl.ds((y * CORES + core) * GROUP, GROUP)

    def gather_stage(kv, slot):
        first, count = GROUPS[slot]
        out = every[kv][slot]
        straight = (kv, slot) in GATHER_STRAIGHT

        def region(step):
            return out.at[group(shift(place.y, step), place.core)]

        def cell(z):
            return pl.ds((place.y * CORES + place.core) * GROUP + z * 2, 2)

        def pass_on(step):
            links.go(("s", kv, slot, step), region(step), region(step), place.sibling())

        def merge():
            own[kv, slot].wait()
            for step in STEPS:
                links.got(
                    ("x", kv, slot, step),
                    tokens.at[kv, token_rows(shift(place.x, -step)), cols(first, count)],
                )
            sums = jnp.dot(
                hot, tokens[kv, :, first * HD : (first + count) * HD], preferred_element_type=F32
            )
            mean = (sums / divisor).astype(BF)
            for i in range(count):
                merged[kv, first + i] = mean[:, i * HD : (i + 1) * HD].reshape(2, KB, HD)

            def head_of(z):
                return z if slot == 0 else SIDE + z % 2

            for step in STEPS:
                links.go(
                    ("z", kv, slot, step),
                    merged.at[kv, head_of(shift(place.z, step))],
                    out.at[cell(place.z)],
                    place.ring("z", step),
                )
            out[cell(place.z)] = merged[kv, head_of(place.z)]
            if (kv, slot) == GATHER_PARTS[0]:
                send_pair(0)
                send_pair(1)
            if (kv, slot) == GATHER_PARTS[1]:
                send_rows(1)

        def row():
            for step in STEPS:
                links.got(("z", kv, slot, step), out.at[cell(shift(place.z, -step))])
            for step in STEPS if straight else STEPS[:2]:
                links.go(("y", kv, slot, step), region(0), region(0), place.ring("y", step))
            pass_on(0)

        def near():
            links.got(("y", kv, slot, 1), region(-1))
            if not straight:
                links.go(("f", kv, slot, 1), low(region(-1)), low(region(-1)), place.ring("y", 1))
            pass_on(-1)
            links.got(("y", kv, slot, -1), region(1))
            if not straight:
                links.go(("f", kv, slot, -1), high(region(1)), high(region(1)), place.ring("y", -1))
            pass_on(1)

        def far():
            if straight:
                links.got(("y", kv, slot, 2), region(2))
            else:
                links.got(("f", kv, slot, 1), low(region(2)))
                links.got(("f", kv, slot, -1), high(region(2)))
            pass_on(2)

        def close():
            for step in (0, -1, 1, 2):
                links.got(
                    ("s", kv, slot, step),
                    out.at[group(shift(place.y, step), 1 - place.core)],
                )

        return merge, row, near, far, close

    def frame_of(slot, at):
        z = at if slot == 0 else jnp.where(at == 0, place.z, place.partner_z())
        return (place.y * SIDE + z) * CORES + place.core

    def note_entries():
        lanes = lax.broadcasted_iota(jnp.int32, (1, HD), 1)
        entries_out[...] = jnp.zeros_like(entries_out)
        for slot, count in enumerate(SLOT_UNITS):
            for at in range(count):
                frame = frame_of(slot, at)
                entry = jnp.full((1, HD), at * ENTRIES + DEAD, jnp.int32)
                for j in range(NSEL):
                    named = (lanes == spot_of(pattern[j, frame])) & (lanes * 0 + j < live[0, frame])
                    entry = jnp.where(named, at * ENTRIES + j, entry)
                entries_out[slot * SIDE + at : slot * SIDE + at + 1, :] = entry
        links.here("entries", entries_out, entries).wait()

    spans = [(a, a + CHUNK) for a in range(0, NSEL * KB, CHUNK)]
    chunk_blocks = CHUNK // KB

    def select(every_one, frame):
        for j in range(NSEL):
            listed[j * KB : (j + 1) * KB, :] = every_one[spot_of(pattern[j, frame])]

    def keep(kv, slot, unit, a, grads):
        into = pl.ds((unit - slot * SIDE) * ENTRIES + a // KB, chunk_blocks)
        parts[kv][slot][into] = grads.astype(BF).reshape(chunk_blocks, KB, HD)

    def weigh(slot, unit):
        frame = frame_of(slot, unit - slot * SIDE)
        select(every[0][slot], frame)
        q_t, g = query_in[unit].T, upstream_in[unit]
        top = jnp.full((1, TOK), -jnp.inf, F32)
        for a, b in spans:
            scores = jnp.dot(listed[a:b, :], q_t, preferred_element_type=F32)
            ids = lax.broadcasted_iota(jnp.int32, (CHUNK, TOK), 0) + a
            scores = jnp.where(ids < live[0, frame] * KB, scores, -jnp.inf)
            expo[unit, a:b, :] = scores
            top = jnp.maximum(top, jnp.max(scores, axis=0, keepdims=True))
        top = top * (SCALE * LOG2_E)
        total = jnp.zeros((1, TOK), F32)
        for a, b in spans:
            weights = jnp.exp2(expo[unit, a:b, :] * (SCALE * LOG2_E) - top)
            expo[unit, a:b, :] = weights
            total = total + jnp.sum(weights, axis=0, keepdims=True)
        inverse = 1.0 / total
        inverses[unit] = inverse
        for a, b in spans:
            probs = (expo[unit, a:b, :] * inverse).astype(BF)
            keep(1, slot, unit, a, jnp.dot(probs, g, preferred_element_type=F32))

    def attend(slot, unit):
        frame = frame_of(slot, unit - slot * SIDE)
        select(every[1][slot], frame)
        q, g_t = query_in[unit], upstream_in[unit].T
        inverse = inverses[unit]
        weighted = jnp.zeros((HD, TOK), F32)
        for a, b in spans:
            weighted = weighted + lax.dot_general(
                listed[a:b, :], expo[unit, a:b, :].astype(BF), (((0,), (0,)), ((), ())),
                preferred_element_type=F32,
            )
            prob_grad[a:b, :] = jnp.dot(listed[a:b, :], g_t, preferred_element_type=F32)
        att_t = (weighted * inverse).astype(BF)
        att_out[unit] = att_t.T
        delta = jnp.sum(g_t.astype(F32) * att_t.astype(F32), axis=0, keepdims=True)
        select(every[0][slot], frame)
        dq = jnp.zeros((HD, TOK), F32)
        for a, b in spans:
            probs = expo[unit, a:b, :] * inverse
            score_grad = (probs * (prob_grad[a:b, :] - delta)).astype(BF)
            keep(0, slot, unit, a, jnp.dot(score_grad, q, preferred_element_type=F32) * SCALE)
            dq = dq + lax.dot_general(
                listed[a:b, :], score_grad, (((0,), (0,)), ((), ())), preferred_element_type=F32
            )
        dq_out[unit] = (dq * SCALE).astype(BF).T

    results = ((att_out, attended), (dq_out, query_grad))

    def send_result(unit, step):
        for which, (src, dst) in enumerate(results):
            if step:
                links.go(
                    ("r", which, step), src.at[unit], dst.at[:, cols(place.z)], place.ring("z", step)
                )
            else:
                own["r", which, 0] = links.here(
                    ("r", which, 0), src.at[unit], dst.at[:, cols(place.z)]
                )

    def send_pair_result():
        for which, (src, dst) in enumerate(results):
            links.go(
                ("r", which, "partner"), src.at[SIDE + 1], dst.at[:, cols(SIDE + mine)],
                place.partner(),
            )
            own["r", which, 1] = links.here(
                ("r", which, 1), src.at[SIDE], dst.at[:, cols(SIDE + mine)]
            )

    def spread(kv, slot):
        def region(y, core):
            def one(i, carry):
                spot = (y * CORES + core) * GROUP + i
                total = jnp.zeros((KB, HD), F32)
                for at in range(SLOT_UNITS[slot]):
                    entry = entries[slot * SIDE + at, spot]
                    total = total + parts[kv][slot][entry].astype(F32)
                dense[kv, slot, spot] = total.astype(BF)
                return carry

            lax.fori_loop(0, GROUP, one, 0)

        for step in (2, 1, -1, 0):
            y = shift(place.y, step)
            region(y, 1 - place.core)
            links.go(
                ("t", kv, slot, step), dense.at[kv, slot, group(y, 1 - place.core)],
                twin.at[kv, slot, y], place.sibling(),
            )
        for step in (2, 1, -1, 0):
            region(shift(place.y, step), place.core)

    def scatter_stage(kv, slot):
        first, count = GROUPS[slot]
        straight = (kv, slot) in SCATTER_STRAIGHT
        half_in, full_in, out = halves.at[kv, slot], fulls.at[kv, slot], outgoing.at[kv, slot]

        def term(step):
            y = shift(place.y, step)
            links.got(("t", kv, slot, step), twin.at[kv, slot, y])
            here = dense[kv, slot, group(y, place.core)]
            return here.astype(F32) + twin[kv, slot, y].astype(F32)

        def start():
            out[2] = term(2).astype(BF)
            if straight:
                links.go(("w", kv, slot, 2), out.at[2], full_in.at[2], place.ring("y", 2))
                return
            links.go(("h", kv, slot, 1), low(out.at[2]), half_in.at[0], place.ring("y", 1))
            links.go(("h", kv, slot, -1), high(out.at[2]), half_in.at[1], place.ring("y", -1))

        def relay():
            ahead = term(1)
            behind = term(-1)
            half = GROUP // 2
            if straight:
                for at, step, value in ((0, 1, ahead), (1, -1, behind)):
                    out[at] = value.astype(BF)
                    links.go(
                        ("w", kv, slot, step), out.at[at], full_in.at[at], place.ring("y", step)
                    )
                return
            links.got(("h", kv, slot, 1), half_in.at[0])
            out[0, 0:half] = (ahead[0:half] + half_in[0].astype(F32)).astype(BF)
            out[0, half:GROUP] = ahead[half:GROUP].astype(BF)
            links.go(("w", kv, slot, 1), out.at[0], full_in.at[0], place.ring("y", 1))
            links.got(("h", kv, slot, -1), half_in.at[1])
            out[1, 0:half] = behind[0:half].astype(BF)
            out[1, half:GROUP] = (behind[half:GROUP] + half_in[1].astype(F32)).astype(BF)
            links.go(("w", kv, slot, -1), out.at[1], full_in.at[1], place.ring("y", -1))

        def total():
            value = term(0)
            links.got(("w", kv, slot, 1), full_in.at[0])
            links.got(("w", kv, slot, -1), full_in.at[1])
            value = value + full_in[0].astype(F32) + full_in[1].astype(F32)
            if straight:
                links.got(("w", kv, slot, 2), full_in.at[2])
                value = value + full_in[2].astype(F32)
            column[kv, slot] = value.astype(BF)
            for step in STEPS:
                links.go(
                    ("v", kv, slot, step),
                    column.at[kv, slot, pl.ds(shift(place.z, step) * 2, 2)],
                    pieces.at[kv, slot, place.z], place.ring("z", step),
                )
            pieces[kv, slot, place.z] = column[kv, slot, pl.ds(place.z * 2, 2)]

        def expand():
            for step in STEPS:
                links.got(("v", kv, slot, step), pieces.at[kv, slot, shift(place.z, -step)])
            ready = [pieces[kv, slot, z].astype(F32).reshape(SLOTS, HD) for z in range(SIDE)]
            if slot == 1:
                ready = [ready[0] + ready[2], ready[1] + ready[3]]
            mean = jnp.concatenate([(one / divisor).astype(BF) for one in ready], axis=1)
            token_out[kv, :, first * HD : (first + count) * HD] = lax.dot_general(
                hot, mean, (((0,), (0,)), ((), ())), preferred_element_type=F32
            ).astype(BF)
            to = cols(place.x * HEADS_X + first, count)
            for step in STEPS:
                links.go(
                    ("u", kv, slot, step),
                    token_out.at[kv, token_rows(shift(place.x, step)), cols(first, count)],
                    outs[kv].at[:, to],
                    place.ring("x", step),
                )
            own["u", kv, slot] = links.here(
                ("u", kv, slot),
                token_out.at[kv, token_rows(place.x), cols(first, count)],
                outs[kv].at[:, to],
            )

        return start, relay, total, expand

    def work(what, slot, first, count):
        def one(i, carry):
            what(slot, SIDE + first + i if slot else shift(place.z, first + 2 * i))
            return carry

        lax.fori_loop(0, count, one, 0)

    merge, row, near, far, close = range(5)
    key1, key0, value0, value1 = [gather_stage(kv, slot) for kv, slot in GATHER_PARTS]
    start, relay, total, expand = range(4)
    key_grad1, key_grad0, value_grad0, value_grad1 = [
        scatter_stage(kv, slot) for kv, slot in GATHER_PARTS
    ]
    note_entries()
    key1[merge]()
    key1[row]()
    key0[merge]()
    key1[near]()
    key0[row]()
    key1[far]()
    value0[merge]()
    key1[close]()
    pair_arrived()
    work(weigh, 1, 0, 1)
    value1[merge]()
    key0[near]()
    value0[row]()
    work(weigh, 1, 1, 1)
    key0[far]()
    value1[row]()
    spread(1, 1)
    key0[close]()
    rows_arrived()
    work(weigh, 0, 1, 2)
    value0[near]()
    value_grad1[start]()
    work(weigh, 0, 2, 2)
    value0[far]()
    value1[near]()
    spread(1, 0)
    value0[close]()
    value_grad1[relay]()
    value_grad0[start]()
    work(attend, 0, 1, 2)
    send_result(shift(place.z, 1), 1)
    send_result(shift(place.z, -1), -1)
    value1[far]()
    value_grad0[relay]()
    value_grad1[total]()
    work(attend, 0, 2, 2)
    send_result(shift(place.z, 2), 2)
    send_result(place.z, 0)
    value1[close]()
    spread(0, 0)
    value_grad1[expand]()
    value_grad0[total]()
    key_grad0[start]()
    work(attend, 1, 0, 2)
    send_pair_result()
    spread(0, 1)
    value_grad0[expand]()
    key_grad0[relay]()
    key_grad1[start]()
    key_grad1[relay]()
    key_grad0[total]()
    key_grad0[expand]()
    key_grad1[total]()
    key_grad1[expand]()

    for which, (_, dst) in enumerate(results):
        for step in STEPS:
            links.got(("r", which, step), dst.at[:, cols(shift(place.z, -step))])
        links.got(("r", which, "partner"), dst.at[:, cols(SIDE + 1 - mine)])
        own["r", which, 0].wait()
        own["r", which, 1].wait()
    for slot, (first, count) in enumerate(GROUPS):
        for kv in range(2):
            for step in STEPS:
                links.got(
                    ("u", kv, slot, step),
                    outs[kv].at[:, cols(shift(place.x, -step) * HEADS_X + first, count)],
                )
            own["u", kv, slot].wait()
    links.finish()


def store_kernel(*refs):
    sems = refs[-1]
    copies = [pltpu.make_async_copy(refs[i], refs[4 + i], sems.at[i]) for i in range(4)]
    for copy in copies:
        copy.start()
    for copy in copies:
        copy.wait()


ANY = pl.BlockSpec(memory_space=pl.ANY)
HBM = pl.BlockSpec(memory_space=pltpu.HBM)
VMEM = pl.BlockSpec(memory_space=pltpu.VMEM)


def body(queries, keys_in, values_in, grad_out, assign, pattern, live_blocks):
    inputs = [
        pltpu.with_memory_space_constraint(one, pltpu.HBM)
        for one in (
            keys_in, values_in, queries, grad_out, assign.reshape(1, TOK), pattern.T,
            live_blocks.reshape(1, ALL_FRAMES),
        )
    ]
    shape = jax.ShapeDtypeStruct
    dma = pltpu.SemaphoreType.DMA
    units = sum(SLOT_UNITS)
    def half(*dims):
        return pltpu.VMEM(dims, BF)

    results = pl.pallas_call(
        layer_kernel,
        out_shape=(
            shape(queries.shape, BF),
            shape(queries.shape, BF),
            shape(keys_in.shape, BF),
            shape(keys_in.shape, BF),
        ),
        in_specs=[HBM] * 7,
        out_specs=(ANY,) * 4,
        scratch_shapes=[
            half(ALL_SPOTS, KB, HD),
            half(ALL_SPOTS, KB, HD),
            half(ALL_SPOTS, KB, HD),
            half(ALL_SPOTS, KB, HD),
            half(2, TOK, WIDTH),
            half(2, HEADS_X, 2, KB, HD),
            pltpu.VMEM((1, TOK), jnp.int32),
            half(units, TOK, HD),
            half(units, TOK, HD),
            half(NSEL * KB, HD),
            pltpu.VMEM((units, NSEL * KB, TOK), F32),
            pltpu.VMEM((units, 1, TOK), F32),
            pltpu.VMEM((NSEL * KB, TOK), F32),
            half(SLOT_UNITS[0] * ENTRIES, KB, HD),
            half(SLOT_UNITS[1] * ENTRIES, KB, HD),
            half(SLOT_UNITS[0] * ENTRIES, KB, HD),
            half(SLOT_UNITS[1] * ENTRIES, KB, HD),
            half(units, TOK, HD),
            half(units, TOK, HD),
            half(2, 2, ALL_SPOTS, KB, HD),
            half(2, 2, SIDE, GROUP, KB, HD),
            half(2, 2, 2, GROUP // 2, KB, HD),
            half(2, 2, 3, GROUP, KB, HD),
            half(2, 2, 3, GROUP, KB, HD),
            half(2, 2, GROUP, KB, HD),
            half(2, 2, SIDE, 2, KB, HD),
            half(2, TOK, WIDTH),
            pltpu.SMEM((NSEL, ALL_FRAMES), jnp.int32),
            pltpu.SMEM((1, ALL_FRAMES), jnp.int32),
            pltpu.VMEM((8, HD), jnp.int32),
            pltpu.SMEM((8, HD), jnp.int32),
            dma((SEMS,)),
            dma((SEMS,)),
            dma((LOCAL,)),
        ],
        compiler_params=pltpu.CompilerParams(
            collective_id=0, has_side_effects=True, vmem_limit_bytes=VMEM_LIMIT
        ),
        name="layer",
    )(*inputs)
    return pl.pallas_call(
        store_kernel,
        out_shape=tuple(shape(one.shape, BF) for one in results),
        in_specs=[VMEM] * 4,
        out_specs=(HBM,) * 4,
        scratch_shapes=[dma((4,))],
        compiler_params=pltpu.CompilerParams(vmem_limit_bytes=STORE_LIMIT),
        name="store",
    )(*results)


def solution(mesh):
    return jax.shard_map(
        body,
        mesh=mesh,
        in_specs=(
            P("frame", "head"),
            P(("frame", "head"), None),
            P(("frame", "head"), None),
            P("frame", "head"),
            P("frame"),
            P(),
            P(),
        ),
        out_specs=(
            P("frame", "head"),
            P("frame", "head"),
            P(("frame", "head"), None),
            P(("frame", "head"), None),
        ),
        check_vma=False,
    )
```

```python
import math

import jax
import jax.numpy as jnp
from jax import lax
from jax.experimental import pallas as pl
from jax.experimental.pallas import tpu as pltpu
from jax.sharding import PartitionSpec as P

HD = 128
KB = 64
NSEL = 16
SIDE = 4
CORES = 2
HEADS_X = 6
WIDTH = HEADS_X * HD
TOK = 512
TOK_DEV = TOK // SIDE
SLOTS = 128
SLOT_UNITS = (4, 2)
CHUNK = 512
SCALE = 1.0 / math.sqrt(HD)
MESH = pl.DeviceIdType.MESH
BF = jnp.bfloat16
F32 = jnp.float32
VMEM_LIMIT = 50 * 1024 * 1024
STORE_LIMIT = 8 * 1024 * 1024
GROUP = SIDE * SLOTS // KB
LOG2_E = math.log2(math.e)
STEPS = (1, -1, 2)
GROUPS = ((0, SIDE), (SIDE, HEADS_X - SIDE))
GATHER_PARTS = ((0, 1), (0, 0), (1, 0), (1, 1))
GATHER_STRAIGHT = (GATHER_PARTS[0],)
SCATTER_STRAIGHT = ((0, 0),)


class Place:
    def __init__(self):
        frame = lax.axis_index("frame")
        self.x = lax.axis_index("head")
        self.core = frame % CORES
        self.z = (frame // CORES) % SIDE
        self.y = frame // (CORES * SIDE)

    def device(self, y, z, core, x):
        return {"frame": (y * SIDE + z) * CORES + core, "head": x}

    def ring(self, axis, step):
        at = {"x": self.x, "y": self.y, "z": self.z}
        at[axis] = (at[axis] + step + SIDE) % SIDE
        return self.device(at["y"], at["z"], self.core, at["x"])

    def sibling(self):
        return self.device(self.y, self.z, 1 - self.core, self.x)

    def partner_z(self):
        return jnp.where(self.core == 0, self.z + 1 - 2 * (self.z % 2), SIDE - 1 - self.z)

    def partner(self):
        return self.device(self.y, self.partner_z(), self.core, self.x)


def shift(at, step):
    return (at + step + SIDE) % SIDE


def meet(place):
    partners = [place.sibling()]
    partners += [place.ring(axis, step) for axis in ("x", "y", "z") for step in STEPS]
    barrier = pltpu.get_barrier_semaphore()
    for target in partners:
        pl.semaphore_signal(barrier, inc=1, device_id=target, device_id_type=MESH)
    pl.semaphore_wait(barrier, len(partners))


class Links:
    def __init__(self, place, send, recv, local):
        self.send, self.recv, self.local = send, recv, local
        self.anyone = place.sibling()
        self.started = []
        self.names = {}
        self.local_names = {}

    def sem(self, name):
        return self.names.setdefault(name, len(self.names))

    def remote(self, name, src, dst, target):
        sem = self.sem(name)
        return pltpu.make_async_remote_copy(
            src_ref=src,
            dst_ref=dst,
            send_sem=self.send.at[sem],
            recv_sem=self.recv.at[sem],
            device_id=target,
            device_id_type=MESH,
        )

    def go(self, name, src, dst, target):
        copy = self.remote(name, src, dst, target)
        copy.start()
        self.started.append(copy)

    def got(self, name, region):
        self.remote(name, region, region, self.anyone).wait_recv()

    def here(self, name, src, dst):
        sem = self.local_names.setdefault(name, len(self.local_names))
        copy = pltpu.make_async_copy(src, dst, self.local.at[sem])
        copy.start()
        return copy

    def finish(self):
        for copy in self.started:
            copy.wait_send()


def low(ref):
    return ref.at[pl.ds(0, GROUP // 2)]


def high(ref):
    return ref.at[pl.ds(GROUP // 2, GROUP // 2)]


def spot_of(block):
    y, z, core, half = block >> 4, (block >> 2) & 3, (block >> 1) & 1, block & 1
    return (y << 4) + (core << 3) + (z << 1) + half


def cols(head, count=1):
    return pl.ds(pl.multiple_of(head * HD, HD), count * HD)


def token_rows(x):
    return pl.ds(pl.multiple_of(x * TOK_DEV, TOK_DEV), TOK_DEV)


def slot_hot_of(assign):
    slots = lax.broadcasted_iota(jnp.int32, (SLOTS, TOK), 0)
    return (slots == assign[0:1, :]).astype(F32)


SEMS = 4 * 14 + 2 * 4 + 4 * 14 + 2 * 4
LOCAL = 4 + 4 + 4 + 4 + 4
ALL_FRAMES = SIDE * SIDE * CORES
ALL_SPOTS = ALL_FRAMES * SLOTS // KB
DEAD = NSEL
ENTRIES = NSEL + 1


def layer_kernel(
    keys, values, queries, upstream, assign, pattern_in, live_in,
    attended, query_grad, grad_keys, grad_values,
    keys0, keys1, values0, values1, tokens, merged, assign_own, query_in, upstream_in,
    listed, expo, inverses, prob_grad, key_part0, key_part1, value_part0, value_part1, att_out, dq_out, dense,
    twin, halves, fulls, outgoing, column, pieces, token_out, pattern, live, entries_out, entries, send, recv, local,
):
    place = Place()
    links = Links(place, send, recv, local)
    lists = [links.here("pattern", pattern_in, pattern), links.here("live", live_in, live)]
    meet(place)
    sources = (keys, values)
    every = ((keys0, keys1), (values0, values1))
    parts = ((key_part0, key_part1), (value_part0, value_part1))
    outs = (grad_keys, grad_values)
    own = {}
    mine = place.z % 2

    def send_tokens(kv, slot):
        first, count = GROUPS[slot]
        for step in STEPS:
            links.go(
                ("x", kv, slot, step),
                sources[kv].at[:, cols(shift(place.x, step) * HEADS_X + first, count)],
                tokens.at[kv, token_rows(place.x), cols(first, count)],
                place.ring("x", step),
            )
        own[kv, slot] = links.here(
            ("x", kv, slot),
            sources[kv].at[:, cols(place.x * HEADS_X + first, count)],
            tokens.at[kv, token_rows(place.x), cols(first, count)],
        )

    moved = ((queries, query_in), (upstream, upstream_in))

    def send_rows(which):
        src, dst = moved[which]
        for step in STEPS:
            links.go(
                ("q", which, step), src.at[:, cols(shift(place.z, step))], dst.at[place.z],
                place.ring("z", step),
            )
        own["q", which, 0] = links.here(("q", which, 0), src.at[:, cols(place.z)], dst.at[place.z])

    def send_pair(which):
        src, dst = moved[which]
        links.go(
            ("q", which, "partner"), src.at[:, cols(SIDE + 1 - mine)], dst.at[SIDE + 1],
            place.partner(),
        )
        own["q", which, 1] = links.here(
            ("q", which, 1), src.at[:, cols(SIDE + mine)], dst.at[SIDE]
        )

    def rows_arrived():
        for which, (_, dst) in enumerate(moved):
            for step in STEPS:
                links.got(("q", which, step), dst.at[shift(place.z, -step)])
            own["q", which, 0].wait()

    def pair_arrived():
        for which, (_, dst) in enumerate(moved):
            links.got(("q", which, "partner"), dst.at[SIDE + 1])
            own["q", which, 1].wait()

    send_tokens(*GATHER_PARTS[0])
    send_tokens(*GATHER_PARTS[1])
    send_rows(0)
    send_tokens(*GATHER_PARTS[2])
    send_tokens(*GATHER_PARTS[3])
    for one in lists:
        one.wait()
    links.here("assign", assign, assign_own).wait()
    hot = slot_hot_of(assign_own)
    divisor = jnp.maximum(jnp.sum(hot, axis=1, keepdims=True), 1.0)
    hot = hot.astype(BF)
    for kv in range(2):
        for slot, count in enumerate(SLOT_UNITS):
            for at in range(count):
                parts[kv][slot][at * ENTRIES + DEAD] = jnp.zeros((KB, HD), BF)

    def group(y, core):
        return pl.ds((y * CORES + core) * GROUP, GROUP)

    def gather_stage(kv, slot):
        first, count = GROUPS[slot]
        out = every[kv][slot]
        straight = (kv, slot) in GATHER_STRAIGHT

        def region(step):
            return out.at[group(shift(place.y, step), place.core)]

        def cell(z):
            return pl.ds((place.y * CORES + place.core) * GROUP + z * 2, 2)

        def pass_on(step):
            links.go(("s", kv, slot, step), region(step), region(step), place.sibling())

        def merge():
            own[kv, slot].wait()
            for step in STEPS:
                links.got(
                    ("x", kv, slot, step),
                    tokens.at[kv, token_rows(shift(place.x, -step)), cols(first, count)],
                )
            sums = jnp.dot(
                hot, tokens[kv, :, first * HD : (first + count) * HD], preferred_element_type=F32
            )
            mean = (sums / divisor).astype(BF)
            for i in range(count):
                merged[kv, first + i] = mean[:, i * HD : (i + 1) * HD].reshape(2, KB, HD)

            def head_of(z):
                return z if slot == 0 else SIDE + z % 2

            for step in STEPS:
                links.go(
                    ("z", kv, slot, step),
                    merged.at[kv, head_of(shift(place.z, step))],
                    out.at[cell(place.z)],
                    place.ring("z", step),
                )
            out[cell(place.z)] = merged[kv, head_of(place.z)]
            if (kv, slot) == GATHER_PARTS[0]:
                send_pair(0)
                send_pair(1)
            if (kv, slot) == GATHER_PARTS[1]:
                send_rows(1)

        def row():
            for step in STEPS:
                links.got(("z", kv, slot, step), out.at[cell(shift(place.z, -step))])
            for step in STEPS if straight else STEPS[:2]:
                links.go(("y", kv, slot, step), region(0), region(0), place.ring("y", step))
            pass_on(0)

        def near():
            links.got(("y", kv, slot, 1), region(-1))
            if not straight:
                links.go(("f", kv, slot, 1), low(region(-1)), low(region(-1)), place.ring("y", 1))
            pass_on(-1)
            links.got(("y", kv, slot, -1), region(1))
            if not straight:
                links.go(("f", kv, slot, -1), high(region(1)), high(region(1)), place.ring("y", -1))
            pass_on(1)

        def far():
            if straight:
                links.got(("y", kv, slot, 2), region(2))
            else:
                links.got(("f", kv, slot, 1), low(region(2)))
                links.got(("f", kv, slot, -1), high(region(2)))
            pass_on(2)

        def close():
            for step in (0, -1, 1, 2):
                links.got(
                    ("s", kv, slot, step),
                    out.at[group(shift(place.y, step), 1 - place.core)],
                )

        return merge, row, near, far, close

    def frame_of(slot, at):
        z = at if slot == 0 else jnp.where(at == 0, place.z, place.partner_z())
        return (place.y * SIDE + z) * CORES + place.core

    def note_entries():
        lanes = lax.broadcasted_iota(jnp.int32, (1, HD), 1)
        entries_out[...] = jnp.zeros_like(entries_out)
        for slot, count in enumerate(SLOT_UNITS):
            for at in range(count):
                frame = frame_of(slot, at)
                entry = jnp.full((1, HD), at * ENTRIES + DEAD, jnp.int32)
                for j in range(NSEL):
                    named = (lanes == spot_of(pattern[j, frame])) & (lanes * 0 + j < live[0, frame])
                    entry = jnp.where(named, at * ENTRIES + j, entry)
                entries_out[slot * SIDE + at : slot * SIDE + at + 1, :] = entry
        links.here("entries", entries_out, entries).wait()

    spans = [(a, a + CHUNK) for a in range(0, NSEL * KB, CHUNK)]
    chunk_blocks = CHUNK // KB

    def select(every_one, frame):
        for j in range(NSEL):
            listed[j * KB : (j + 1) * KB, :] = every_one[spot_of(pattern[j, frame])]

    def keep(kv, slot, unit, a, grads):
        into = pl.ds((unit - slot * SIDE) * ENTRIES + a // KB, chunk_blocks)
        parts[kv][slot][into] = grads.astype(BF).reshape(chunk_blocks, KB, HD)

    def weigh(slot, unit):
        frame = frame_of(slot, unit - slot * SIDE)
        select(every[0][slot], frame)
        q_t, g = query_in[unit].T, upstream_in[unit]
        top = jnp.full((1, TOK), -jnp.inf, F32)
        for a, b in spans:
            scores = jnp.dot(listed[a:b, :], q_t, preferred_element_type=F32)
            ids = lax.broadcasted_iota(jnp.int32, (CHUNK, TOK), 0) + a
            scores = jnp.where(ids < live[0, frame] * KB, scores, -jnp.inf)
            expo[unit, a:b, :] = scores
            top = jnp.maximum(top, jnp.max(scores, axis=0, keepdims=True))
        top = top * (SCALE * LOG2_E)
        total = jnp.zeros((1, TOK), F32)
        for a, b in spans:
            weights = jnp.exp2(expo[unit, a:b, :] * (SCALE * LOG2_E) - top)
            expo[unit, a:b, :] = weights
            total = total + jnp.sum(weights, axis=0, keepdims=True)
        inverse = 1.0 / total
        inverses[unit] = inverse
        for a, b in spans:
            probs = (expo[unit, a:b, :] * inverse).astype(BF)
            keep(1, slot, unit, a, jnp.dot(probs, g, preferred_element_type=F32))

    def attend(slot, unit):
        frame = frame_of(slot, unit - slot * SIDE)
        select(every[1][slot], frame)
        q, g_t = query_in[unit], upstream_in[unit].T
        inverse = inverses[unit]
        weighted = jnp.zeros((HD, TOK), F32)
        for a, b in spans:
            weighted = weighted + lax.dot_general(
                listed[a:b, :], expo[unit, a:b, :].astype(BF), (((0,), (0,)), ((), ())),
                preferred_element_type=F32,
            )
            prob_grad[a:b, :] = jnp.dot(listed[a:b, :], g_t, preferred_element_type=F32)
        att_t = (weighted * inverse).astype(BF)
        att_out[unit] = att_t.T
        delta = jnp.sum(g_t.astype(F32) * att_t.astype(F32), axis=0, keepdims=True)
        select(every[0][slot], frame)
        dq = jnp.zeros((HD, TOK), F32)
        for a, b in spans:
            probs = expo[unit, a:b, :] * inverse
            score_grad = (probs * (prob_grad[a:b, :] - delta)).astype(BF)
            keep(0, slot, unit, a, jnp.dot(score_grad, q, preferred_element_type=F32) * SCALE)
            dq = dq + lax.dot_general(
                listed[a:b, :], score_grad, (((0,), (0,)), ((), ())), preferred_element_type=F32
            )
        dq_out[unit] = (dq * SCALE).astype(BF).T

    results = ((att_out, attended), (dq_out, query_grad))

    def send_result(unit, step):
        for which, (src, dst) in enumerate(results):
            if step:
                links.go(
                    ("r", which, step), src.at[unit], dst.at[:, cols(place.z)], place.ring("z", step)
                )
            else:
                own["r", which, 0] = links.here(
                    ("r", which, 0), src.at[unit], dst.at[:, cols(place.z)]
                )

    def send_pair_result():
        for which, (src, dst) in enumerate(results):
            links.go(
                ("r", which, "partner"), src.at[SIDE + 1], dst.at[:, cols(SIDE + mine)],
                place.partner(),
            )
            own["r", which, 1] = links.here(
                ("r", which, 1), src.at[SIDE], dst.at[:, cols(SIDE + mine)]
            )

    def spread(kv, slot):
        def region(y, core):
            def one(i, carry):
                spot = (y * CORES + core) * GROUP + i
                total = jnp.zeros((KB, HD), F32)
                for at in range(SLOT_UNITS[slot]):
                    entry = entries[slot * SIDE + at, spot]
                    total = total + parts[kv][slot][entry].astype(F32)
                dense[kv, slot, spot] = total.astype(BF)
                return carry

            lax.fori_loop(0, GROUP, one, 0)

        for step in (2, 1, -1, 0):
            y = shift(place.y, step)
            region(y, 1 - place.core)
            links.go(
                ("t", kv, slot, step), dense.at[kv, slot, group(y, 1 - place.core)],
                twin.at[kv, slot, y], place.sibling(),
            )
        for step in (2, 1, -1, 0):
            region(shift(place.y, step), place.core)

    def scatter_stage(kv, slot):
        first, count = GROUPS[slot]
        straight = (kv, slot) in SCATTER_STRAIGHT
        half_in, full_in, out = halves.at[kv, slot], fulls.at[kv, slot], outgoing.at[kv, slot]

        def term(step):
            y = shift(place.y, step)
            links.got(("t", kv, slot, step), twin.at[kv, slot, y])
            here = dense[kv, slot, group(y, place.core)]
            return here.astype(F32) + twin[kv, slot, y].astype(F32)

        def start():
            out[2] = term(2).astype(BF)
            if straight:
                links.go(("w", kv, slot, 2), out.at[2], full_in.at[2], place.ring("y", 2))
                return
            links.go(("h", kv, slot, 1), low(out.at[2]), half_in.at[0], place.ring("y", 1))
            links.go(("h", kv, slot, -1), high(out.at[2]), half_in.at[1], place.ring("y", -1))

        def relay():
            ahead = term(1)
            behind = term(-1)
            half = GROUP // 2
            if straight:
                for at, step, value in ((0, 1, ahead), (1, -1, behind)):
                    out[at] = value.astype(BF)
                    links.go(
                        ("w", kv, slot, step), out.at[at], full_in.at[at], place.ring("y", step)
                    )
                return
            links.got(("h", kv, slot, 1), half_in.at[0])
            out[0, 0:half] = (ahead[0:half] + half_in[0].astype(F32)).astype(BF)
            out[0, half:GROUP] = ahead[half:GROUP].astype(BF)
            links.go(("w", kv, slot, 1), out.at[0], full_in.at[0], place.ring("y", 1))
            links.got(("h", kv, slot, -1), half_in.at[1])
            out[1, 0:half] = behind[0:half].astype(BF)
            out[1, half:GROUP] = (behind[half:GROUP] + half_in[1].astype(F32)).astype(BF)
            links.go(("w", kv, slot, -1), out.at[1], full_in.at[1], place.ring("y", -1))

        def total():
            value = term(0)
            links.got(("w", kv, slot, 1), full_in.at[0])
            links.got(("w", kv, slot, -1), full_in.at[1])
            value = value + full_in[0].astype(F32) + full_in[1].astype(F32)
            if straight:
                links.got(("w", kv, slot, 2), full_in.at[2])
                value = value + full_in[2].astype(F32)
            column[kv, slot] = value.astype(BF)
            for step in STEPS:
                links.go(
                    ("v", kv, slot, step),
                    column.at[kv, slot, pl.ds(shift(place.z, step) * 2, 2)],
                    pieces.at[kv, slot, place.z], place.ring("z", step),
                )
            pieces[kv, slot, place.z] = column[kv, slot, pl.ds(place.z * 2, 2)]

        def expand():
            for step in STEPS:
                links.got(("v", kv, slot, step), pieces.at[kv, slot, shift(place.z, -step)])
            ready = [pieces[kv, slot, z].astype(F32).reshape(SLOTS, HD) for z in range(SIDE)]
            if slot == 1:
                ready = [ready[0] + ready[2], ready[1] + ready[3]]
            mean = jnp.concatenate([(one / divisor).astype(BF) for one in ready], axis=1)
            token_out[kv, :, first * HD : (first + count) * HD] = lax.dot_general(
                hot, mean, (((0,), (0,)), ((), ())), preferred_element_type=F32
            ).astype(BF)
            to = cols(place.x * HEADS_X + first, count)
            for step in STEPS:
                links.go(
                    ("u", kv, slot, step),
                    token_out.at[kv, token_rows(shift(place.x, step)), cols(first, count)],
                    outs[kv].at[:, to],
                    place.ring("x", step),
                )
            own["u", kv, slot] = links.here(
                ("u", kv, slot),
                token_out.at[kv, token_rows(place.x), cols(first, count)],
                outs[kv].at[:, to],
            )

        return start, relay, total, expand

    def work(what, slot, first, count):
        def one(i, carry):
            what(slot, SIDE + first + i if slot else shift(place.z, first + 2 * i))
            return carry

        lax.fori_loop(0, count, one, 0)

    merge, row, near, far, close = range(5)
    key1, key0, value0, value1 = [gather_stage(kv, slot) for kv, slot in GATHER_PARTS]
    start, relay, total, expand = range(4)
    key_grad1, key_grad0, value_grad0, value_grad1 = [
        scatter_stage(kv, slot) for kv, slot in GATHER_PARTS
    ]
    note_entries()
    key1[merge]()
    key1[row]()
    key0[merge]()
    key1[near]()
    key0[row]()
    key1[far]()
    value0[merge]()
    key1[close]()
    pair_arrived()
    work(weigh, 1, 0, 1)
    value1[merge]()
    key0[near]()
    value0[row]()
    work(weigh, 1, 1, 1)
    key0[far]()
    value1[row]()
    spread(1, 1)
    key0[close]()
    rows_arrived()
    work(weigh, 0, 1, 2)
    value0[near]()
    value_grad1[start]()
    work(weigh, 0, 2, 2)
    value0[far]()
    value1[near]()
    spread(1, 0)
    value0[close]()
    value_grad1[relay]()
    value_grad0[start]()
    work(attend, 0, 1, 2)
    send_result(shift(place.z, 1), 1)
    send_result(shift(place.z, -1), -1)
    value1[far]()
    value_grad0[relay]()
    value_grad1[total]()
    work(attend, 0, 2, 2)
    send_result(shift(place.z, 2), 2)
    send_result(place.z, 0)
    value1[close]()
    spread(0, 0)
    value_grad1[expand]()
    value_grad0[total]()
    key_grad0[start]()
    key_grad0[relay]()
    work(attend, 1, 0, 2)
    send_pair_result()
    spread(0, 1)
    value_grad0[expand]()
    key_grad1[start]()
    key_grad1[relay]()
    key_grad0[total]()
    key_grad0[expand]()
    key_grad1[total]()
    key_grad1[expand]()

    for which, (_, dst) in enumerate(results):
        for step in STEPS:
            links.got(("r", which, step), dst.at[:, cols(shift(place.z, -step))])
        links.got(("r", which, "partner"), dst.at[:, cols(SIDE + 1 - mine)])
        own["r", which, 0].wait()
        own["r", which, 1].wait()
    for slot, (first, count) in enumerate(GROUPS):
        for kv in range(2):
            for step in STEPS:
                links.got(
                    ("u", kv, slot, step),
                    outs[kv].at[:, cols(shift(place.x, -step) * HEADS_X + first, count)],
                )
            own["u", kv, slot].wait()
    links.finish()


def store_kernel(*refs):
    sems = refs[-1]
    copies = [pltpu.make_async_copy(refs[i], refs[4 + i], sems.at[i]) for i in range(4)]
    for copy in copies:
        copy.start()
    for copy in copies:
        copy.wait()


ANY = pl.BlockSpec(memory_space=pl.ANY)
HBM = pl.BlockSpec(memory_space=pltpu.HBM)
VMEM = pl.BlockSpec(memory_space=pltpu.VMEM)


def body(queries, keys_in, values_in, grad_out, assign, pattern, live_blocks):
    inputs = [
        pltpu.with_memory_space_constraint(one, pltpu.HBM)
        for one in (
            keys_in, values_in, queries, grad_out, assign.reshape(1, TOK), pattern.T,
            live_blocks.reshape(1, ALL_FRAMES),
        )
    ]
    shape = jax.ShapeDtypeStruct
    dma = pltpu.SemaphoreType.DMA
    units = sum(SLOT_UNITS)
    def half(*dims):
        return pltpu.VMEM(dims, BF)

    results = pl.pallas_call(
        layer_kernel,
        out_shape=(
            shape(queries.shape, BF),
            shape(queries.shape, BF),
            shape(keys_in.shape, BF),
            shape(keys_in.shape, BF),
        ),
        in_specs=[HBM] * 7,
        out_specs=(ANY,) * 4,
        scratch_shapes=[
            half(ALL_SPOTS, KB, HD),
            half(ALL_SPOTS, KB, HD),
            half(ALL_SPOTS, KB, HD),
            half(ALL_SPOTS, KB, HD),
            half(2, TOK, WIDTH),
            half(2, HEADS_X, 2, KB, HD),
            pltpu.VMEM((1, TOK), jnp.int32),
            half(units, TOK, HD),
            half(units, TOK, HD),
            half(NSEL * KB, HD),
            pltpu.VMEM((units, NSEL * KB, TOK), F32),
            pltpu.VMEM((units, 1, TOK), F32),
            pltpu.VMEM((NSEL * KB, TOK), F32),
            half(SLOT_UNITS[0] * ENTRIES, KB, HD),
            half(SLOT_UNITS[1] * ENTRIES, KB, HD),
            half(SLOT_UNITS[0] * ENTRIES, KB, HD),
            half(SLOT_UNITS[1] * ENTRIES, KB, HD),
            half(units, TOK, HD),
            half(units, TOK, HD),
            half(2, 2, ALL_SPOTS, KB, HD),
            half(2, 2, SIDE, GROUP, KB, HD),
            half(2, 2, 2, GROUP // 2, KB, HD),
            half(2, 2, 3, GROUP, KB, HD),
            half(2, 2, 3, GROUP, KB, HD),
            half(2, 2, GROUP, KB, HD),
            half(2, 2, SIDE, 2, KB, HD),
            half(2, TOK, WIDTH),
            pltpu.SMEM((NSEL, ALL_FRAMES), jnp.int32),
            pltpu.SMEM((1, ALL_FRAMES), jnp.int32),
            pltpu.VMEM((8, HD), jnp.int32),
            pltpu.SMEM((8, HD), jnp.int32),
            dma((SEMS,)),
            dma((SEMS,)),
            dma((LOCAL,)),
        ],
        compiler_params=pltpu.CompilerParams(
            collective_id=0, has_side_effects=True, vmem_limit_bytes=VMEM_LIMIT
        ),
        name="layer",
    )(*inputs)
    return pl.pallas_call(
        store_kernel,
        out_shape=tuple(shape(one.shape, BF) for one in results),
        in_specs=[VMEM] * 4,
        out_specs=(HBM,) * 4,
        scratch_shapes=[dma((4,))],
        compiler_params=pltpu.CompilerParams(vmem_limit_bytes=STORE_LIMIT),
        name="store",
    )(*results)


def solution(mesh):
    return jax.shard_map(
        body,
        mesh=mesh,
        in_specs=(
            P("frame", "head"),
            P(("frame", "head"), None),
            P(("frame", "head"), None),
            P("frame", "head"),
            P("frame"),
            P(),
            P(),
        ),
        out_specs=(
            P("frame", "head"),
            P("frame", "head"),
            P(("frame", "head"), None),
            P(("frame", "head"), None),
        ),
        check_vma=False,
    )
```

```python
import math

import jax
import jax.numpy as jnp
from jax import lax
from jax.experimental import pallas as pl
from jax.experimental.pallas import tpu as pltpu
from jax.sharding import PartitionSpec as P

HD = 128
KB = 64
NSEL = 16
SIDE = 4
CORES = 2
HEADS_X = 6
WIDTH = HEADS_X * HD
TOK = 512
TOK_DEV = TOK // SIDE
SLOTS = 128
SLOT_UNITS = (4, 2)
CHUNK = 512
SCALE = 1.0 / math.sqrt(HD)
MESH = pl.DeviceIdType.MESH
BF = jnp.bfloat16
F32 = jnp.float32
VMEM_LIMIT = 50 * 1024 * 1024
STORE_LIMIT = 8 * 1024 * 1024
GROUP = SIDE * SLOTS // KB
LOG2_E = math.log2(math.e)
STEPS = (1, -1, 2)
GROUPS = ((0, SIDE), (SIDE, HEADS_X - SIDE))
GATHER_PARTS = ((0, 1), (0, 0), (1, 0), (1, 1))
GATHER_STRAIGHT = (GATHER_PARTS[0],)
SCATTER_STRAIGHT = ((0, 0),)


class Place:
    def __init__(self):
        frame = lax.axis_index("frame")
        self.x = lax.axis_index("head")
        self.core = frame % CORES
        self.z = (frame // CORES) % SIDE
        self.y = frame // (CORES * SIDE)

    def device(self, y, z, core, x):
        return {"frame": (y * SIDE + z) * CORES + core, "head": x}

    def ring(self, axis, step):
        at = {"x": self.x, "y": self.y, "z": self.z}
        at[axis] = (at[axis] + step + SIDE) % SIDE
        return self.device(at["y"], at["z"], self.core, at["x"])

    def sibling(self):
        return self.device(self.y, self.z, 1 - self.core, self.x)

    def partner_z(self):
        return jnp.where(self.core == 0, self.z + 1 - 2 * (self.z % 2), SIDE - 1 - self.z)

    def partner(self):
        return self.device(self.y, self.partner_z(), self.core, self.x)


def shift(at, step):
    return (at + step + SIDE) % SIDE


def meet(place):
    partners = [place.sibling()]
    partners += [place.ring(axis, step) for axis in ("x", "y", "z") for step in STEPS]
    barrier = pltpu.get_barrier_semaphore()
    for target in partners:
        pl.semaphore_signal(barrier, inc=1, device_id=target, device_id_type=MESH)
    pl.semaphore_wait(barrier, len(partners))


class Links:
    def __init__(self, place, send, recv, local):
        self.send, self.recv, self.local = send, recv, local
        self.anyone = place.sibling()
        self.started = []
        self.names = {}
        self.local_names = {}

    def sem(self, name):
        return self.names.setdefault(name, len(self.names))

    def remote(self, name, src, dst, target):
        sem = self.sem(name)
        return pltpu.make_async_remote_copy(
            src_ref=src,
            dst_ref=dst,
            send_sem=self.send.at[sem],
            recv_sem=self.recv.at[sem],
            device_id=target,
            device_id_type=MESH,
        )

    def go(self, name, src, dst, target):
        copy = self.remote(name, src, dst, target)
        copy.start()
        self.started.append(copy)

    def got(self, name, region):
        self.remote(name, region, region, self.anyone).wait_recv()

    def here(self, name, src, dst):
        sem = self.local_names.setdefault(name, len(self.local_names))
        copy = pltpu.make_async_copy(src, dst, self.local.at[sem])
        copy.start()
        return copy

    def finish(self):
        for copy in self.started:
            copy.wait_send()


def low(ref):
    return ref.at[pl.ds(0, GROUP // 2)]


def high(ref):
    return ref.at[pl.ds(GROUP // 2, GROUP // 2)]


def spot_of(block):
    y, z, core, half = block >> 4, (block >> 2) & 3, (block >> 1) & 1, block & 1
    return (y << 4) + (core << 3) + (z << 1) + half


def cols(head, count=1):
    return pl.ds(pl.multiple_of(head * HD, HD), count * HD)


def token_rows(x):
    return pl.ds(pl.multiple_of(x * TOK_DEV, TOK_DEV), TOK_DEV)


def slot_hot_of(assign):
    slots = lax.broadcasted_iota(jnp.int32, (SLOTS, TOK), 0)
    return (slots == assign[0:1, :]).astype(F32)


SEMS = 4 * 14 + 2 * 4 + 4 * 14 + 2 * 4
LOCAL = 4 + 4 + 4 + 4 + 4
ALL_FRAMES = SIDE * SIDE * CORES
ALL_SPOTS = ALL_FRAMES * SLOTS // KB
DEAD = NSEL
ENTRIES = NSEL + 1


def layer_kernel(
    keys, values, queries, upstream, assign, pattern_in, live_in,
    attended, query_grad, grad_keys, grad_values,
    keys0, keys1, values0, values1, tokens, merged, assign_own, query_in, upstream_in,
    listed, expo, inverses, prob_grad, key_part0, key_part1, value_part0, value_part1, att_out, dq_out, dense,
    twin, halves, fulls, outgoing, column, pieces, token_out, pattern, live, entries_out, entries, send, recv, local,
):
    place = Place()
    links = Links(place, send, recv, local)
    lists = [links.here("pattern", pattern_in, pattern), links.here("live", live_in, live)]
    meet(place)
    sources = (keys, values)
    every = ((keys0, keys1), (values0, values1))
    parts = ((key_part0, key_part1), (value_part0, value_part1))
    outs = (grad_keys, grad_values)
    own = {}
    mine = place.z % 2

    def send_tokens(kv, slot):
        first, count = GROUPS[slot]
        for step in STEPS:
            links.go(
                ("x", kv, slot, step),
                sources[kv].at[:, cols(shift(place.x, step) * HEADS_X + first, count)],
                tokens.at[kv, token_rows(place.x), cols(first, count)],
                place.ring("x", step),
            )
        own[kv, slot] = links.here(
            ("x", kv, slot),
            sources[kv].at[:, cols(place.x * HEADS_X + first, count)],
            tokens.at[kv, token_rows(place.x), cols(first, count)],
        )

    moved = ((queries, query_in), (upstream, upstream_in))

    def send_rows(which):
        src, dst = moved[which]
        for step in STEPS:
            links.go(
                ("q", which, step), src.at[:, cols(shift(place.z, step))], dst.at[place.z],
                place.ring("z", step),
            )
        own["q", which, 0] = links.here(("q", which, 0), src.at[:, cols(place.z)], dst.at[place.z])

    def send_pair(which):
        src, dst = moved[which]
        links.go(
            ("q", which, "partner"), src.at[:, cols(SIDE + 1 - mine)], dst.at[SIDE + 1],
            place.partner(),
        )
        own["q", which, 1] = links.here(
            ("q", which, 1), src.at[:, cols(SIDE + mine)], dst.at[SIDE]
        )

    def rows_arrived():
        for which, (_, dst) in enumerate(moved):
            for step in STEPS:
                links.got(("q", which, step), dst.at[shift(place.z, -step)])
            own["q", which, 0].wait()

    def pair_arrived():
        for which, (_, dst) in enumerate(moved):
            links.got(("q", which, "partner"), dst.at[SIDE + 1])
            own["q", which, 1].wait()

    send_tokens(*GATHER_PARTS[0])
    send_tokens(*GATHER_PARTS[1])
    send_rows(0)
    send_tokens(*GATHER_PARTS[2])
    send_tokens(*GATHER_PARTS[3])
    for one in lists:
        one.wait()
    links.here("assign", assign, assign_own).wait()
    hot = slot_hot_of(assign_own)
    divisor = jnp.maximum(jnp.sum(hot, axis=1, keepdims=True), 1.0)
    hot = hot.astype(BF)
    for kv in range(2):
        for slot, count in enumerate(SLOT_UNITS):
            for at in range(count):
                parts[kv][slot][at * ENTRIES + DEAD] = jnp.zeros((KB, HD), BF)

    def group(y, core):
        return pl.ds((y * CORES + core) * GROUP, GROUP)

    def gather_stage(kv, slot):
        first, count = GROUPS[slot]
        out = every[kv][slot]
        straight = (kv, slot) in GATHER_STRAIGHT

        def region(step):
            return out.at[group(shift(place.y, step), place.core)]

        def cell(z):
            return pl.ds((place.y * CORES + place.core) * GROUP + z * 2, 2)

        def pass_on(step):
            links.go(("s", kv, slot, step), region(step), region(step), place.sibling())

        def merge():
            own[kv, slot].wait()
            for step in STEPS:
                links.got(
                    ("x", kv, slot, step),
                    tokens.at[kv, token_rows(shift(place.x, -step)), cols(first, count)],
                )
            sums = jnp.dot(
                hot, tokens[kv, :, first * HD : (first + count) * HD], preferred_element_type=F32
            )
            mean = (sums / divisor).astype(BF)
            for i in range(count):
                merged[kv, first + i] = mean[:, i * HD : (i + 1) * HD].reshape(2, KB, HD)

            def head_of(z):
                return z if slot == 0 else SIDE + z % 2

            for step in STEPS:
                links.go(
                    ("z", kv, slot, step),
                    merged.at[kv, head_of(shift(place.z, step))],
                    out.at[cell(place.z)],
                    place.ring("z", step),
                )
            out[cell(place.z)] = merged[kv, head_of(place.z)]
            if (kv, slot) == GATHER_PARTS[0]:
                send_pair(0)
                send_pair(1)
            if (kv, slot) == GATHER_PARTS[1]:
                send_rows(1)

        def row():
            for step in STEPS:
                links.got(("z", kv, slot, step), out.at[cell(shift(place.z, -step))])
            for step in STEPS if straight else STEPS[:2]:
                links.go(("y", kv, slot, step), region(0), region(0), place.ring("y", step))
            pass_on(0)

        def near():
            links.got(("y", kv, slot, 1), region(-1))
            if not straight:
                links.go(("f", kv, slot, 1), low(region(-1)), low(region(-1)), place.ring("y", 1))
            pass_on(-1)
            links.got(("y", kv, slot, -1), region(1))
            if not straight:
                links.go(("f", kv, slot, -1), high(region(1)), high(region(1)), place.ring("y", -1))
            pass_on(1)

        def far():
            if straight:
                links.got(("y", kv, slot, 2), region(2))
            else:
                links.got(("f", kv, slot, 1), low(region(2)))
                links.got(("f", kv, slot, -1), high(region(2)))
            pass_on(2)

        def close():
            for step in (0, -1, 1, 2):
                links.got(
                    ("s", kv, slot, step),
                    out.at[group(shift(place.y, step), 1 - place.core)],
                )

        return merge, row, near, far, close

    def frame_of(slot, at):
        z = at if slot == 0 else jnp.where(at == 0, place.z, place.partner_z())
        return (place.y * SIDE + z) * CORES + place.core

    def note_entries():
        lanes = lax.broadcasted_iota(jnp.int32, (1, HD), 1)
        entries_out[...] = jnp.zeros_like(entries_out)
        for slot, count in enumerate(SLOT_UNITS):
            for at in range(count):
                frame = frame_of(slot, at)
                entry = jnp.full((1, HD), at * ENTRIES + DEAD, jnp.int32)
                for j in range(NSEL):
                    named = (lanes == spot_of(pattern[j, frame])) & (lanes * 0 + j < live[0, frame])
                    entry = jnp.where(named, at * ENTRIES + j, entry)
                entries_out[slot * SIDE + at : slot * SIDE + at + 1, :] = entry
        links.here("entries", entries_out, entries).wait()

    spans = [(a, a + CHUNK) for a in range(0, NSEL * KB, CHUNK)]
    chunk_blocks = CHUNK // KB

    def select(every_one, frame):
        for j in range(NSEL):
            listed[j * KB : (j + 1) * KB, :] = every_one[spot_of(pattern[j, frame])]

    def keep(kv, slot, unit, a, grads):
        into = pl.ds((unit - slot * SIDE) * ENTRIES + a // KB, chunk_blocks)
        parts[kv][slot][into] = grads.astype(BF).reshape(chunk_blocks, KB, HD)

    def weigh(slot, unit):
        frame = frame_of(slot, unit - slot * SIDE)
        select(every[0][slot], frame)
        q_t, g = query_in[unit].T, upstream_in[unit]
        top = jnp.full((1, TOK), -jnp.inf, F32)
        for a, b in spans:
            scores = jnp.dot(listed[a:b, :], q_t, preferred_element_type=F32)
            ids = lax.broadcasted_iota(jnp.int32, (CHUNK, TOK), 0) + a
            scores = jnp.where(ids < live[0, frame] * KB, scores, -jnp.inf)
            expo[unit, a:b, :] = scores
            top = jnp.maximum(top, jnp.max(scores, axis=0, keepdims=True))
        top = top * (SCALE * LOG2_E)
        total = jnp.zeros((1, TOK), F32)
        for a, b in spans:
            weights = jnp.exp2(expo[unit, a:b, :] * (SCALE * LOG2_E) - top)
            expo[unit, a:b, :] = weights
            total = total + jnp.sum(weights, axis=0, keepdims=True)
        inverse = 1.0 / total
        inverses[unit] = inverse
        for a, b in spans:
            probs = (expo[unit, a:b, :] * inverse).astype(BF)
            keep(1, slot, unit, a, jnp.dot(probs, g, preferred_element_type=F32))

    def attend(slot, unit):
        frame = frame_of(slot, unit - slot * SIDE)
        select(every[1][slot], frame)
        q, g_t = query_in[unit], upstream_in[unit].T
        inverse = inverses[unit]
        weighted = jnp.zeros((HD, TOK), F32)
        for a, b in spans:
            weighted = weighted + lax.dot_general(
                listed[a:b, :], expo[unit, a:b, :].astype(BF), (((0,), (0,)), ((), ())),
                preferred_element_type=F32,
            )
            prob_grad[a:b, :] = jnp.dot(listed[a:b, :], g_t, preferred_element_type=F32)
        att_t = (weighted * inverse).astype(BF)
        att_out[unit] = att_t.T
        delta = jnp.sum(g_t.astype(F32) * att_t.astype(F32), axis=0, keepdims=True)
        select(every[0][slot], frame)
        dq = jnp.zeros((HD, TOK), F32)
        for a, b in spans:
            probs = expo[unit, a:b, :] * inverse
            score_grad = (probs * (prob_grad[a:b, :] - delta)).astype(BF)
            keep(0, slot, unit, a, jnp.dot(score_grad, q, preferred_element_type=F32) * SCALE)
            dq = dq + lax.dot_general(
                listed[a:b, :], score_grad, (((0,), (0,)), ((), ())), preferred_element_type=F32
            )
        dq_out[unit] = (dq * SCALE).astype(BF).T

    results = ((att_out, attended), (dq_out, query_grad))

    def send_result(unit, step):
        for which, (src, dst) in enumerate(results):
            if step:
                links.go(
                    ("r", which, step), src.at[unit], dst.at[:, cols(place.z)], place.ring("z", step)
                )
            else:
                own["r", which, 0] = links.here(
                    ("r", which, 0), src.at[unit], dst.at[:, cols(place.z)]
                )

    def send_pair_result():
        for which, (src, dst) in enumerate(results):
            links.go(
                ("r", which, "partner"), src.at[SIDE + 1], dst.at[:, cols(SIDE + mine)],
                place.partner(),
            )
            own["r", which, 1] = links.here(
                ("r", which, 1), src.at[SIDE], dst.at[:, cols(SIDE + mine)]
            )

    def spread(kv, slot):
        def region(y, core):
            def one(i, carry):
                spot = (y * CORES + core) * GROUP + i
                total = jnp.zeros((KB, HD), F32)
                for at in range(SLOT_UNITS[slot]):
                    entry = entries[slot * SIDE + at, spot]
                    total = total + parts[kv][slot][entry].astype(F32)
                dense[kv, slot, spot] = total.astype(BF)
                return carry

            lax.fori_loop(0, GROUP, one, 0, unroll=GROUP)

        for step in (2, 1, -1, 0):
            y = shift(place.y, step)
            region(y, 1 - place.core)
            links.go(
                ("t", kv, slot, step), dense.at[kv, slot, group(y, 1 - place.core)],
                twin.at[kv, slot, y], place.sibling(),
            )
        for step in (2, 1, -1, 0):
            region(shift(place.y, step), place.core)

    def scatter_stage(kv, slot):
        first, count = GROUPS[slot]
        straight = (kv, slot) in SCATTER_STRAIGHT
        half_in, full_in, out = halves.at[kv, slot], fulls.at[kv, slot], outgoing.at[kv, slot]

        def term(step):
            y = shift(place.y, step)
            links.got(("t", kv, slot, step), twin.at[kv, slot, y])
            here = dense[kv, slot, group(y, place.core)]
            return here.astype(F32) + twin[kv, slot, y].astype(F32)

        def start():
            out[2] = term(2).astype(BF)
            if straight:
                links.go(("w", kv, slot, 2), out.at[2], full_in.at[2], place.ring("y", 2))
                return
            links.go(("h", kv, slot, 1), low(out.at[2]), half_in.at[0], place.ring("y", 1))
            links.go(("h", kv, slot, -1), high(out.at[2]), half_in.at[1], place.ring("y", -1))

        def relay():
            ahead = term(1)
            behind = term(-1)
            half = GROUP // 2
            if straight:
                for at, step, value in ((0, 1, ahead), (1, -1, behind)):
                    out[at] = value.astype(BF)
                    links.go(
                        ("w", kv, slot, step), out.at[at], full_in.at[at], place.ring("y", step)
                    )
                return
            links.got(("h", kv, slot, 1), half_in.at[0])
            out[0, 0:half] = (ahead[0:half] + half_in[0].astype(F32)).astype(BF)
            out[0, half:GROUP] = ahead[half:GROUP].astype(BF)
            links.go(("w", kv, slot, 1), out.at[0], full_in.at[0], place.ring("y", 1))
            links.got(("h", kv, slot, -1), half_in.at[1])
            out[1, 0:half] = behind[0:half].astype(BF)
            out[1, half:GROUP] = (behind[half:GROUP] + half_in[1].astype(F32)).astype(BF)
            links.go(("w", kv, slot, -1), out.at[1], full_in.at[1], place.ring("y", -1))

        def total():
            value = term(0)
            links.got(("w", kv, slot, 1), full_in.at[0])
            links.got(("w", kv, slot, -1), full_in.at[1])
            value = value + full_in[0].astype(F32) + full_in[1].astype(F32)
            if straight:
                links.got(("w", kv, slot, 2), full_in.at[2])
                value = value + full_in[2].astype(F32)
            column[kv, slot] = value.astype(BF)
            for step in STEPS:
                links.go(
                    ("v", kv, slot, step),
                    column.at[kv, slot, pl.ds(shift(place.z, step) * 2, 2)],
                    pieces.at[kv, slot, place.z], place.ring("z", step),
                )
            pieces[kv, slot, place.z] = column[kv, slot, pl.ds(place.z * 2, 2)]

        def expand():
            for step in STEPS:
                links.got(("v", kv, slot, step), pieces.at[kv, slot, shift(place.z, -step)])
            ready = [pieces[kv, slot, z].astype(F32).reshape(SLOTS, HD) for z in range(SIDE)]
            if slot == 1:
                ready = [ready[0] + ready[2], ready[1] + ready[3]]
            mean = jnp.concatenate([(one / divisor).astype(BF) for one in ready], axis=1)
            token_out[kv, :, first * HD : (first + count) * HD] = lax.dot_general(
                hot, mean, (((0,), (0,)), ((), ())), preferred_element_type=F32
            ).astype(BF)
            to = cols(place.x * HEADS_X + first, count)
            for step in STEPS:
                links.go(
                    ("u", kv, slot, step),
                    token_out.at[kv, token_rows(shift(place.x, step)), cols(first, count)],
                    outs[kv].at[:, to],
                    place.ring("x", step),
                )
            own["u", kv, slot] = links.here(
                ("u", kv, slot),
                token_out.at[kv, token_rows(place.x), cols(first, count)],
                outs[kv].at[:, to],
            )

        return start, relay, total, expand

    def work(what, slot, first, count):
        def one(i, carry):
            what(slot, SIDE + first + i if slot else shift(place.z, first + 2 * i))
            return carry

        lax.fori_loop(0, count, one, 0)

    merge, row, near, far, close = range(5)
    key1, key0, value0, value1 = [gather_stage(kv, slot) for kv, slot in GATHER_PARTS]
    start, relay, total, expand = range(4)
    key_grad1, key_grad0, value_grad0, value_grad1 = [
        scatter_stage(kv, slot) for kv, slot in GATHER_PARTS
    ]
    note_entries()
    key1[merge]()
    key1[row]()
    key0[merge]()
    key1[near]()
    key0[row]()
    key1[far]()
    value0[merge]()
    key1[close]()
    pair_arrived()
    work(weigh, 1, 0, 1)
    value1[merge]()
    key0[near]()
    value0[row]()
    work(weigh, 1, 1, 1)
    key0[far]()
    value1[row]()
    spread(1, 1)
    key0[close]()
    rows_arrived()
    work(weigh, 0, 1, 2)
    value0[near]()
    value_grad1[start]()
    work(weigh, 0, 2, 2)
    value0[far]()
    value1[near]()
    spread(1, 0)
    value0[close]()
    value_grad1[relay]()
    value_grad0[start]()
    work(attend, 0, 1, 2)
    send_result(shift(place.z, 1), 1)
    send_result(shift(place.z, -1), -1)
    value1[far]()
    value_grad0[relay]()
    value_grad1[total]()
    work(attend, 0, 2, 2)
    send_result(shift(place.z, 2), 2)
    send_result(place.z, 0)
    value1[close]()
    spread(0, 0)
    value_grad1[expand]()
    value_grad0[total]()
    key_grad0[start]()
    key_grad0[relay]()
    work(attend, 1, 0, 2)
    send_pair_result()
    spread(0, 1)
    value_grad0[expand]()
    key_grad1[start]()
    key_grad0[total]()
    key_grad1[relay]()
    key_grad0[expand]()
    key_grad1[total]()
    key_grad1[expand]()

    for which, (_, dst) in enumerate(results):
        for step in STEPS:
            links.got(("r", which, step), dst.at[:, cols(shift(place.z, -step))])
        links.got(("r", which, "partner"), dst.at[:, cols(SIDE + 1 - mine)])
        own["r", which, 0].wait()
        own["r", which, 1].wait()
    for slot, (first, count) in enumerate(GROUPS):
        for kv in range(2):
            for step in STEPS:
                links.got(
                    ("u", kv, slot, step),
                    outs[kv].at[:, cols(shift(place.x, -step) * HEADS_X + first, count)],
                )
            own["u", kv, slot].wait()
    links.finish()


def store_kernel(*refs):
    sems = refs[-1]
    copies = [pltpu.make_async_copy(refs[i], refs[4 + i], sems.at[i]) for i in range(4)]
    for copy in copies:
        copy.start()
    for copy in copies:
        copy.wait()


ANY = pl.BlockSpec(memory_space=pl.ANY)
HBM = pl.BlockSpec(memory_space=pltpu.HBM)
VMEM = pl.BlockSpec(memory_space=pltpu.VMEM)


def body(queries, keys_in, values_in, grad_out, assign, pattern, live_blocks):
    inputs = [
        pltpu.with_memory_space_constraint(one, pltpu.HBM)
        for one in (
            keys_in, values_in, queries, grad_out, assign.reshape(1, TOK), pattern.T,
            live_blocks.reshape(1, ALL_FRAMES),
        )
    ]
    shape = jax.ShapeDtypeStruct
    dma = pltpu.SemaphoreType.DMA
    units = sum(SLOT_UNITS)
    def half(*dims):
        return pltpu.VMEM(dims, BF)

    results = pl.pallas_call(
        layer_kernel,
        out_shape=(
            shape(queries.shape, BF),
            shape(queries.shape, BF),
            shape(keys_in.shape, BF),
            shape(keys_in.shape, BF),
        ),
        in_specs=[HBM] * 7,
        out_specs=(ANY,) * 4,
        scratch_shapes=[
            half(ALL_SPOTS, KB, HD),
            half(ALL_SPOTS, KB, HD),
            half(ALL_SPOTS, KB, HD),
            half(ALL_SPOTS, KB, HD),
            half(2, TOK, WIDTH),
            half(2, HEADS_X, 2, KB, HD),
            pltpu.VMEM((1, TOK), jnp.int32),
            half(units, TOK, HD),
            half(units, TOK, HD),
            half(NSEL * KB, HD),
            pltpu.VMEM((units, NSEL * KB, TOK), F32),
            pltpu.VMEM((units, 1, TOK), F32),
            pltpu.VMEM((NSEL * KB, TOK), F32),
            half(SLOT_UNITS[0] * ENTRIES, KB, HD),
            half(SLOT_UNITS[1] * ENTRIES, KB, HD),
            half(SLOT_UNITS[0] * ENTRIES, KB, HD),
            half(SLOT_UNITS[1] * ENTRIES, KB, HD),
            half(units, TOK, HD),
            half(units, TOK, HD),
            half(2, 2, ALL_SPOTS, KB, HD),
            half(2, 2, SIDE, GROUP, KB, HD),
            half(2, 2, 2, GROUP // 2, KB, HD),
            half(2, 2, 3, GROUP, KB, HD),
            half(2, 2, 3, GROUP, KB, HD),
            half(2, 2, GROUP, KB, HD),
            half(2, 2, SIDE, 2, KB, HD),
            half(2, TOK, WIDTH),
            pltpu.SMEM((NSEL, ALL_FRAMES), jnp.int32),
            pltpu.SMEM((1, ALL_FRAMES), jnp.int32),
            pltpu.VMEM((8, HD), jnp.int32),
            pltpu.SMEM((8, HD), jnp.int32),
            dma((SEMS,)),
            dma((SEMS,)),
            dma((LOCAL,)),
        ],
        compiler_params=pltpu.CompilerParams(
            collective_id=0, has_side_effects=True, vmem_limit_bytes=VMEM_LIMIT
        ),
        name="layer",
    )(*inputs)
    return pl.pallas_call(
        store_kernel,
        out_shape=tuple(shape(one.shape, BF) for one in results),
        in_specs=[VMEM] * 4,
        out_specs=(HBM,) * 4,
        scratch_shapes=[dma((4,))],
        compiler_params=pltpu.CompilerParams(vmem_limit_bytes=STORE_LIMIT),
        name="store",
    )(*results)


def solution(mesh):
    return jax.shard_map(
        body,
        mesh=mesh,
        in_specs=(
            P("frame", "head"),
            P(("frame", "head"), None),
            P(("frame", "head"), None),
            P("frame", "head"),
            P("frame"),
            P(),
            P(),
        ),
        out_specs=(
            P("frame", "head"),
            P("frame", "head"),
            P(("frame", "head"), None),
            P(("frame", "head"), None),
        ),
        check_vma=False,
    )
```
